32 devices in a mesh: obs: 16 (over z, x, core), ind: 2 (over y).
Axes of the slice: x: 2, y: 2, z: 4, core: 2. Of those that a mesh axis runs over, the one named last changes fastest.
Arguments:
- obs_coords: float32 [2, 32768], P(None, 'obs'), may hold values from 0 to 1
- obs_codes: int32 [32768], P('obs'), may hold values from 0 to 47
- route_plan: int32 [16, 16], replicated, may hold values from 0 to 1, as said below
- inducing_coords: float32 [2, 2048], P(None, 'ind'), may hold values from 0 to 1
- inducing_bands: int32 [2048], P('ind'), may hold values from 0 to 5
- band_mix: float32 [6, 6], replicated, may hold values from -2.4 to 2.4
- lengthscales: float32 [2], replicated, may hold values from 0.04 to 0.1
- class_scales: float32 [8], replicated, may hold values from 0.5 to 2
- prior_factor: bfloat16 [2048, 1024], P(('ind', 'obs')), may hold values from -0.046875 to 0.046875
- variational_chol: bfloat16 [2048, 1024], P(('ind', 'obs')), may hold values from -1 to 1, as said below
- variational_mean: bfloat16 [8, 2048], P(None, 'ind'), may hold values from -6 to 6
Outputs:
- class_probs: float32 [8, 32768], P(None, 'obs')
- grad_chol: float32 [2048, 1024], P(('ind', 'obs'))
- grad_mean: float32 [8, 2048], P(None, 'ind')
The draws below stay inside these ranges and needn't reach their ends.
Inputs may be any that keep to these rules, and one draw needn't show every extreme that they name: `route_plan`: entry [s, d] is the number of 128-row blocks that reader s hands to device d; every column sums to 16; a reader's blocks go out in order of destination from the front of its buffer. `variational_chol`: each block's rows are lower triangular within the block, with diagonal entries of 0.3 to 1.
All inputs are finite; a program needn't handle non-finite values.
Results may differ from the reference program's by a relative error of at most 0.014.
Values may be sent and summed in bfloat16 or wider, within the bound.
No kernel may reach another device: no remote copies, remote signals or barrier semaphores. Data moves between devices by JAX's collectives and lax.ppermute only.
A program may use at most 64 MiB of HBM per device.

```python
import math
import jax
import jax.numpy as jnp
from jax import lax

MB = 1024
C = 8
NB = 6
ROWS_DEV = 2048
M = 2048
READ_BUF = 32768
N_OBS = 16
N_IND = 2


def draw_route_plan(key, part):
    quota = ROWS_DEV // 128
    first, second = jax.random.split(jax.random.fold_in(key, 11))
    bias = jax.random.randint(first, (N_OBS, 1), 0, 4)
    noise = jax.random.randint(second, (N_OBS, N_OBS), 0, 1 << 20)
    sources = jnp.arange(N_OBS, dtype=jnp.int32)
    score = (bias * (1 << 20) + noise) * 64 + sources[:, None]
    chosen = lax.top_k(score.T, quota)[1]
    hits = jnp.sum((chosen[:, :, None] == sources[None, None, :]).astype(jnp.int32), axis=1)
    return hits.T.astype(jnp.int32)


def draw_variational_chol(key, part):
    first, second = jax.random.split(jax.random.fold_in(key, 23))
    row_ids = jnp.arange(M, dtype=jnp.int32)[:, None] % MB
    column_ids = jnp.arange(MB, dtype=jnp.int32)[None, :]
    diagonal = jax.random.uniform(first, (M, MB), jnp.float32, 0.3, 1.0)
    spread = jnp.clip(jax.random.normal(second, (M, MB), jnp.float32) * (0.6 / MB ** 0.5), -1.0, 1.0)
    value = jnp.where(column_ids == row_ids, diagonal, jnp.where(column_ids < row_ids, spread, 0.0))
    return value.astype(jnp.bfloat16)


def place_ends(values, stream_key, smallest, top_value):
    longest = values.shape.index(max(values.shape))
    spots = []
    for shift in (0, 1):
        where = [jax.random.randint(jax.random.fold_in(stream_key, axis), (), 0, length) for axis, length in enumerate(values.shape)]
        where[longest] = (where[longest] + shift) % values.shape[longest]
        spots.append(tuple(where))
    return values.at[spots[0]].set(smallest).at[spots[1]].set(top_value)


def steps_of(rng, shape, cuts, low, top_value):
    def one(axis_at, blocks):
        steps = jax.random.uniform(jax.random.fold_in(jax.random.fold_in(rng, 6), axis_at), (blocks,), jnp.float32, low / len(cuts), top_value / len(cuts))
        return jnp.repeat(jnp.exp(steps), shape[axis_at] // blocks).reshape((-1,) + (1,) * (len(shape) - axis_at - 1))

    factor_of = one(*cuts[0])
    for cut in cuts[1:]:
        factor_of = factor_of * one(*cut)
    return factor_of


def normal_values(stream_key, extent, width, reach, cuts=(), held_as=jnp.bfloat16):
    drawn = jax.random.normal(stream_key, extent, jnp.float32) * width
    if len(cuts) > 0:
        drawn = steps_of(stream_key, extent, cuts, -0.22, 0.18) * drawn
    return jnp.clip(drawn, min=-reach, max=reach).astype(held_as)


def setup_inputs(seed: int = 0) -> dict:
    keys = jax.random.split(jax.random.key(seed), 12)
    obs_coords = jnp.clip(1.0 * jax.random.uniform(keys[0], (2, READ_BUF), jnp.float32) ** steps_of(keys[0], (2, READ_BUF), ((1, 16),), -0.2, 0.2), 0.0, 1.0)
    obs_codes = place_ends(jax.random.randint(keys[1], (READ_BUF,), 0, NB * C), jax.random.fold_in(keys[1], 1), 0, (NB * C) - 1).astype(jnp.int32)
    route_plan = draw_route_plan(jax.random.fold_in(keys[11], 71), 0)
    inducing_coords = jnp.clip(1.0 * jax.random.uniform(keys[3], (2, M), jnp.float32) ** steps_of(keys[3], (2, M), ((1, 2),), -0.2, 0.2), 0.0, 1.0)
    inducing_bands = place_ends(jax.random.randint(keys[4], (M,), 0, NB), jax.random.fold_in(keys[4], 1), 0, NB - 1).astype(jnp.int32)
    band_mix = normal_values(keys[5], (NB, NB), 0.4, 2.4, (), jnp.float32)
    lengthscales = jnp.clip(jnp.exp(jax.random.uniform(keys[6], (2,), jnp.float32, math.log(0.04), math.log(0.1))), 0.04, 0.1)
    class_scales = jnp.clip(jnp.exp(jax.random.uniform(keys[7], (C,), jnp.float32, math.log(0.5), math.log(2.0))), 0.5, 2.0)
    prior_factor = normal_values(keys[8], (M, MB), (16 * MB) ** -0.5, 0.046875, ((0, 32),))
    variational_chol = draw_variational_chol(jax.random.fold_in(keys[11], 71), 0)
    variational_mean = normal_values(keys[10], (C, M), 1.0, 6.0, ((1, 2),))
    return dict(obs_coords=obs_coords, obs_codes=obs_codes, route_plan=route_plan, inducing_coords=inducing_coords, inducing_bands=inducing_bands, band_mix=band_mix, lengthscales=lengthscales, class_scales=class_scales, prior_factor=prior_factor, variational_chol=variational_chol, variational_mean=variational_mean)


precise = lax.Precision.HIGHEST


def arrange(obs_coords, obs_codes, route_plan):
    capacity = obs_coords.shape[1] // N_OBS
    blocks = route_plan * 128
    send_start = (jnp.cumsum(blocks, axis=1) - blocks).astype(jnp.int32)
    recv_start = (jnp.cumsum(blocks, axis=0) - blocks).astype(jnp.int32)
    position = jnp.arange(ROWS_DEV, dtype=jnp.int32)
    sources = jnp.arange(N_OBS, dtype=jnp.int32)

    def one_device(target):
        offsets = recv_start[:, target]
        source = (jnp.sum((offsets[None, :] <= position[:, None]).astype(jnp.int32), axis=1) - 1).astype(jnp.int32)
        pick = (source[:, None] == sources[None, :]).astype(jnp.int32)
        begin_row = jnp.sum(pick * offsets[None, :], axis=1).astype(jnp.int32)
        sent_row = jnp.sum(pick * send_start[:, target][None, :], axis=1).astype(jnp.int32)
        return (source * capacity + sent_row + position - begin_row).astype(jnp.int32)

    indices = jax.vmap(one_device)(sources).reshape(-1)
    return obs_coords[:, indices], obs_codes[indices]


def cross_cov(coords, band_ids, centers, center_bands, lengthscales, coupling):
    delta_t = (coords[0][:, None] - centers[0][None, :]) / lengthscales[0]
    delta_w = (coords[1][:, None] - centers[1][None, :]) / lengthscales[1]
    kinds = jnp.arange(NB, dtype=jnp.int32)
    row_hot = (band_ids[:, None] == kinds[None, :]).astype(jnp.float32)
    col_hot = (center_bands[:, None] == kinds[None, :]).astype(jnp.float32)
    mixing = jnp.dot(jnp.dot(row_hot, coupling, precision=precise), col_hot.T, precision=precise)
    return (jnp.exp(-0.5 * (delta_t * delta_t + delta_w * delta_w)) * mixing).astype(jnp.bfloat16)


def likelihood(mean_sum, variance, class_scales):
    logits = mean_sum + 0.5 * class_scales[:, None] * variance[None, :]
    weights = jnp.exp(logits)
    chances = weights / jnp.sum(weights, axis=0, keepdims=True)
    var_slope = -0.5 * jnp.sum(chances * class_scales[:, None], axis=0)
    return chances, var_slope


def reference(obs_coords, obs_codes, route_plan, inducing_coords, inducing_bands, band_mix, lengthscales, class_scales, prior_factor, variational_chol, variational_mean):
    coords, code_ids = arrange(obs_coords, obs_codes, route_plan)
    band_ids = code_ids % NB
    labels = code_ids // NB
    coupling = jnp.eye(NB, dtype=jnp.float32) + jnp.dot(band_mix, band_mix.T, precision=precise)
    kinds = jnp.arange(NB, dtype=jnp.int32)
    row_hot = (band_ids[:, None] == kinds[None, :]).astype(jnp.float32)
    self_cov = jnp.sum(row_hot * jnp.dot(row_hot, coupling, precision=precise), axis=1)
    total_rows = coords.shape[1]
    mean_sum = jnp.zeros((C, total_rows), jnp.float32)
    var_sum = jnp.zeros((total_rows,), jnp.float32)
    whitened_all = []
    for block in range(N_IND):
        lower = block * MB
        kernel_rows = cross_cov(coords, band_ids, inducing_coords[:, lower:lower + MB], inducing_bands[lower:lower + MB], lengthscales, coupling)
        whitened = jnp.dot(kernel_rows, prior_factor[lower:lower + MB], preferred_element_type=jnp.float32)
        whitened_bf = whitened.astype(jnp.bfloat16)
        covariant = jnp.dot(whitened_bf, variational_chol[lower:lower + MB], preferred_element_type=jnp.float32)
        mean_sum = mean_sum + lax.dot_general(variational_mean[:, lower:lower + MB], whitened_bf, (((1,), (1,)), ((), ())), preferred_element_type=jnp.float32)
        var_sum = var_sum + (jnp.sum(covariant * covariant, axis=1) - jnp.sum(whitened * whitened, axis=1))
        whitened_all.append(whitened_bf)
    chances, var_slope = likelihood(mean_sum, self_cov + var_sum, class_scales)
    classes = jnp.arange(C, dtype=jnp.int32)
    mean_slope = ((labels[None, :] == classes[:, None]).astype(jnp.float32) - chances).astype(jnp.bfloat16)
    chol_grads = []
    mean_grads = []
    for block in range(N_IND):
        lower = block * MB
        whitened_bf = whitened_all[block]
        chol_block = variational_chol[lower:lower + MB]
        covariant = jnp.dot(whitened_bf, chol_block, preferred_element_type=jnp.float32)
        heavy = (2.0 * var_slope[:, None] * covariant).astype(jnp.bfloat16)
        data_term = lax.dot_general(whitened_bf, heavy, (((0,), (0,)), ((), ())), preferred_element_type=jnp.float32)
        diagonal = jnp.diagonal(chol_block).astype(jnp.float32)
        chol_grads.append(jnp.tril(data_term) - chol_block.astype(jnp.float32) + jnp.diag(1.0 / diagonal))
        mean_term = lax.dot_general(mean_slope, whitened_bf, (((1,), (0,)), ((), ())), preferred_element_type=jnp.float32)
        mean_grads.append(mean_term - variational_mean[:, lower:lower + MB].astype(jnp.float32))
    return chances, jnp.concatenate(chol_grads, axis=0), jnp.concatenate(mean_grads, axis=1)
```

```python
import functools

import jax
import jax.numpy as jnp
from jax import lax
from jax.experimental import pallas as pl
from jax.experimental.pallas import tpu as pltpu
from jax.sharding import PartitionSpec as P

C = 8
NB = 6
ROWS_DEV = 2048
SLOT = 128
COL = 512

precise = lax.Precision.HIGHEST
f32 = jnp.float32
bf16 = jnp.bfloat16
SMEM = pl.BlockSpec(memory_space=pltpu.SMEM)
VMEM = pl.BlockSpec(memory_space=pltpu.VMEM)
ANY = pl.BlockSpec(memory_space=pl.ANY)


def dot(a, b):
    return jnp.dot(a, b, preferred_element_type=f32)


def dot_nt(a, b):
    return lax.dot_general(a, b, (((1,), (1,)), ((), ())), preferred_element_type=f32)


def swap(value, axis, bit):
    size = lax.axis_size(axis)
    return lax.ppermute(value, axis, [(i, i ^ bit) for i in range(size)])


def gather_pieces(own, nz):
    near = jnp.concatenate([own] + [swap(own, "obs", 4 * k) for k in range(1, nz)], axis=0)
    far = swap(near, "obs", 2)
    return near, far, swap(near, "obs", 1), swap(far, "obs", 1)


def load_pieces(me, groups, whole, sems, nz):
    rows = whole.shape[0] // (4 * nz)
    copies = []
    for g, group in enumerate(groups):
        for s in range(nz):
            piece = me ^ (4 * s) ^ (2 * (g % 2)) ^ (g // 2)
            copies.append(
                pltpu.make_async_copy(
                    group.at[pl.ds(rows * s, rows)],
                    whole.at[pl.ds(pl.multiple_of(rows * piece, rows), rows)],
                    sems.at[g, s],
                )
            )
    for copy in copies:
        copy.start()
    for copy in copies:
        copy.wait()


def whiten_kernel(nz, me, kt, g0, g1, g2, g3, means, ab, stats, whole, turned, sems):
    width = whole.shape[0]

    @pl.when(pl.program_id(0) == 0)
    def _():
        load_pieces(me[0], (g0, g1, g2, g3), whole, sems, nz)
        for j in range(0, width, 256):
            turned[:, j : j + 256] = whole[j : j + 256, :].T

    square = jnp.zeros((1, kt.shape[1]), f32)
    for k in range(0, width, 256):
        part = dot(turned[k : k + 256, :], kt[...])
        square = square + jnp.sum(part * part, axis=0, keepdims=True)
        ab[k : k + 256, :] = part.astype(bf16)
    stats[0:C, :] = dot(means[...], ab[...])
    stats[C : 2 * C, :] = jnp.broadcast_to(-square, (C, kt.shape[1]))


def covary_kernel(nz, me, ab, stats, g0, g1, g2, g3, bt, sums, whole, turned, sems):
    width = whole.shape[0]
    step = pl.program_id(0)

    @pl.when(step == 0)
    def _():
        load_pieces(me[0], (g0, g1, g2, g3), whole, sems, nz)
        for j in range(0, width, 256):
            turned[:, j : j + 256] = whole[j : j + 256, :].T

    square = stats[C : C + 1, :]
    for l in range(0, width, 256):
        part = dot(turned[l : l + 256, l:], ab[l:, :])
        square = square + jnp.sum(part * part, axis=0, keepdims=True)
        bt[l : l + 256, :] = part.astype(bf16)
    columns = pl.multiple_of(step * COL, COL)
    sums[:, pl.ds(columns, COL)] = stats[0:C, :]
    half = COL // 2
    sums[pl.ds(2 * step, 1), ROWS_DEV:] = square[:, :half]
    sums[pl.ds(2 * step + 1, 1), ROWS_DEV:] = square[:, half:]


def slope_kernel(
    nz, me, own, other, scales, labels, self_cov, ab, bt, chances_out, keep, send, heavy, slope, twice
):
    step = pl.program_id(0)
    core = me[0] % 2
    block = ab.shape[0]
    quarter = block // 4
    groups = quarter // 16

    @pl.when(step == 0)
    def _():
        total = own[...] + other[...]
        variance = jnp.concatenate(
            [total[i : i + 1, ROWS_DEV:] for i in range(C)], axis=1
        ) + self_cov[...]
        logits = total[:, :ROWS_DEV] + 0.5 * scales[...] * variance
        weights = jnp.exp(logits)
        chances = weights / jnp.sum(weights, axis=0, keepdims=True)
        chances_out[...] = chances
        twice[...] = -jnp.sum(chances * scales[...], axis=0, keepdims=True)
        classes = lax.broadcasted_iota(jnp.int32, chances.shape, 0)
        slope[...] = ((labels[...] == classes).astype(f32) - chances).astype(bf16)

    rows = pl.multiple_of(step * block, block)
    heavy[pl.ds(rows, block), :] = (bt[...].astype(f32) * twice[...]).astype(bf16)
    extra = block * nz * (nz + 1) // 2

    for z in range(nz):

        @pl.when(step == z)
        def _():
            wide = block * (z + 1)
            start = block * z * (z + 1) // 2
            term = dot_nt(ab[...], heavy[:wide, :])
            for x in range(2):
                first = term[2 * quarter * x : 2 * quarter * x + quarter, :]
                second = term[2 * quarter * x + quarter : 2 * quarter * (x + 1), :]
                keep[x, :, start : start + wide] = jnp.where(core == 0, first, second)
                send[x, :, start : start + wide] = jnp.where(core == 0, second, first).astype(bf16)
            mean = dot_nt(slope[...], ab[...])
            high = mean.astype(bf16).astype(f32)
            both = jnp.concatenate([high, mean - high], axis=0).astype(bf16)
            held = jnp.concatenate([mean, jnp.zeros_like(mean)], axis=0)
            top = 16 * (z % groups)
            left = extra + block * (z // groups)
            for x in range(2):
                keep[x, top : top + 16, left : left + block] = held
                send[x, top : top + 16, left : left + block] = both


def add_extra(kept, arrived, groups):
    parts = []
    for g in range(groups):
        top = kept[16 * g : 16 * g + 8] + arrived[16 * g : 16 * g + 8] + arrived[16 * g + 8 : 16 * g + 16]
        parts.append(top)
    return parts


def fold_extra(parts):
    held, sent = [], []
    for part in parts:
        high = part.astype(bf16).astype(f32)
        held += [part, jnp.zeros_like(part)]
        sent += [high, part - high]
    return jnp.concatenate(held, axis=0), jnp.concatenate(sent, axis=0).astype(bf16)


def pair_kernel(body_width, me, keep, arrived, kept, send):
    x = (me[0] // 2) % 2
    groups = keep.shape[1] // 16
    send[:, :body_width] = (
        keep[1 - x, :, :body_width] + arrived[1 - x, :, :body_width].astype(f32)
    ).astype(bf16)
    kept[:, :body_width] = keep[x, :, :body_width] + arrived[x, :, :body_width].astype(f32)
    parts = add_extra(
        keep[0, :, body_width:], arrived[0, :, body_width:].astype(f32), groups
    )
    held, sent = fold_extra(parts)
    kept[:, body_width:] = held
    send[:, body_width:] = sent


def chip_kernel(nz, body_width, me, kept, arrived, mine, *sends):
    z = me[0] // 4
    groups = kept.shape[0] // 16
    width = mine.shape[1] - (kept.shape[1] - body_width)
    block = width // nz
    parts = add_extra(kept[:, body_width:], arrived[:, body_width:].astype(f32), groups)
    held, sent = fold_extra(parts)
    for k in range(nz):
        target = z ^ k
        start = pl.multiple_of(block * (target * (target + 1) // 2), block)
        value = kept[:, pl.ds(start, width)] + arrived[:, pl.ds(start, width)].astype(f32)
        if k == 0:
            mine[:, :width] = value
            mine[:, width:] = held
        else:
            sends[k - 1][:, :width] = value.astype(bf16)
            sends[k - 1][:, width:] = sent


def finish_kernel(nz, me, mine, chol, means, *rest):
    arrived, grad_chol, grad_mean = rest[: nz - 1], rest[nz - 1], rest[nz]
    rows, width = chol.shape
    groups = rows // 16
    total = mine[:, :width]
    for piece in arrived:
        total = total + piece[:, :width].astype(f32)
    row_ids = me[0] * rows + lax.broadcasted_iota(jnp.int32, (rows, width), 0)
    column_ids = lax.broadcasted_iota(jnp.int32, (rows, width), 1)
    own = chol[...].astype(f32)
    on_diag = column_ids == row_ids
    diagonal = jnp.sum(jnp.where(on_diag, own, 0.0), axis=1, keepdims=True)
    grad_chol[...] = (
        jnp.where(column_ids <= row_ids, total, 0.0) - own + jnp.where(on_diag, 1.0 / diagonal, 0.0)
    )
    extra = mine[:, width:]
    parts = [extra[16 * g : 16 * g + 8] for g in range(groups)]
    for piece in arrived:
        values = piece[:, width:].astype(f32)
        parts = [
            part + values[16 * g : 16 * g + 8] + values[16 * g + 8 : 16 * g + 16]
            for g, part in enumerate(parts)
        ]
    block = width // nz
    for z in range(nz):
        part = parts[z % groups][:, block * (z // groups) : block * (z // groups + 1)]
        here = slice(block * z, block * (z + 1))
        grad_mean[:, here] = part - means[:, here].astype(f32)


def route(obs_coords, obs_codes, route_plan):
    devices = lax.axis_size("obs")
    stacked = jnp.concatenate([obs_coords, obs_codes.astype(f32)[None, :]], axis=0)
    if devices * SLOT == ROWS_DEV:
        return lax.all_to_all(stacked, "obs", split_axis=1, concat_axis=1, tiled=True)
    me = lax.axis_index("obs")
    blocks = route_plan * SLOT
    send_start = jnp.cumsum(blocks, axis=1) - blocks
    recv_start = jnp.cumsum(blocks, axis=0) - blocks
    my_sends = lax.dynamic_index_in_dim(send_start, me, 0, keepdims=False)
    my_recvs = lax.dynamic_index_in_dim(recv_start, me, 1, keepdims=False)
    padded = jnp.concatenate([stacked, jnp.zeros((3, SLOT), f32)], axis=1)
    outgoing = jax.vmap(lambda offset: lax.dynamic_slice_in_dim(padded, offset, SLOT, 1))(my_sends)
    incoming = lax.all_to_all(outgoing, "obs", split_axis=0, concat_axis=0, tiled=True)
    position = jnp.arange(ROWS_DEV, dtype=jnp.int32)
    sources = jnp.arange(devices, dtype=jnp.int32)
    source = jnp.sum((my_recvs[None, :] <= position[:, None]).astype(jnp.int32), axis=1) - 1
    pick = (source[:, None] == sources[None, :]).astype(jnp.int32)
    begin_row = jnp.sum(pick * my_recvs[None, :], axis=1)
    return incoming[source, :, position - begin_row].T


def body(
    obs_coords,
    obs_codes,
    route_plan,
    inducing_coords,
    inducing_bands,
    band_mix,
    lengthscales,
    class_scales,
    prior_factor,
    variational_chol,
    variational_mean,
):
    n = lax.axis_size("obs")
    nz = n // 4
    me = lax.axis_index("obs").astype(jnp.int32)[None]
    rows, width = variational_chol.shape
    steps = ROWS_DEV // COL
    block = width // nz
    body_width = block * nz * (nz + 1) // 2
    extra_width = 16 * width // rows
    packed = body_width + extra_width

    prior_groups = gather_pieces(prior_factor, nz)
    arrived = route(obs_coords, obs_codes, route_plan)
    chol_groups = gather_pieces(variational_chol, nz)

    code_ids = arrived[2:3].astype(jnp.int32)
    band_ids = code_ids % NB
    labels = code_ids // NB
    coupling = jnp.eye(NB, dtype=f32) + jnp.dot(band_mix, band_mix.T, precision=precise)
    kinds = jnp.arange(NB, dtype=jnp.int32)
    row_hot = (band_ids == kinds[:, None]).astype(f32)
    col_hot = (inducing_bands[:, None] == kinds[None, :]).astype(f32)
    self_cov = jnp.sum(row_hot * jnp.diagonal(coupling)[:, None], axis=0, keepdims=True)
    mixing = jnp.dot(jnp.dot(col_hot, coupling, precision=precise), row_hot, precision=precise)
    delta_t = (arrived[0][None, :] - inducing_coords[0][:, None]) / lengthscales[0]
    delta_w = (arrived[1][None, :] - inducing_coords[1][:, None]) / lengthscales[1]
    kt = (jnp.exp(-0.5 * (delta_t * delta_t + delta_w * delta_w)) * mixing).astype(bf16)

    whole = [
        pltpu.VMEM((width, width), bf16),
        pltpu.VMEM((width, width), bf16),
        pltpu.SemaphoreType.DMA((4, nz)),
    ]
    by_column = lambda height: pl.BlockSpec((height, COL), lambda i: (0, i))
    fixed = lambda shape: pl.BlockSpec(shape, lambda i: tuple(0 for _ in shape))
    big = pltpu.CompilerParams(vmem_limit_bytes=40 * 1024 * 1024)
    ab, part_stats = pl.pallas_call(
        functools.partial(whiten_kernel, nz),
        grid=(steps,),
        out_shape=(
            jax.ShapeDtypeStruct((width, ROWS_DEV), bf16),
            jax.ShapeDtypeStruct((2 * C, ROWS_DEV), f32),
        ),
        in_specs=[SMEM, by_column(width), ANY, ANY, ANY, ANY, fixed((C, width))],
        out_specs=(by_column(width), by_column(2 * C)),
        scratch_shapes=whole,
        compiler_params=big,
        cost_estimate=pl.CostEstimate(
            flops=2 * width * width * ROWS_DEV, bytes_accessed=10 * 1024 * 1024, transcendentals=0
        ),
        name="whiten",
    )(me, kt, *prior_groups, variational_mean)
    bt, sums = pl.pallas_call(
        functools.partial(covary_kernel, nz),
        grid=(steps,),
        out_shape=(
            jax.ShapeDtypeStruct((width, ROWS_DEV), bf16),
            jax.ShapeDtypeStruct((C, ROWS_DEV + COL // 2), f32),
        ),
        in_specs=[SMEM, by_column(width), by_column(2 * C), ANY, ANY, ANY, ANY],
        out_specs=(by_column(width), fixed((C, ROWS_DEV + COL // 2))),
        scratch_shapes=whole,
        compiler_params=big,
        cost_estimate=pl.CostEstimate(
            flops=width * width * ROWS_DEV, bytes_accessed=10 * 1024 * 1024, transcendentals=0
        ),
        name="covary",
    )(me, ab, part_stats, *chol_groups)

    other = swap(sums, "ind", 1)
    bit = 2
    while bit < lax.axis_size("ind"):
        sums = sums + other
        other = swap(sums, "ind", bit)
        bit *= 2

    by_row = pl.BlockSpec((block, ROWS_DEV), lambda i: (i, 0))
    chances, keep, send = pl.pallas_call(
        functools.partial(slope_kernel, nz),
        grid=(nz,),
        out_shape=(
            jax.ShapeDtypeStruct((C, ROWS_DEV), f32),
            jax.ShapeDtypeStruct((2, rows, packed), f32),
            jax.ShapeDtypeStruct((2, rows, packed), bf16),
        ),
        in_specs=[
            SMEM,
            fixed(sums.shape),
            fixed(sums.shape),
            fixed((C, 1)),
            fixed((1, ROWS_DEV)),
            fixed((1, ROWS_DEV)),
            by_row,
            by_row,
        ],
        out_specs=(fixed((C, ROWS_DEV)), fixed((2, rows, packed)), fixed((2, rows, packed))),
        scratch_shapes=[
            pltpu.VMEM((width, ROWS_DEV), bf16),
            pltpu.VMEM((C, ROWS_DEV), bf16),
            pltpu.VMEM((1, ROWS_DEV), f32),
        ],
        compiler_params=big,
        cost_estimate=pl.CostEstimate(
            flops=width * width * ROWS_DEV, bytes_accessed=10 * 1024 * 1024, transcendentals=0
        ),
        name="slopes",
    )(me, sums, other, class_scales[:, None], labels, self_cov, ab, bt)

    kept, send = pl.pallas_call(
        functools.partial(pair_kernel, body_width),
        out_shape=(
            jax.ShapeDtypeStruct((rows, packed), f32),
            jax.ShapeDtypeStruct((rows, packed), bf16),
        ),
        in_specs=[SMEM, VMEM, VMEM],
        out_specs=(VMEM, VMEM),
        compiler_params=big,
        name="add_pair",
    )(me, keep, swap(send, "obs", 1))
    piece = (rows, width + extra_width)
    mine, *sends = pl.pallas_call(
        functools.partial(chip_kernel, nz, body_width),
        out_shape=[jax.ShapeDtypeStruct(piece, f32)]
        + [jax.ShapeDtypeStruct(piece, bf16)] * (nz - 1),
        in_specs=[SMEM, VMEM, VMEM],
        out_specs=[VMEM] * nz,
        compiler_params=big,
        name="add_chip",
    )(me, kept, swap(send, "obs", 2))
    arrivals = [swap(value, "obs", 4 * (k + 1)) for k, value in enumerate(sends)]
    grad_chol, grad_mean = pl.pallas_call(
        functools.partial(finish_kernel, nz),
        out_shape=(
            jax.ShapeDtypeStruct((rows, width), f32),
            jax.ShapeDtypeStruct((C, width), f32),
        ),
        in_specs=[SMEM] + [VMEM] * (nz + 2),
        out_specs=(VMEM, VMEM),
        compiler_params=big,
        name="finish",
    )(me, mine, variational_chol, variational_mean, *arrivals)
    return (chances, grad_chol, grad_mean)


def solution(mesh):
    placed = (
        P(None, "obs"),
        P("obs"),
        P(),
        P(None, "ind"),
        P("ind"),
        P(),
        P(),
        P(),
        P(("ind", "obs"), None),
        P(("ind", "obs"), None),
        P(None, "ind"),
    )
    return jax.shard_map(
        body,
        mesh=mesh,
        in_specs=placed,
        out_specs=(P(None, "obs"), P(("ind", "obs"), None), P(None, "ind")),
        check_vma=False,
    )
```

```python
import functools

import jax
import jax.numpy as jnp
from jax import lax
from jax.experimental import pallas as pl
from jax.experimental.pallas import tpu as pltpu
from jax.sharding import PartitionSpec as P

C = 8
NB = 6
ROWS_DEV = 2048
SLOT = 128
COL = 1024
SQRT_HALF_LOG2E = 0.8493218002880191

precise = lax.Precision.HIGHEST
f32 = jnp.float32
bf16 = jnp.bfloat16
SMEM = pl.BlockSpec(memory_space=pltpu.SMEM)
VMEM = pl.BlockSpec(memory_space=pltpu.VMEM)
HBM = pl.BlockSpec(memory_space=pltpu.HBM)
SMALL = pltpu.CompilerParams(vmem_limit_bytes=4 * 1024 * 1024)


def dot(a, b):
    return jnp.dot(a, b, preferred_element_type=f32)


def dot_nt(a, b):
    return lax.dot_general(a, b, (((1,), (1,)), ((), ())), preferred_element_type=f32)


def swap(value, axis, bit):
    size = lax.axis_size(axis)
    return lax.ppermute(value, axis, [(i, i ^ bit) for i in range(size)])


def after(value, *earlier):
    return lax.optimization_barrier((value,) + earlier)[0]


def join_kernel(*refs):
    out = refs[-1]
    top = 0
    for ref in refs[:-1]:
        out[top : top + ref.shape[0], :] = ref[...]
        top += ref.shape[0]


def join(*pieces):
    rows = sum(piece.shape[0] for piece in pieces)
    return pl.pallas_call(
        join_kernel,
        out_shape=jax.ShapeDtypeStruct((rows, pieces[0].shape[1]), pieces[0].dtype),
        in_specs=[VMEM] * len(pieces),
        out_specs=VMEM,
        compiler_params=SMALL,
        name="join",
    )(*pieces)


def phases_of(nz):
    offsets = range(2, 4 * nz, 2)
    most = max(offset.bit_count() for offset in offsets)
    return [[o for o in reversed(offsets) if o.bit_count() == p] for p in range(1, most + 1)]


def store_pieces(groups, whole, nz, at):
    me = lax.axis_index("obs")
    rows = whole.shape[0] // (4 * nz)
    phases = phases_of(nz)
    phases[0] = [0] + phases[0]
    for g, group in enumerate(groups):
        for s, offset in enumerate(phases[g // 2]):
            piece = me ^ offset ^ (g % 2)
            top = (2 * s + at) * rows
            whole[pl.ds(pl.multiple_of(rows * piece, rows), rows), :] = group[top : top + rows, :]


def stack_kernel(coords_in, codes_in, out, coords, codes, sems):
    fetch((coords_in, codes_in), (coords, codes), sems)
    out[0:2, :] = coords[...]
    out[2:3, :] = codes[...].astype(f32)


def fetch(sources, targets, sems):
    copies = [pltpu.make_async_copy(a, b, sems.at[i]) for i, (a, b) in enumerate(zip(sources, targets))]
    for copy in copies:
        copy.start()
    for copy in copies:
        copy.wait()


def kernel_rows_kernel(
    arrived, points_in, bands_in, mix_in, lengthscales, kt, labels, self_cov, points, point_bands, band_mix, sems
):
    fetch((points_in, bands_in, mix_in), (points, point_bands, band_mix), sems)
    codes = arrived[2:3, :]
    label = jnp.floor((codes + 0.5) * (1.0 / NB))
    labels[...] = label.astype(jnp.int32)
    bands = (codes - NB * label).astype(jnp.int32)
    kinds = lax.broadcasted_iota(jnp.int32, (C, ROWS_DEV), 0)
    hot = (kinds == bands).astype(f32)
    eye = lax.broadcasted_iota(jnp.int32, (C, C), 0) == lax.broadcasted_iota(jnp.int32, (C, C), 1)
    factor = jnp.concatenate([band_mix[...], jnp.zeros((NB, C - NB), f32)], axis=1)
    factor = jnp.concatenate([factor, jnp.zeros((C - NB, C), f32)], axis=0)
    mix = eye.astype(f32) + lax.dot_general(
        factor, factor, (((1,), (1,)), ((), ())), precision=precise, preferred_element_type=f32
    )
    scales = [SQRT_HALF_LOG2E / lengthscales[i] for i in range(2)]
    diagonal = jnp.sum(jnp.where(eye, mix, 0.0), axis=1, keepdims=True)
    self_cov[...] = jnp.sum(hot * diagonal, axis=0, keepdims=True)
    hots = jnp.concatenate([hot, hot, hot, jnp.zeros_like(hot)], axis=0).astype(bf16)
    times = arrived[0:1, :] * scales[0]
    waves = arrived[1:2, :] * scales[1]
    width = points.shape[1]
    columns = jnp.concatenate(
        [points[...], point_bands[...].astype(f32), jnp.zeros((C - 3, width), f32)], axis=0
    ).T
    step = 128
    for j in range(0, width, step):
        here = columns[j : j + step, :]
        picked = jnp.zeros((step, C), f32)
        for kind in range(NB):
            picked = jnp.where(here[:, 2:3] == float(kind), mix[kind : kind + 1, :], picked)
        high = picked.astype(bf16).astype(f32)
        middle = (picked - high).astype(bf16).astype(f32)
        low = picked - high - middle
        split = jnp.concatenate([high, middle, low, jnp.zeros_like(low)], axis=1).astype(bf16)
        mixing = dot(split, hots)
        delta_t = times - here[:, 0:1] * scales[0]
        delta_w = waves - here[:, 1:2] * scales[1]
        value = jnp.exp2(-(delta_t * delta_t + delta_w * delta_w)) * mixing
        kt[j : j + step, :] = value.astype(bf16)


def whiten_kernel(nz, kt, means, *rest):
    groups, (ab, stats, whole, turned) = rest[:-4], rest[-4:]
    width = whole.shape[0]
    store_pieces(groups, whole, nz, 0)
    for j in range(0, width, 256):
        turned[:, j : j + 256] = whole[j : j + 256, :].T

    @pl.loop(0, ROWS_DEV // COL)
    def _(step):
        columns = pl.ds(pl.multiple_of(step * COL, COL), COL)
        square = jnp.zeros((1, COL), f32)
        for k in range(0, width, 256):
            part = dot(turned[k : k + 256, :], kt[:, columns])
            square = square + jnp.sum(part * part, axis=0, keepdims=True)
            ab[k : k + 256, columns] = part.astype(bf16)
        stats[0:C, columns] = dot(means[...], ab[:, columns])
        stats[C : 2 * C, columns] = jnp.broadcast_to(-square, (C, COL))


def covary_kernel(nz, ab, stats, *rest):
    groups, (bt, sums, whole, turned) = rest[:-4], rest[-4:]
    width = whole.shape[0]
    store_pieces(groups, whole, nz, 1)
    for j in range(0, width, 256):
        turned[:, j : j + 256] = whole[j : j + 256, :].T

    @pl.loop(0, ROWS_DEV // COL)
    def _(step):
        columns = pl.ds(pl.multiple_of(step * COL, COL), COL)
        square = stats[C : C + 1, columns]
        for l in range(0, width, 256):
            part = dot(turned[l : l + 256, l:], ab[l:, columns])
            square = square + jnp.sum(part * part, axis=0, keepdims=True)
            bt[l : l + 256, columns] = part.astype(bf16)
        sums[:, columns] = stats[0:C, columns]
        piece = ROWS_DEV // C
        for i in range(COL // piece):
            sums[pl.ds((COL // piece) * step + i, 1), ROWS_DEV:] = square[:, piece * i : piece * (i + 1)]


def slope_kernel(nz, own, other, scales, labels, self_cov, ab, bt, chances_out, keep, send, heavy):
    core = lax.axis_index("obs") % 2
    block = ab.shape[0] // nz
    quarter = block // 4
    groups = quarter // 16
    total = own[...] + other[...]
    variance = jnp.concatenate([total[i : i + 1, ROWS_DEV:] for i in range(C)], axis=1) + self_cov[...]
    classes = lax.broadcasted_iota(jnp.int32, (C, 1), 0)
    scale = jnp.zeros((C, 1), f32)
    for i in range(C):
        scale = jnp.where(classes == i, scales[i], scale)
    logits = total[:, :ROWS_DEV] + 0.5 * scale * variance
    weights = jnp.exp(logits)
    chances = weights / jnp.sum(weights, axis=0, keepdims=True)
    chances_out[...] = chances
    twice = -jnp.sum(chances * scale, axis=0, keepdims=True)
    slope = ((labels[...] == classes).astype(f32) - chances).astype(bf16)
    extra = block * nz * (nz + 1) // 2
    for z in range(nz):
        rows = slice(block * z, block * (z + 1))
        heavy[rows, :] = (bt[rows, :].astype(f32) * twice).astype(bf16)
        wide = block * (z + 1)
        start = block * z * (z + 1) // 2
        term = dot_nt(ab[rows, :], heavy[:wide, :])
        for x in range(2):
            first = term[2 * quarter * x : 2 * quarter * x + quarter, :]
            second = term[2 * quarter * x + quarter : 2 * quarter * (x + 1), :]
            keep[x, :, start : start + wide] = jnp.where(core == 0, first, second)
            send[x, :, start : start + wide] = jnp.where(core == 0, second, first).astype(bf16)
        mean = dot_nt(slope, ab[rows, :])
        high = mean.astype(bf16).astype(f32)
        both = jnp.concatenate([high, mean - high], axis=0).astype(bf16)
        held = jnp.concatenate([mean, jnp.zeros_like(mean)], axis=0)
        top = 16 * (z % groups)
        left = extra + block * (z // groups)
        for x in range(2):
            keep[x, top : top + 16, left : left + block] = held
            send[x, top : top + 16, left : left + block] = both


def add_extra(kept, arrived, groups):
    parts = []
    for g in range(groups):
        top = kept[16 * g : 16 * g + 8] + arrived[16 * g : 16 * g + 8] + arrived[16 * g + 8 : 16 * g + 16]
        parts.append(top)
    return parts


def fold_extra(parts):
    held, sent = [], []
    for part in parts:
        high = part.astype(bf16).astype(f32)
        held += [part, jnp.zeros_like(part)]
        sent += [high, part - high]
    return jnp.concatenate(held, axis=0), jnp.concatenate(sent, axis=0).astype(bf16)


def pair_kernel(body_width, keep, arrived, kept, send):
    x = (lax.axis_index("obs") // 2) % 2
    groups = keep.shape[1] // 16
    send[:, :body_width] = (
        keep[1 - x, :, :body_width] + arrived[1 - x, :, :body_width].astype(f32)
    ).astype(bf16)
    kept[:, :body_width] = keep[x, :, :body_width] + arrived[x, :, :body_width].astype(f32)
    parts = add_extra(
        keep[0, :, body_width:], arrived[0, :, body_width:].astype(f32), groups
    )
    held, sent = fold_extra(parts)
    kept[:, body_width:] = held
    send[:, body_width:] = sent


def chip_kernel(nz, body_width, kept, arrived, mine, *sends):
    z = lax.axis_index("obs") // 4
    groups = kept.shape[0] // 16
    width = mine.shape[1] - (kept.shape[1] - body_width)
    block = width // nz
    parts = add_extra(kept[:, body_width:], arrived[:, body_width:].astype(f32), groups)
    held, sent = fold_extra(parts)
    for k in range(nz):
        target = z ^ k
        start = pl.multiple_of(block * (target * (target + 1) // 2), block)
        value = kept[:, pl.ds(start, width)] + arrived[:, pl.ds(start, width)].astype(f32)
        if k == 0:
            mine[:, :width] = value
            mine[:, width:] = held
        else:
            sends[k - 1][:, :width] = value.astype(bf16)
            sends[k - 1][:, width:] = sent


def finish_kernel(nz, mine, chol, means, *rest):
    arrived, grad_chol, grad_mean = rest[: nz - 1], rest[nz - 1], rest[nz]
    rows, width = chol.shape
    groups = rows // 16
    total = mine[:, :width]
    for piece in arrived:
        total = total + piece[:, :width].astype(f32)
    row_ids = lax.axis_index("obs") * rows + lax.broadcasted_iota(jnp.int32, (rows, width), 0)
    column_ids = lax.broadcasted_iota(jnp.int32, (rows, width), 1)
    own = chol[...].astype(f32)
    on_diag = column_ids == row_ids
    diagonal = jnp.sum(jnp.where(on_diag, own, 0.0), axis=1, keepdims=True)
    grad_chol[...] = (
        jnp.where(column_ids <= row_ids, total, 0.0) - own + jnp.where(on_diag, 1.0 / diagonal, 0.0)
    )
    extra = mine[:, width:]
    parts = [extra[16 * g : 16 * g + 8] for g in range(groups)]
    for piece in arrived:
        values = piece[:, width:].astype(f32)
        parts = [
            part + values[16 * g : 16 * g + 8] + values[16 * g + 8 : 16 * g + 16]
            for g, part in enumerate(parts)
        ]
    block = width // nz
    for z in range(nz):
        part = parts[z % groups][:, block * (z // groups) : block * (z // groups + 1)]
        here = slice(block * z, block * (z + 1))
        grad_mean[:, here] = part - means[:, here].astype(f32)


def route(obs_coords, obs_codes, route_plan):
    devices = lax.axis_size("obs")
    stacked = pl.pallas_call(
        stack_kernel,
        out_shape=jax.ShapeDtypeStruct((3, obs_coords.shape[1]), f32),
        in_specs=[HBM, HBM],
        out_specs=VMEM,
        scratch_shapes=[
            pltpu.VMEM(obs_coords.shape, f32),
            pltpu.VMEM((1, obs_coords.shape[1]), jnp.int32),
            pltpu.SemaphoreType.DMA((2,)),
        ],
        compiler_params=SMALL,
        name="stack",
    )(obs_coords, obs_codes[None, :])
    if devices * SLOT == ROWS_DEV:
        return lax.all_to_all(stacked, "obs", split_axis=1, concat_axis=1, tiled=True)
    me = lax.axis_index("obs")
    blocks = route_plan * SLOT
    send_start = jnp.cumsum(blocks, axis=1) - blocks
    recv_start = jnp.cumsum(blocks, axis=0) - blocks
    my_sends = lax.dynamic_index_in_dim(send_start, me, 0, keepdims=False)
    my_recvs = lax.dynamic_index_in_dim(recv_start, me, 1, keepdims=False)
    padded = jnp.concatenate([stacked, jnp.zeros((3, SLOT), f32)], axis=1)
    outgoing = jax.vmap(lambda offset: lax.dynamic_slice_in_dim(padded, offset, SLOT, 1))(my_sends)
    incoming = lax.all_to_all(outgoing, "obs", split_axis=0, concat_axis=0, tiled=True)
    position = jnp.arange(ROWS_DEV, dtype=jnp.int32)
    sources = jnp.arange(devices, dtype=jnp.int32)
    source = jnp.sum((my_recvs[None, :] <= position[:, None]).astype(jnp.int32), axis=1) - 1
    pick = (source[:, None] == sources[None, :]).astype(jnp.int32)
    begin_row = jnp.sum(pick * my_recvs[None, :], axis=1)
    return incoming[source, :, position - begin_row].T


def body(
    obs_coords,
    obs_codes,
    route_plan,
    inducing_coords,
    inducing_bands,
    band_mix,
    lengthscales,
    class_scales,
    prior_factor,
    variational_chol,
    variational_mean,
):
    n = lax.axis_size("obs")
    nz = n // 4
    rows, width = variational_chol.shape
    body_width = width // nz * (nz * (nz + 1) // 2)
    extra_width = 16 * width // rows
    packed = body_width + extra_width

    phases = phases_of(nz)
    pieces = {0: join(prior_factor, variational_chol)}
    pieces.update({offset: swap(pieces[0], "obs", offset) for offset in phases[0]})
    arrived = route(obs_coords, obs_codes, route_plan)
    pieces, arrived = lax.optimization_barrier((pieces, arrived))
    own_side = join(*[pieces[offset] for offset in [0] + phases[0]])
    groups = [own_side, swap(own_side, "obs", 1)]

    big = pltpu.CompilerParams(vmem_limit_bytes=16 * 1024 * 1024)
    kt, labels, self_cov = pl.pallas_call(
        kernel_rows_kernel,
        out_shape=(
            jax.ShapeDtypeStruct((width, ROWS_DEV), bf16),
            jax.ShapeDtypeStruct((1, ROWS_DEV), jnp.int32),
            jax.ShapeDtypeStruct((1, ROWS_DEV), f32),
        ),
        in_specs=[VMEM, HBM, HBM, HBM, SMEM],
        out_specs=(VMEM, VMEM, VMEM),
        scratch_shapes=[
            pltpu.VMEM((2, width), f32),
            pltpu.VMEM((1, width), jnp.int32),
            pltpu.VMEM((NB, NB), f32),
            pltpu.SemaphoreType.DMA((3,)),
        ],
        compiler_params=big,
        cost_estimate=pl.CostEstimate(
            flops=20 * width * ROWS_DEV, bytes_accessed=4 * 1024 * 1024, transcendentals=width * ROWS_DEV
        ),
        name="kernel_rows",
    )(after(arrived, own_side), inducing_coords, inducing_bands[None, :], band_mix, lengthscales)

    for phase in phases[1:]:
        for offset in phase:
            low = offset & -offset
            pieces[offset] = swap(pieces[offset ^ low], "obs", low)
        if phase is phases[1]:
            pieces, kt = lax.optimization_barrier((pieces, kt))
        group = join(*[pieces[offset] for offset in phase]) if len(phase) > 1 else pieces[phase[0]]
        groups += [group, swap(group, "obs", 1)]

    whole = [pltpu.VMEM((width, width), bf16), pltpu.VMEM((width, width), bf16)]
    ab, part_stats = pl.pallas_call(
        functools.partial(whiten_kernel, nz),
        out_shape=(
            jax.ShapeDtypeStruct((width, ROWS_DEV), bf16),
            jax.ShapeDtypeStruct((2 * C, ROWS_DEV), f32),
        ),
        in_specs=[VMEM] * (2 + len(groups)),
        out_specs=(VMEM, VMEM),
        scratch_shapes=whole,
        compiler_params=big,
        cost_estimate=pl.CostEstimate(
            flops=2 * width * width * ROWS_DEV, bytes_accessed=10 * 1024 * 1024, transcendentals=0
        ),
        name="whiten",
    )(kt, variational_mean, *groups)
    bt, sums = pl.pallas_call(
        functools.partial(covary_kernel, nz),
        out_shape=(
            jax.ShapeDtypeStruct((width, ROWS_DEV), bf16),
            jax.ShapeDtypeStruct((C, ROWS_DEV + ROWS_DEV // C), f32),
        ),
        in_specs=[VMEM] * (2 + len(groups)),
        out_specs=(VMEM, VMEM),
        scratch_shapes=whole,
        compiler_params=big,
        cost_estimate=pl.CostEstimate(
            flops=width * width * ROWS_DEV, bytes_accessed=10 * 1024 * 1024, transcendentals=0
        ),
        name="covary",
    )(ab, part_stats, *groups)

    other = swap(sums, "ind", 1)
    bit = 2
    while bit < lax.axis_size("ind"):
        sums = sums + other
        other = swap(sums, "ind", bit)
        bit *= 2

    chances, keep, send = pl.pallas_call(
        functools.partial(slope_kernel, nz),
        out_shape=(
            jax.ShapeDtypeStruct((C, ROWS_DEV), f32),
            jax.ShapeDtypeStruct((2, rows, packed), f32),
            jax.ShapeDtypeStruct((2, rows, packed), bf16),
        ),
        in_specs=[VMEM, VMEM, SMEM] + [VMEM] * 4,
        out_specs=(VMEM, VMEM, VMEM),
        scratch_shapes=[pltpu.VMEM((width, ROWS_DEV), bf16)],
        compiler_params=big,
        cost_estimate=pl.CostEstimate(
            flops=width * width * ROWS_DEV, bytes_accessed=10 * 1024 * 1024, transcendentals=0
        ),
        name="slopes",
    )(sums, other, class_scales, labels, self_cov, ab, bt)

    kept, send = pl.pallas_call(
        functools.partial(pair_kernel, body_width),
        out_shape=(
            jax.ShapeDtypeStruct((rows, packed), f32),
            jax.ShapeDtypeStruct((rows, packed), bf16),
        ),
        in_specs=[VMEM, VMEM],
        out_specs=(VMEM, VMEM),
        compiler_params=big,
        name="add_pair",
    )(keep, swap(send, "obs", 1))
    piece = (rows, width + extra_width)
    mine, *sends = pl.pallas_call(
        functools.partial(chip_kernel, nz, body_width),
        out_shape=[jax.ShapeDtypeStruct(piece, f32)]
        + [jax.ShapeDtypeStruct(piece, bf16)] * (nz - 1),
        in_specs=[VMEM, VMEM],
        out_specs=[VMEM] * nz,
        compiler_params=big,
        name="add_chip",
    )(kept, swap(send, "obs", 2))
    arrivals = [swap(value, "obs", 4 * (k + 1)) for k, value in enumerate(sends)]
    grad_chol, grad_mean = pl.pallas_call(
        functools.partial(finish_kernel, nz),
        out_shape=(
            jax.ShapeDtypeStruct((rows, width), f32),
            jax.ShapeDtypeStruct((C, width), f32),
        ),
        in_specs=[VMEM] * (nz + 2),
        out_specs=(VMEM, VMEM),
        compiler_params=big,
        name="finish",
    )(mine, variational_chol, variational_mean, *arrivals)
    return (chances, grad_chol, grad_mean)


def solution(mesh):
    placed = (
        P(None, "obs"),
        P("obs"),
        P(),
        P(None, "ind"),
        P("ind"),
        P(),
        P(),
        P(),
        P(("ind", "obs"), None),
        P(("ind", "obs"), None),
        P(None, "ind"),
    )
    return jax.shard_map(
        body,
        mesh=mesh,
        in_specs=placed,
        out_specs=(P(None, "obs"), P(("ind", "obs"), None), P(None, "ind")),
        check_vma=False,
    )
```

```python
import functools

import jax
import jax.numpy as jnp
from jax import lax
from jax.experimental import pallas as pl
from jax.experimental.pallas import tpu as pltpu
from jax.sharding import PartitionSpec as P

C = 8
NB = 6
ROWS_DEV = 2048
SLOT = 128
COL = 1024
SQRT_HALF_LOG2E = 0.8493218002880191

precise = lax.Precision.HIGHEST
f32 = jnp.float32
bf16 = jnp.bfloat16
SMEM = pl.BlockSpec(memory_space=pltpu.SMEM)
VMEM = pl.BlockSpec(memory_space=pltpu.VMEM)
HBM = pl.BlockSpec(memory_space=pltpu.HBM)
SMALL = pltpu.CompilerParams(vmem_limit_bytes=4 * 1024 * 1024)


def dot(a, b):
    return jnp.dot(a, b, preferred_element_type=f32)


def dot_nt(a, b):
    return lax.dot_general(a, b, (((1,), (1,)), ((), ())), preferred_element_type=f32)


def swap(value, axis, bit):
    size = lax.axis_size(axis)
    return lax.ppermute(value, axis, [(i, i ^ bit) for i in range(size)])


def after(value, *earlier):
    return lax.optimization_barrier((value,) + earlier)[0]


def join_kernel(places, rows, *refs):
    out = refs[-1]
    for i, (source, slot) in enumerate(places):
        out[rows * i : rows * (i + 1), :] = refs[source][rows * slot : rows * (slot + 1), :]


def join(parts, rows):
    first = parts[0][0]
    if first.shape[0] == rows * len(parts) and parts == [(first, slot) for slot in range(len(parts))]:
        return first
    arrays = list({id(array): array for array, _ in parts}.values())
    places = [([array is other for other in arrays].index(True), slot) for array, slot in parts]
    return pl.pallas_call(
        functools.partial(join_kernel, places, rows),
        out_shape=jax.ShapeDtypeStruct((rows * len(parts), parts[0][0].shape[1]), parts[0][0].dtype),
        in_specs=[VMEM] * len(arrays),
        out_specs=VMEM,
        compiler_params=SMALL,
        name="join",
    )(*arrays)


def phases_of(nz):
    offsets = range(2, 4 * nz, 2)
    most = max(offset.bit_count() for offset in offsets)
    return [[o for o in reversed(offsets) if o.bit_count() == p] for p in range(1, most + 1)]


class Gather:
    def __init__(self, factors, nz):
        self.rows = factors[0].shape[0]
        own = join([(factor, 0) for factor in factors], self.rows)
        self.pieces = {(m, 0): (own, m) for m in range(2)}
        self.phases = phases_of(nz)
        self.groups = []

    def phase(self, number, beside=None):
        wanted = {}
        for offset in self.phases[number]:
            for m in range(2):
                bit = 4 if m == 1 and offset & 4 else offset & -offset
                wanted.setdefault(bit, []).append((m, offset))
        arrivals = {}
        for bit, keys in sorted(wanted.items(), reverse=True):
            sent = join([self.pieces[m, offset ^ bit] for m, offset in keys], self.rows)
            arrivals[bit] = swap(sent, "obs", bit)
        if beside is not None:
            arrivals, beside = lax.optimization_barrier((arrivals, beside()))
        new = [(0, 0), (1, 0)] if number == 0 else []
        for bit, keys in sorted(wanted.items()):
            self.pieces.update({key: (arrivals[bit], slot) for slot, key in enumerate(keys)})
            new += keys
        last = number == len(self.phases) - 1
        for part in [[key] for key in new] if last else [new]:
            group = join([self.pieces[key] for key in part], self.rows)
            self.groups.append((part, group, swap(group, "obs", 1)))
        return beside

    def of(self, m):
        arrays, places = [], []
        for new, *pair in self.groups:
            slots = [(slot, offset) for slot, (owner, offset) in enumerate(new) if owner == m]
            for core, array in enumerate(pair):
                places += [(len(arrays), slot, offset ^ core) for slot, offset in slots]
                arrays += [array] if slots else []
        return arrays, places


def store_pieces(groups, places, whole):
    me = lax.axis_index("obs")
    rows = whole.shape[0] // len(places)
    for source, slot, offset in places:
        target = pl.ds(pl.multiple_of(rows * (me ^ offset), rows), rows)
        whole[target, :] = groups[source][rows * slot : rows * (slot + 1), :]


def stack_kernel(coords_in, codes_in, out, coords, codes, sems):
    fetch((coords_in, codes_in), (coords, codes), sems)
    out[0:2, :] = coords[...]
    out[2:3, :] = codes[...].astype(f32)


def fetch(sources, targets, sems):
    copies = [pltpu.make_async_copy(a, b, sems.at[i]) for i, (a, b) in enumerate(zip(sources, targets))]
    for copy in copies:
        copy.start()
    for copy in copies:
        copy.wait()


def kernel_rows_kernel(
    arrived, points_in, bands_in, mix_in, lengthscales, kt, labels, self_cov, points, point_bands, band_mix, sems
):
    fetch((points_in, bands_in, mix_in), (points, point_bands, band_mix), sems)
    codes = arrived[2:3, :]
    label = jnp.floor((codes + 0.5) * (1.0 / NB))
    labels[...] = label.astype(jnp.int32)
    bands = (codes - NB * label).astype(jnp.int32)
    kinds = lax.broadcasted_iota(jnp.int32, (C, ROWS_DEV), 0)
    hot = (kinds == bands).astype(f32)
    eye = lax.broadcasted_iota(jnp.int32, (C, C), 0) == lax.broadcasted_iota(jnp.int32, (C, C), 1)
    factor = jnp.concatenate([band_mix[...], jnp.zeros((NB, C - NB), f32)], axis=1)
    factor = jnp.concatenate([factor, jnp.zeros((C - NB, C), f32)], axis=0)
    mix = eye.astype(f32) + lax.dot_general(
        factor, factor, (((1,), (1,)), ((), ())), precision=precise, preferred_element_type=f32
    )
    scales = [SQRT_HALF_LOG2E / lengthscales[i] for i in range(2)]
    diagonal = jnp.sum(jnp.where(eye, mix, 0.0), axis=1, keepdims=True)
    self_cov[...] = jnp.sum(hot * diagonal, axis=0, keepdims=True)
    hots = jnp.concatenate([hot, hot, hot, jnp.zeros_like(hot)], axis=0).astype(bf16)
    times = arrived[0:1, :] * scales[0]
    waves = arrived[1:2, :] * scales[1]
    width = points.shape[1]
    columns = jnp.concatenate(
        [points[...], point_bands[...].astype(f32), jnp.zeros((C - 3, width), f32)], axis=0
    ).T
    step = 128
    for j in range(0, width, step):
        here = columns[j : j + step, :]
        picked = jnp.zeros((step, C), f32)
        for kind in range(NB):
            picked = jnp.where(here[:, 2:3] == float(kind), mix[kind : kind + 1, :], picked)
        high = picked.astype(bf16).astype(f32)
        middle = (picked - high).astype(bf16).astype(f32)
        low = picked - high - middle
        split = jnp.concatenate([high, middle, low, jnp.zeros_like(low)], axis=1).astype(bf16)
        mixing = dot(split, hots)
        delta_t = times - here[:, 0:1] * scales[0]
        delta_w = waves - here[:, 1:2] * scales[1]
        value = jnp.exp2(-(delta_t * delta_t + delta_w * delta_w)) * mixing
        kt[j : j + step, :] = value.astype(bf16)


def whiten_kernel(places, kt, means, *rest):
    groups, (ab, stats, whole, turned) = rest[:-4], rest[-4:]
    width = whole.shape[0]
    store_pieces(groups, places, whole)
    for j in range(0, width, 256):
        turned[:, j : j + 256] = whole[j : j + 256, :].T

    @pl.loop(0, ROWS_DEV // COL)
    def _(step):
        columns = pl.ds(pl.multiple_of(step * COL, COL), COL)
        square = jnp.zeros((1, COL), f32)
        for k in range(0, width, 256):
            part = dot(turned[k : k + 256, :], kt[:, columns])
            square = square + jnp.sum(part * part, axis=0, keepdims=True)
            ab[k : k + 256, columns] = part.astype(bf16)
        stats[0:C, columns] = dot(means[...], ab[:, columns])
        stats[C : 2 * C, columns] = jnp.broadcast_to(-square, (C, COL))


def covary_kernel(places, ab, stats, *rest):
    groups, (bt, sums, whole, turned) = rest[:-4], rest[-4:]
    width = whole.shape[0]
    store_pieces(groups, places, whole)
    for j in range(0, width, 256):
        turned[:, j : j + 256] = whole[j : j + 256, :].T

    @pl.loop(0, ROWS_DEV // COL)
    def _(step):
        columns = pl.ds(pl.multiple_of(step * COL, COL), COL)
        square = stats[C : C + 1, columns]
        for l in range(0, width, 256):
            part = dot(turned[l : l + 256, l:], ab[l:, columns])
            square = square + jnp.sum(part * part, axis=0, keepdims=True)
            bt[l : l + 256, columns] = part.astype(bf16)
        sums[:, columns] = stats[0:C, columns]
        piece = ROWS_DEV // C
        for i in range(COL // piece):
            sums[pl.ds((COL // piece) * step + i, 1), ROWS_DEV:] = square[:, piece * i : piece * (i + 1)]


def slope_kernel(nz, own, other, scales, labels, self_cov, ab, bt, chances_out, mean, keep, send, heavy):
    total = own[...] + other[...]
    variance = jnp.concatenate([total[i : i + 1, ROWS_DEV:] for i in range(C)], axis=1) + self_cov[...]
    classes = lax.broadcasted_iota(jnp.int32, (C, 1), 0)
    scale = jnp.zeros((C, 1), f32)
    for i in range(C):
        scale = jnp.where(classes == i, scales[i], scale)
    logits = total[:, :ROWS_DEV] + 0.5 * scale * variance
    weights = jnp.exp(logits)
    chances = weights / jnp.sum(weights, axis=0, keepdims=True)
    chances_out[...] = chances
    twice = -jnp.sum(chances * scale, axis=0, keepdims=True)
    slope = ((labels[...] == classes).astype(f32) - chances).astype(bf16)
    core = lax.axis_index("obs") % 2
    block = ab.shape[0] // nz
    quarter = block // 4
    for z in range(nz):
        rows = slice(block * z, block * (z + 1))
        heavy[rows, :] = (bt[rows, :].astype(f32) * twice).astype(bf16)
        wide = block * (z + 1)
        start = block * z * (z + 1) // 2
        here = slice(start, start + wide)
        term = dot_nt(ab[rows, :], heavy[:wide, :])
        for x in range(2):
            even = term[2 * quarter * x : 2 * quarter * x + quarter, :]
            odd = term[2 * quarter * x + quarter : 2 * quarter * (x + 1), :]
            keep[quarter * x : quarter * (x + 1), here] = jnp.where(core == 0, even, odd)
            send[quarter * x : quarter * (x + 1), here] = jnp.where(core == 0, odd, even).astype(bf16)
    value = dot_nt(slope, ab[...])
    mean[...] = value
    send[2 * quarter :, : ab.shape[0]] = halves(value)


def halves(value):
    high = value.astype(bf16).astype(f32)
    return jnp.concatenate([high, value - high], axis=0).astype(bf16)


def joined(pair):
    return pair[:C].astype(f32) + pair[C:].astype(f32)


def pair_kernel(mean, keep, arrived, mean_out, total):
    rows, width = keep.shape[0], mean.shape[1]
    total[...] = keep[...] + arrived[:rows, :].astype(f32)
    mean_out[...] = mean[...] + joined(arrived[rows:, :width])


def part_of(nz, total, width, offset):
    target = lax.axis_index("obs") ^ offset
    rows = total.shape[0] // 2
    x, z = (target // 2) % 2, target // 4
    start = pl.multiple_of(width // nz * (z * (z + 1) // 2), width // nz)
    return total[pl.ds(pl.multiple_of(rows * x, rows), rows), pl.ds(start, width)]


def with_children(nz, total, width, offset, children, refs):
    rows = total.shape[0] // 2
    value = part_of(nz, total, width, offset)
    for source, slot in children:
        value = value + refs[source][rows * slot : rows * (slot + 1), :].astype(f32)
    return value


def level_kernel(nz, plan, mean_from, mean, total, *refs):
    outs = refs[len(refs) - len(plan) - 1 :]
    rows, width = total.shape[0] // 2, mean.shape[1]
    value = mean[...]
    if mean_from is not None:
        value = value + joined(refs[mean_from][refs[mean_from].shape[0] - 2 * C :, :])
    outs[0][...] = value
    for out, (pieces, with_mean) in zip(outs[1:], plan):
        for i, (offset, children) in enumerate(pieces):
            out[rows * i : rows * (i + 1), :] = with_children(nz, total, width, offset, children, refs).astype(bf16)
        if with_mean:
            out[rows * len(pieces) :, :] = halves(value)


class Scatter:
    def __init__(self, nz, mean, total):
        self.nz, self.mean, self.total = nz, mean, total
        self.arrived = {}
        self.mean_from = None

    def children(self, offset, arrays):
        found = []
        for child, (array, slot) in self.arrived.items():
            if child ^ (child & -child) == offset:
                if not any(array is other for other in arrays):
                    arrays.append(array)
                found.append(([array is other for other in arrays].index(True), slot))
        return found

    def level(self, sends, mean_bit):
        arrays = []
        plan = [([(o, self.children(o, arrays)) for o in offsets], offsets[0] & -offsets[0] == mean_bit and i == 0)
                for i, offsets in enumerate(sends)]
        mean_from = None
        if self.mean_from is not None:
            if not any(self.mean_from is other for other in arrays):
                arrays.append(self.mean_from)
            mean_from = [self.mean_from is other for other in arrays].index(True)
        rows, width = self.total.shape[0] // 2, self.mean.shape[1]
        self.mean, *outs = pl.pallas_call(
            functools.partial(level_kernel, self.nz, plan, mean_from),
            out_shape=[jax.ShapeDtypeStruct(self.mean.shape, f32)]
            + [jax.ShapeDtypeStruct((rows * len(pieces) + 2 * C * m, width), bf16) for pieces, m in plan],
            in_specs=[VMEM] * (2 + len(arrays)),
            out_specs=[VMEM] * (1 + len(plan)),
            compiler_params=SMALL,
            name="add_level",
        )(self.mean, self.total, *arrays)
        for i, (offsets, out) in enumerate(zip(sends, outs)):
            out = swap(out, "obs", offsets[0] & -offsets[0])
            self.arrived.update({offset: (out, slot) for slot, offset in enumerate(offsets)})
            if i == 0:
                self.mean_from = out


def finish_kernel(nz, children, mean_from, mean, total, chol, means, *refs):
    grad_chol, grad_mean = refs[-2:]
    rows, width = chol.shape
    value = with_children(nz, total, width, 0, children, refs)
    row_ids = lax.axis_index("obs") * rows + lax.broadcasted_iota(jnp.int32, (rows, width), 0)
    column_ids = lax.broadcasted_iota(jnp.int32, (rows, width), 1)
    own = chol[...].astype(f32)
    on_diag = column_ids == row_ids
    inverse = 1.0 / jnp.where(on_diag, own, 1.0)
    grad_chol[...] = jnp.where(column_ids <= row_ids, value, 0.0) - own + jnp.where(on_diag, inverse, 0.0)
    summed = mean[...] + joined(refs[mean_from][rows:, :])
    grad_mean[...] = summed - means[...].astype(f32)


def route(obs_coords, obs_codes, route_plan):
    devices = lax.axis_size("obs")
    stacked = pl.pallas_call(
        stack_kernel,
        out_shape=jax.ShapeDtypeStruct((3, obs_coords.shape[1]), f32),
        in_specs=[HBM, HBM],
        out_specs=VMEM,
        scratch_shapes=[
            pltpu.VMEM(obs_coords.shape, f32),
            pltpu.VMEM((1, obs_coords.shape[1]), jnp.int32),
            pltpu.SemaphoreType.DMA((2,)),
        ],
        compiler_params=SMALL,
        name="stack",
    )(obs_coords, obs_codes[None, :])
    if devices * SLOT == ROWS_DEV:
        return lax.all_to_all(stacked, "obs", split_axis=1, concat_axis=1, tiled=True)
    me = lax.axis_index("obs")
    blocks = route_plan * SLOT
    send_start = jnp.cumsum(blocks, axis=1) - blocks
    recv_start = jnp.cumsum(blocks, axis=0) - blocks
    my_sends = lax.dynamic_index_in_dim(send_start, me, 0, keepdims=False)
    my_recvs = lax.dynamic_index_in_dim(recv_start, me, 1, keepdims=False)
    padded = jnp.concatenate([stacked, jnp.zeros((3, SLOT), f32)], axis=1)
    outgoing = jax.vmap(lambda offset: lax.dynamic_slice_in_dim(padded, offset, SLOT, 1))(my_sends)
    incoming = lax.all_to_all(outgoing, "obs", split_axis=0, concat_axis=0, tiled=True)
    position = jnp.arange(ROWS_DEV, dtype=jnp.int32)
    sources = jnp.arange(devices, dtype=jnp.int32)
    source = jnp.sum((my_recvs[None, :] <= position[:, None]).astype(jnp.int32), axis=1) - 1
    pick = (source[:, None] == sources[None, :]).astype(jnp.int32)
    begin_row = jnp.sum(pick * my_recvs[None, :], axis=1)
    return incoming[source, :, position - begin_row].T


def body(
    obs_coords,
    obs_codes,
    route_plan,
    inducing_coords,
    inducing_bands,
    band_mix,
    lengthscales,
    class_scales,
    prior_factor,
    variational_chol,
    variational_mean,
):
    n = lax.axis_size("obs")
    nz = n // 4
    rows, width = variational_chol.shape
    gather = Gather((prior_factor, variational_chol), nz)
    arrived = gather.phase(0, lambda: route(obs_coords, obs_codes, route_plan))
    big = pltpu.CompilerParams(vmem_limit_bytes=16 * 1024 * 1024)
    cover = lambda: pl.pallas_call(
        kernel_rows_kernel,
        out_shape=(
            jax.ShapeDtypeStruct((width, ROWS_DEV), bf16),
            jax.ShapeDtypeStruct((1, ROWS_DEV), jnp.int32),
            jax.ShapeDtypeStruct((1, ROWS_DEV), f32),
        ),
        in_specs=[VMEM, HBM, HBM, HBM, SMEM],
        out_specs=(VMEM, VMEM, VMEM),
        scratch_shapes=[
            pltpu.VMEM((2, width), f32),
            pltpu.VMEM((1, width), jnp.int32),
            pltpu.VMEM((NB, NB), f32),
            pltpu.SemaphoreType.DMA((3,)),
        ],
        compiler_params=big,
        cost_estimate=pl.CostEstimate(
            flops=20 * width * ROWS_DEV, bytes_accessed=4 * 1024 * 1024, transcendentals=width * ROWS_DEV
        ),
        name="kernel_rows",
    )(arrived, inducing_coords, inducing_bands[None, :], band_mix, lengthscales)
    kt, labels, self_cov = gather.phase(1, cover)
    for number in range(2, len(gather.phases)):
        gather.phase(number)
    prior_arrays, prior_places = gather.of(0)
    chol_arrays, chol_places = gather.of(1)
    whole = [pltpu.VMEM((width, width), bf16), pltpu.VMEM((width, width), bf16)]
    ab, part_stats = pl.pallas_call(
        functools.partial(whiten_kernel, prior_places),
        out_shape=(
            jax.ShapeDtypeStruct((width, ROWS_DEV), bf16),
            jax.ShapeDtypeStruct((2 * C, ROWS_DEV), f32),
        ),
        in_specs=[VMEM] * (2 + len(prior_arrays)),
        out_specs=(VMEM, VMEM),
        scratch_shapes=whole,
        compiler_params=big,
        cost_estimate=pl.CostEstimate(
            flops=2 * width * width * ROWS_DEV, bytes_accessed=10 * 1024 * 1024, transcendentals=0
        ),
        name="whiten",
    )(kt, variational_mean, *prior_arrays)
    bt, sums = pl.pallas_call(
        functools.partial(covary_kernel, chol_places),
        out_shape=(
            jax.ShapeDtypeStruct((width, ROWS_DEV), bf16),
            jax.ShapeDtypeStruct((C, ROWS_DEV + ROWS_DEV // C), f32),
        ),
        in_specs=[VMEM] * (2 + len(chol_arrays)),
        out_specs=(VMEM, VMEM),
        scratch_shapes=whole,
        compiler_params=big,
        cost_estimate=pl.CostEstimate(
            flops=width * width * ROWS_DEV, bytes_accessed=10 * 1024 * 1024, transcendentals=0
        ),
        name="covary",
    )(ab, part_stats, *chol_arrays)

    other = swap(sums, "ind", 1)
    bit = 2
    while bit < lax.axis_size("ind"):
        sums = sums + other
        other = swap(sums, "ind", bit)
        bit *= 2

    packed = width // nz * (nz * (nz + 1) // 2)
    chances, mean, keep, send = pl.pallas_call(
        functools.partial(slope_kernel, nz),
        out_shape=[
            jax.ShapeDtypeStruct((C, ROWS_DEV), f32),
            jax.ShapeDtypeStruct((C, width), f32),
            jax.ShapeDtypeStruct((2 * rows, packed), f32),
            jax.ShapeDtypeStruct((2 * rows + 2 * C, packed), bf16),
        ],
        in_specs=[VMEM, VMEM, SMEM] + [VMEM] * 4,
        out_specs=[VMEM] * 4,
        scratch_shapes=[pltpu.VMEM((width, ROWS_DEV), bf16)],
        compiler_params=big,
        name="slopes",
    )(sums, other, class_scales, labels, self_cov, ab, bt)
    mean, total = pl.pallas_call(
        pair_kernel,
        out_shape=[jax.ShapeDtypeStruct(mean.shape, f32), jax.ShapeDtypeStruct(keep.shape, f32)],
        in_specs=[VMEM] * 3,
        out_specs=[VMEM] * 2,
        compiler_params=SMALL,
        name="add_pair",
    )(mean, keep, swap(send, "obs", 1))
    scatter = Scatter(nz, mean, total)
    along_x = [o for phase in reversed(gather.phases) for o in phase if o & 2]
    scatter.level([along_x[:1], along_x[1:-1], along_x[-1:]], 2)
    along_z = [[o for o in phase if not o & 2] for phase in gather.phases]
    along_z = [phase for phase in along_z if phase]
    for i, phase in enumerate(reversed(along_z)):
        bits = sorted({o & -o for o in phase}, reverse=True)
        scatter.level([[o for o in phase if o & -o == bit] for bit in bits], 4 << i)
    arrays = []
    children = scatter.children(0, arrays)
    mean_from = [scatter.mean_from is array for array in arrays].index(True)
    grad_chol, grad_mean = pl.pallas_call(
        functools.partial(finish_kernel, nz, children, mean_from),
        out_shape=(
            jax.ShapeDtypeStruct((rows, width), f32),
            jax.ShapeDtypeStruct((C, width), f32),
        ),
        in_specs=[VMEM] * (4 + len(arrays)),
        out_specs=(VMEM, VMEM),
        compiler_params=SMALL,
        name="finish",
    )(scatter.mean, total, variational_chol, variational_mean, *arrays)
    return (chances, grad_chol, grad_mean)


def solution(mesh):
    placed = (
        P(None, "obs"),
        P("obs"),
        P(),
        P(None, "ind"),
        P("ind"),
        P(),
        P(),
        P(),
        P(("ind", "obs"), None),
        P(("ind", "obs"), None),
        P(None, "ind"),
    )
    return jax.shard_map(
        body,
        mesh=mesh,
        in_specs=placed,
        out_specs=(P(None, "obs"), P(("ind", "obs"), None), P(None, "ind")),
        check_vma=False,
    )
```

```python
import functools

import jax
import jax.numpy as jnp
from jax import lax
from jax.experimental import pallas as pl
from jax.experimental.pallas import tpu as pltpu
from jax.sharding import PartitionSpec as P

C = 8
NB = 6
ROWS_DEV = 2048
SLOT = 128
COL = 1024
SQRT_HALF_LOG2E = 0.8493218002880191

precise = lax.Precision.HIGHEST
f32 = jnp.float32
bf16 = jnp.bfloat16
SMEM = pl.BlockSpec(memory_space=pltpu.SMEM)
VMEM = pl.BlockSpec(memory_space=pltpu.VMEM)
HBM = pl.BlockSpec(memory_space=pltpu.HBM)
SMALL = pltpu.CompilerParams(vmem_limit_bytes=4 * 1024 * 1024)


def dot(a, b):
    return jnp.dot(a, b, preferred_element_type=f32)


def dot_nt(a, b):
    return lax.dot_general(a, b, (((1,), (1,)), ((), ())), preferred_element_type=f32)


def swap(value, axis, bit):
    size = lax.axis_size(axis)
    return lax.ppermute(value, axis, [(i, i ^ bit) for i in range(size)])


def after(value, *earlier):
    return lax.optimization_barrier((value,) + earlier)[0]


def join_kernel(places, rows, *refs):
    out = refs[-1]
    for i, (source, slot) in enumerate(places):
        out[rows * i : rows * (i + 1), :] = refs[source][rows * slot : rows * (slot + 1), :]


def join(parts, rows):
    first = parts[0][0]
    if first.shape[0] == rows * len(parts) and parts == [(first, slot) for slot in range(len(parts))]:
        return first
    arrays = list({id(array): array for array, _ in parts}.values())
    places = [([array is other for other in arrays].index(True), slot) for array, slot in parts]
    return pl.pallas_call(
        functools.partial(join_kernel, places, rows),
        out_shape=jax.ShapeDtypeStruct((rows * len(parts), parts[0][0].shape[1]), parts[0][0].dtype),
        in_specs=[VMEM] * len(arrays),
        out_specs=VMEM,
        compiler_params=SMALL,
        name="join",
    )(*arrays)


def phases_of(nz):
    offsets = range(2, 4 * nz, 2)
    most = max(offset.bit_count() for offset in offsets)
    return [[o for o in reversed(offsets) if o.bit_count() == p] for p in range(1, most + 1)]


class Gather:
    def __init__(self, factors, nz):
        self.rows = factors[0].shape[0]
        own = join([(factor, 0) for factor in factors], self.rows)
        self.pieces = {(m, 0): (own, m) for m in range(2)}
        self.phases = phases_of(nz)
        self.groups = []

    def phase(self, number, beside=None):
        wanted = {}
        for offset in self.phases[number]:
            for m in range(2):
                bit = 4 if m == 1 and offset & 4 else offset & -offset
                wanted.setdefault(bit, []).append((m, offset))
        arrivals = {}
        for bit, keys in sorted(wanted.items(), reverse=True):
            sent = join([self.pieces[m, offset ^ bit] for m, offset in keys], self.rows)
            arrivals[bit] = swap(sent, "obs", bit)
        if beside is not None:
            arrivals, beside = lax.optimization_barrier((arrivals, beside()))
        new = [(0, 0), (1, 0)] if number == 0 else []
        for bit, keys in sorted(wanted.items()):
            self.pieces.update({key: (arrivals[bit], slot) for slot, key in enumerate(keys)})
            new += keys
        last = number == len(self.phases) - 1
        for part in [[key] for key in new] if last else [new]:
            group = join([self.pieces[key] for key in part], self.rows)
            self.groups.append((number, part, group, swap(group, "obs", 1)))
        return beside

    def of(self, m, number=None):
        arrays, places = [], []
        for at, new, *pair in self.groups:
            if number not in (None, at):
                continue
            slots = [(slot, offset) for slot, (owner, offset) in enumerate(new) if owner == m]
            for core, array in enumerate(pair):
                places += [(len(arrays), slot, offset ^ core) for slot, offset in slots]
                arrays += [array] if slots else []
        return arrays, places


def store_pieces(groups, places, whole):
    me = lax.axis_index("obs")
    rows = whole.shape[0] // len(places)
    for source, slot, offset in places:
        target = pl.ds(pl.multiple_of(rows * (me ^ offset), rows), rows)
        whole[target, :] = groups[source][rows * slot : rows * (slot + 1), :]


def stack_kernel(coords_in, codes_in, out, coords, codes, sems):
    fetch((coords_in, codes_in), (coords, codes), sems)
    out[0:2, :] = coords[...]
    out[2:3, :] = codes[...].astype(f32)


def fetch(sources, targets, sems):
    copies = [pltpu.make_async_copy(a, b, sems.at[i]) for i, (a, b) in enumerate(zip(sources, targets))]
    for copy in copies:
        copy.start()
    for copy in copies:
        copy.wait()


def kernel_rows_kernel(
    arrived, points_in, bands_in, mix_in, lengthscales, kt, labels, self_cov, points, point_bands, band_mix, sems
):
    fetch((points_in, bands_in, mix_in), (points, point_bands, band_mix), sems)
    codes = arrived[2:3, :]
    label = jnp.floor((codes + 0.5) * (1.0 / NB))
    labels[...] = label.astype(jnp.int32)
    bands = (codes - NB * label).astype(jnp.int32)
    kinds = lax.broadcasted_iota(jnp.int32, (C, ROWS_DEV), 0)
    hot = (kinds == bands).astype(f32)
    eye = lax.broadcasted_iota(jnp.int32, (C, C), 0) == lax.broadcasted_iota(jnp.int32, (C, C), 1)
    factor = jnp.concatenate([band_mix[...], jnp.zeros((NB, C - NB), f32)], axis=1)
    factor = jnp.concatenate([factor, jnp.zeros((C - NB, C), f32)], axis=0)
    mix = eye.astype(f32) + lax.dot_general(
        factor, factor, (((1,), (1,)), ((), ())), precision=precise, preferred_element_type=f32
    )
    scales = [SQRT_HALF_LOG2E / lengthscales[i] for i in range(2)]
    diagonal = jnp.sum(jnp.where(eye, mix, 0.0), axis=1, keepdims=True)
    self_cov[...] = jnp.sum(hot * diagonal, axis=0, keepdims=True)
    hots = jnp.concatenate([hot, hot, hot, jnp.zeros_like(hot)], axis=0).astype(bf16)
    times = arrived[0:1, :] * scales[0]
    waves = arrived[1:2, :] * scales[1]
    width = points.shape[1]
    columns = jnp.concatenate(
        [points[...], point_bands[...].astype(f32), jnp.zeros((C - 3, width), f32)], axis=0
    ).T
    step = 128
    for j in range(0, width, step):
        here = columns[j : j + step, :]
        picked = jnp.zeros((step, C), f32)
        for kind in range(NB):
            picked = jnp.where(here[:, 2:3] == float(kind), mix[kind : kind + 1, :], picked)
        high = picked.astype(bf16).astype(f32)
        middle = (picked - high).astype(bf16).astype(f32)
        low = picked - high - middle
        split = jnp.concatenate([high, middle, low, jnp.zeros_like(low)], axis=1).astype(bf16)
        mixing = dot(split, hots)
        delta_t = times - here[:, 0:1] * scales[0]
        delta_w = waves - here[:, 1:2] * scales[1]
        value = jnp.exp2(-(delta_t * delta_t + delta_w * delta_w)) * mixing
        kt[j : j + step, :] = value.astype(bf16)


def join_pairs(nz, number, places, groups, kt, factor, rows_of):
    me = lax.axis_index("obs")
    offsets = pair_offsets(nz, number)
    size = factor.shape[0] // len(offsets) // 2
    for source, slot, offset in places:
        base = 2 * size * offsets.index(offset & -2)
        target = pl.multiple_of(base + size * ((me ^ offset) & 1), size)
        factor[pl.ds(target, size), :] = groups[source][size * slot : size * (slot + 1), :]
    for i, offset in enumerate(offsets):
        here = pl.ds(pl.multiple_of(2 * size * ((me ^ offset) // 2), 2 * size), 2 * size)
        rows_of[2 * size * i : 2 * size * (i + 1), :] = kt[here, :]


def pair_offsets(nz, number):
    return ([0] if number == 0 else []) + phases_of(nz)[number]


def whiten_kernel(nz, number, places, kt, *refs):
    start = refs[:-4][0] if number > 0 else None
    groups, (total, factor, turned, met) = refs[(number > 0) : -4], refs[-4:]
    join_pairs(nz, number, places, groups, kt, factor, met)
    turned[...] = factor[...].T

    @pl.loop(0, ROWS_DEV // COL)
    def _(step):
        columns = pl.ds(pl.multiple_of(step * COL, COL), COL)
        for k in range(0, turned.shape[0], 256):
            part = dot(turned[k : k + 256, :], met[:, columns])
            if number > 0:
                part = part + start[k : k + 256, columns]
            total[k : k + 256, columns] = part


def covary_kernel(nz, last, last_places, places, kt, start, means, *refs):
    ab, bt, sums, factor, last_turned, met, whole, turned = refs[-8:]
    count = 1 + max(source for source, _, _ in last_places)
    last_groups, groups = refs[:count], refs[count:-8]
    width = whole.shape[0]
    join_pairs(nz, last, last_places, last_groups, kt, factor, met)
    last_turned[...] = factor[...].T
    store_pieces(groups, places, whole)
    for j in range(0, width, 256):
        turned[:, j : j + 256] = whole[j : j + 256, :].T

    @pl.loop(0, ROWS_DEV // COL)
    def _(step):
        columns = pl.ds(pl.multiple_of(step * COL, COL), COL)
        square = jnp.zeros((1, COL), f32)
        for k in range(0, width, 256):
            part = start[k : k + 256, columns] + dot(last_turned[k : k + 256, :], met[:, columns])
            square = square - jnp.sum(part * part, axis=0, keepdims=True)
            ab[k : k + 256, columns] = part.astype(bf16)
        sums[:, columns] = dot(means[...], ab[:, columns])
        for l in range(0, width, 256):
            part = dot(turned[l : l + 256, l:], ab[l:, columns])
            square = square + jnp.sum(part * part, axis=0, keepdims=True)
            bt[l : l + 256, columns] = part.astype(bf16)
        piece = ROWS_DEV // C
        for i in range(COL // piece):
            sums[pl.ds((COL // piece) * step + i, 1), ROWS_DEV:] = square[:, piece * i : piece * (i + 1)]


def outer_rows(nz, x, ab, heavy, picked, keep, send):
    core = lax.axis_index("obs") % 2
    block = ab.shape[0] // nz
    pair = block // 2
    for z in range(nz):
        picked[pair * z : pair * (z + 1), :] = ab[pl.ds(pl.multiple_of(block * z + pair * x, pair), pair), :]
    for chunk in range(nz):
        term = dot_nt(picked[pair * chunk :, :], heavy[block * chunk : block * (chunk + 1), :])
        for z in range(chunk, nz):
            left = block * (z * (z + 1) // 2 + chunk)
            top = pair * (z - chunk)
            even = term[top : top + pair // 2, :]
            odd = term[top + pair // 2 : top + pair, :]
            keep[:, left : left + block] = jnp.where(core == 0, even, odd)
            send[: pair // 2, left : left + block] = jnp.where(core == 0, odd, even).astype(bf16)


def slope_kernel(nz, own, other, scales, labels, self_cov, ab, bt, chances_out, mean, heavy, keep, send, picked):
    total = own[...] + other[...]
    variance = jnp.concatenate([total[i : i + 1, ROWS_DEV:] for i in range(C)], axis=1) + self_cov[...]
    classes = lax.broadcasted_iota(jnp.int32, (C, 1), 0)
    scale = jnp.zeros((C, 1), f32)
    for i in range(C):
        scale = jnp.where(classes == i, scales[i], scale)
    logits = total[:, :ROWS_DEV] + 0.5 * scale * variance
    weights = jnp.exp(logits)
    chances = weights / jnp.sum(weights, axis=0, keepdims=True)
    chances_out[...] = chances
    twice = -jnp.sum(chances * scale, axis=0, keepdims=True)
    slope = ((labels[...] == classes).astype(f32) - chances).astype(bf16)
    heavy[...] = (bt[...].astype(f32) * twice).astype(bf16)
    value = dot_nt(slope, ab[...])
    mean[...] = value
    send[keep.shape[0] :, : ab.shape[0]] = halves(value)
    outer_rows(nz, 1 - (lax.axis_index("obs") // 2) % 2, ab, heavy, picked, keep, send)


def near_kernel(nz, ab, heavy, keep, send, picked):
    outer_rows(nz, (lax.axis_index("obs") // 2) % 2, ab, heavy, picked, keep, send)


def halves(value):
    high = value.astype(bf16).astype(f32)
    return jnp.concatenate([high, value - high], axis=0).astype(bf16)


def joined(pair):
    return pair[:C].astype(f32) + pair[C:].astype(f32)


def pair_kernel(mean, keep, arrived, mean_out, total):
    rows, width = keep.shape[0], mean.shape[1]
    total[...] = keep[...] + arrived[:rows, :].astype(f32)
    mean_out[...] = mean[...] + joined(arrived[rows:, :width])


def near_pair_kernel(keep, arrived, total):
    total[...] = keep[...] + arrived[...].astype(f32)


def with_children(nz, totals, width, offset, children, refs):
    total = totals[(offset // 2) % 2]
    rows = total.shape[0]
    z = (lax.axis_index("obs") ^ offset) // 4
    start = pl.multiple_of(width // nz * (z * (z + 1) // 2), width // nz)
    value = total[:, pl.ds(start, width)]
    for source, slot in children:
        value = value + refs[source][rows * slot : rows * (slot + 1), :].astype(f32)
    return value


def mean_of(mean, refs, mean_from):
    if mean_from is None:
        return mean[...]
    arrived = refs[mean_from]
    if arrived.dtype == f32:
        return mean[...] + arrived[...]
    return mean[...] + joined(arrived[arrived.shape[0] - 2 * C :, :])


def level_kernel(nz, plan, mean_from, mean, near, far, *refs):
    outs = refs[len(refs) - len(plan) - 1 :]
    rows, width = far.shape[0], mean.shape[1]
    value = mean_of(mean, refs, mean_from)
    outs[0][...] = value
    for out, (pieces, with_mean) in zip(outs[1:], plan):
        for i, (offset, children) in enumerate(pieces):
            part = with_children(nz, (near, far), width, offset, children, refs)
            out[rows * i : rows * (i + 1), :] = part.astype(bf16)
        if with_mean:
            out[rows * len(pieces) :, :] = halves(value)


def index_in(arrays, array):
    for i, other in enumerate(arrays):
        if other is array:
            return i
    arrays.append(array)
    return len(arrays) - 1


class Scatter:
    def __init__(self, nz, mean):
        self.nz, self.mean = nz, mean
        self.arrived = {}
        self.mean_from = None

    def children(self, offset, arrays):
        return [
            (index_in(arrays, array), slot)
            for child, (array, slot) in self.arrived.items()
            if child ^ (child & -child) == offset
        ]

    def level(self, near, far, sends, mean_bit):
        arrays = []
        plan = [
            ([(o, self.children(o, arrays)) for o in offsets], offsets[0] & -offsets[0] == mean_bit)
            for offsets in sends
        ]
        mean_from = None if self.mean_from is None else index_in(arrays, self.mean_from)
        rows, width = far.shape[0], self.mean.shape[1]
        self.mean, *outs = pl.pallas_call(
            functools.partial(level_kernel, self.nz, plan, mean_from),
            out_shape=[jax.ShapeDtypeStruct(self.mean.shape, f32)]
            + [jax.ShapeDtypeStruct((rows * len(pieces) + 2 * C * m, width), bf16) for pieces, m in plan],
            in_specs=[VMEM] * (3 + len(arrays)),
            out_specs=[VMEM] * (1 + len(plan)),
            compiler_params=SMALL,
            name="add_level",
        )(self.mean, near, far, *arrays)
        for (pieces, with_mean), out in zip(plan, outs):
            offsets = [offset for offset, _ in pieces]
            out = swap(out, "obs", offsets[0] & -offsets[0])
            self.arrived.update({offset: (out, slot) for slot, offset in enumerate(offsets)})
            if with_mean:
                self.mean_from = out


def finish_kernel(nz, children, mean_from, mean, near, chol, means, *refs):
    grad_chol, grad_mean = refs[-2:]
    rows, width = chol.shape
    value = with_children(nz, (near, near), width, 0, children, refs)
    row_ids = lax.axis_index("obs") * rows + lax.broadcasted_iota(jnp.int32, (rows, width), 0)
    column_ids = lax.broadcasted_iota(jnp.int32, (rows, width), 1)
    own = chol[...].astype(f32)
    on_diag = column_ids == row_ids
    inverse = 1.0 / jnp.where(on_diag, own, 1.0)
    grad_chol[...] = jnp.where(column_ids <= row_ids, value, 0.0) - own + jnp.where(on_diag, inverse, 0.0)
    grad_mean[...] = mean_of(mean, refs, mean_from) - means[...].astype(f32)


def route(obs_coords, obs_codes, route_plan):
    devices = lax.axis_size("obs")
    stacked = pl.pallas_call(
        stack_kernel,
        out_shape=jax.ShapeDtypeStruct((3, obs_coords.shape[1]), f32),
        in_specs=[HBM, HBM],
        out_specs=VMEM,
        scratch_shapes=[
            pltpu.VMEM(obs_coords.shape, f32),
            pltpu.VMEM((1, obs_coords.shape[1]), jnp.int32),
            pltpu.SemaphoreType.DMA((2,)),
        ],
        compiler_params=SMALL,
        name="stack",
    )(obs_coords, obs_codes[None, :])
    if devices * SLOT == ROWS_DEV:
        return lax.all_to_all(stacked, "obs", split_axis=1, concat_axis=1, tiled=True)
    me = lax.axis_index("obs")
    blocks = route_plan * SLOT
    send_start = jnp.cumsum(blocks, axis=1) - blocks
    recv_start = jnp.cumsum(blocks, axis=0) - blocks
    my_sends = lax.dynamic_index_in_dim(send_start, me, 0, keepdims=False)
    my_recvs = lax.dynamic_index_in_dim(recv_start, me, 1, keepdims=False)
    padded = jnp.concatenate([stacked, jnp.zeros((3, SLOT), f32)], axis=1)
    outgoing = jax.vmap(lambda offset: lax.dynamic_slice_in_dim(padded, offset, SLOT, 1))(my_sends)
    incoming = lax.all_to_all(outgoing, "obs", split_axis=0, concat_axis=0, tiled=True)
    position = jnp.arange(ROWS_DEV, dtype=jnp.int32)
    sources = jnp.arange(devices, dtype=jnp.int32)
    source = jnp.sum((my_recvs[None, :] <= position[:, None]).astype(jnp.int32), axis=1) - 1
    pick = (source[:, None] == sources[None, :]).astype(jnp.int32)
    begin_row = jnp.sum(pick * my_recvs[None, :], axis=1)
    return incoming[source, :, position - begin_row].T


def body(
    obs_coords,
    obs_codes,
    route_plan,
    inducing_coords,
    inducing_bands,
    band_mix,
    lengthscales,
    class_scales,
    prior_factor,
    variational_chol,
    variational_mean,
):
    n = lax.axis_size("obs")
    nz = n // 4
    rows, width = variational_chol.shape
    gather = Gather((prior_factor, variational_chol), nz)
    arrived = gather.phase(0, lambda: route(obs_coords, obs_codes, route_plan))
    big = pltpu.CompilerParams(vmem_limit_bytes=16 * 1024 * 1024)
    cover = lambda: pl.pallas_call(
        kernel_rows_kernel,
        out_shape=(
            jax.ShapeDtypeStruct((width, ROWS_DEV), bf16),
            jax.ShapeDtypeStruct((1, ROWS_DEV), jnp.int32),
            jax.ShapeDtypeStruct((1, ROWS_DEV), f32),
        ),
        in_specs=[VMEM, HBM, HBM, HBM, SMEM],
        out_specs=(VMEM, VMEM, VMEM),
        scratch_shapes=[
            pltpu.VMEM((2, width), f32),
            pltpu.VMEM((1, width), jnp.int32),
            pltpu.VMEM((NB, NB), f32),
            pltpu.SemaphoreType.DMA((3,)),
        ],
        compiler_params=big,
        cost_estimate=pl.CostEstimate(
            flops=20 * width * ROWS_DEV, bytes_accessed=4 * 1024 * 1024, transcendentals=width * ROWS_DEV
        ),
        name="kernel_rows",
    )(arrived, inducing_coords, inducing_bands[None, :], band_mix, lengthscales)

    def whiten(number, kt, *start):
        arrays, places = gather.of(0, number)
        inner = 2 * rows * len(pair_offsets(nz, number))
        return pl.pallas_call(
            functools.partial(whiten_kernel, nz, number, places),
            out_shape=jax.ShapeDtypeStruct((width, ROWS_DEV), f32),
            in_specs=[VMEM] * (1 + len(start) + len(arrays)),
            out_specs=VMEM,
            scratch_shapes=[
                pltpu.VMEM((inner, width), bf16),
                pltpu.VMEM((width, inner), bf16),
                pltpu.VMEM((inner, ROWS_DEV), bf16),
            ],
            input_output_aliases={1: 0} if start else {},
            compiler_params=big,
            cost_estimate=pl.CostEstimate(
                flops=2 * width * inner * ROWS_DEV, bytes_accessed=10 * 1024 * 1024, transcendentals=0
            ),
            name="whiten",
        )(kt, *start, *arrays)

    def cover_and_whiten():
        kt, labels, self_cov = cover()
        return kt, labels, self_cov, whiten(0, kt)

    kt, labels, self_cov, whitened = gather.phase(1, cover_and_whiten)
    last = len(gather.phases) - 1
    for number in range(2, last + 1):
        whitened = gather.phase(number, lambda: whiten(number - 1, kt, whitened))
    last_arrays, last_places = gather.of(0, last)
    chol_arrays, chol_places = gather.of(1)
    ab, bt, sums = pl.pallas_call(
        functools.partial(covary_kernel, nz, last, last_places, chol_places),
        out_shape=(
            jax.ShapeDtypeStruct((width, ROWS_DEV), bf16),
            jax.ShapeDtypeStruct((width, ROWS_DEV), bf16),
            jax.ShapeDtypeStruct((C, ROWS_DEV + ROWS_DEV // C), f32),
        ),
        in_specs=[VMEM] * (3 + len(last_arrays) + len(chol_arrays)),
        out_specs=(VMEM, VMEM, VMEM),
        scratch_shapes=[
            pltpu.VMEM((2 * rows, width), bf16),
            pltpu.VMEM((width, 2 * rows), bf16),
            pltpu.VMEM((2 * rows, ROWS_DEV), bf16),
            pltpu.VMEM((width, width), bf16),
            pltpu.VMEM((width, width), bf16),
        ],
        compiler_params=big,
        cost_estimate=pl.CostEstimate(
            flops=width * width * ROWS_DEV, bytes_accessed=10 * 1024 * 1024, transcendentals=0
        ),
        name="covary",
    )(kt, whitened, variational_mean, *last_arrays, *chol_arrays)

    other = swap(sums, "ind", 1)
    bit = 2
    while bit < lax.axis_size("ind"):
        sums = sums + other
        other = swap(sums, "ind", bit)
        bit *= 2

    packed = width // nz * (nz * (nz + 1) // 2)
    kept = jax.ShapeDtypeStruct((rows, packed), f32)
    chances, mean, heavy, keep, send = pl.pallas_call(
        functools.partial(slope_kernel, nz),
        out_shape=[
            jax.ShapeDtypeStruct((C, ROWS_DEV), f32),
            jax.ShapeDtypeStruct((C, width), f32),
            jax.ShapeDtypeStruct((width, ROWS_DEV), bf16),
            kept,
            jax.ShapeDtypeStruct((rows + 2 * C, packed), bf16),
        ],
        in_specs=[VMEM, VMEM, SMEM] + [VMEM] * 4,
        out_specs=[VMEM] * 5,
        scratch_shapes=[pltpu.VMEM((width // 2, ROWS_DEV), bf16)],
        compiler_params=big,
        name="slopes",
    )(sums, other, class_scales, labels, self_cov, ab, bt)
    near_keep, near_send = pl.pallas_call(
        functools.partial(near_kernel, nz),
        out_shape=[kept, jax.ShapeDtypeStruct((rows, packed), bf16)],
        in_specs=[VMEM] * 2,
        out_specs=[VMEM] * 2,
        scratch_shapes=[pltpu.VMEM((width // 2, ROWS_DEV), bf16)],
        compiler_params=big,
        name="near_outer",
    )(ab, heavy)
    mean, far = pl.pallas_call(
        pair_kernel,
        out_shape=[jax.ShapeDtypeStruct(mean.shape, f32), kept],
        in_specs=[VMEM] * 3,
        out_specs=[VMEM] * 2,
        compiler_params=SMALL,
        name="add_pair",
    )(mean, keep, swap(send, "obs", 1))
    near = pl.pallas_call(
        near_pair_kernel,
        out_shape=kept,
        in_specs=[VMEM] * 2,
        out_specs=VMEM,
        compiler_params=SMALL,
        name="add_near_pair",
    )(near_keep, swap(near_send, "obs", 1))
    scatter = Scatter(nz, mean)
    along_x = [o for phase in reversed(gather.phases) for o in phase if o & 2]
    scatter.level(far, far, [along_x[:1], along_x[1:-1]], None)
    scatter.mean_from = swap(scatter.mean, "obs", 2 * nz)
    along_z = [[o for o in phase if not o & 2] for phase in gather.phases]
    along_z = [phase for phase in along_z if phase]
    for i, phase in enumerate(reversed(along_z)):
        bits = sorted({o & -o for o in phase}, reverse=True)
        sends = [[o for o in phase if o & -o == bit] for bit in bits]
        last_step = i == len(along_z) - 1
        scatter.level(near, far, sends + [along_x[-1:]] * last_step, 2 if last_step else 4 << i)
    arrays = []
    children = scatter.children(0, arrays)
    mean_from = index_in(arrays, scatter.mean_from)
    grad_chol, grad_mean = pl.pallas_call(
        functools.partial(finish_kernel, nz, children, mean_from),
        out_shape=(
            jax.ShapeDtypeStruct((rows, width), f32),
            jax.ShapeDtypeStruct((C, width), f32),
        ),
        in_specs=[VMEM] * (4 + len(arrays)),
        out_specs=(VMEM, VMEM),
        compiler_params=SMALL,
        name="finish",
    )(scatter.mean, near, variational_chol, variational_mean, *arrays)
    return (chances, grad_chol, grad_mean)


def solution(mesh):
    placed = (
        P(None, "obs"),
        P("obs"),
        P(),
        P(None, "ind"),
        P("ind"),
        P(),
        P(),
        P(),
        P(("ind", "obs"), None),
        P(("ind", "obs"), None),
        P(None, "ind"),
    )
    return jax.shard_map(
        body,
        mesh=mesh,
        in_specs=placed,
        out_specs=(P(None, "obs"), P(("ind", "obs"), None), P(None, "ind")),
        check_vma=False,
    )
```

```python
import functools

import jax
import jax.numpy as jnp
from jax import lax
from jax.experimental import pallas as pl
from jax.experimental.pallas import tpu as pltpu
from jax.sharding import PartitionSpec as P

C = 8
NB = 6
ROWS_DEV = 2048
SLOT = 128
COL = 2048
SQRT_HALF_LOG2E = 0.8493218002880191

precise = lax.Precision.HIGHEST
f32 = jnp.float32
bf16 = jnp.bfloat16
SMEM = pl.BlockSpec(memory_space=pltpu.SMEM)
VMEM = pl.BlockSpec(memory_space=pltpu.VMEM)
HBM = pl.BlockSpec(memory_space=pltpu.HBM)
SMALL = pltpu.CompilerParams(vmem_limit_bytes=4 * 1024 * 1024)


def dot(a, b):
    return jnp.dot(a, b, preferred_element_type=f32)


def dot_nt(a, b):
    return lax.dot_general(a, b, (((1,), (1,)), ((), ())), preferred_element_type=f32)


def swap(value, axis, bit):
    size = lax.axis_size(axis)
    return lax.ppermute(value, axis, [(i, i ^ bit) for i in range(size)])


def after(value, *earlier):
    return lax.optimization_barrier((value,) + earlier)[0]


def join_kernel(places, rows, *refs):
    out = refs[-1]
    for i, (source, slot) in enumerate(places):
        out[rows * i : rows * (i + 1), :] = refs[source][rows * slot : rows * (slot + 1), :]


def join(parts, rows):
    first = parts[0][0]
    if first.shape[0] == rows * len(parts) and parts == [(first, slot) for slot in range(len(parts))]:
        return first
    arrays = list({id(array): array for array, _ in parts}.values())
    places = [([array is other for other in arrays].index(True), slot) for array, slot in parts]
    return pl.pallas_call(
        functools.partial(join_kernel, places, rows),
        out_shape=jax.ShapeDtypeStruct((rows * len(parts), parts[0][0].shape[1]), parts[0][0].dtype),
        in_specs=[VMEM] * len(arrays),
        out_specs=VMEM,
        compiler_params=SMALL,
        name="join",
    )(*arrays)


def phases_of(nz):
    offsets = range(2, 4 * nz, 2)
    most = max(offset.bit_count() for offset in offsets)
    return [[o for o in reversed(offsets) if o.bit_count() == p] for p in range(1, most + 1)]


class Gather:
    def __init__(self, factors, nz):
        self.rows = factors[0].shape[0]
        own = join([(factor, 0) for factor in factors], self.rows)
        self.pieces = {(m, 0): (own, m) for m in range(2)}
        self.phases = phases_of(nz)
        self.groups = []

    def phase(self, number, beside=None):
        wanted = {}
        for offset in self.phases[number]:
            for m in range(2):
                bit = 4 if m == 1 and offset & 4 else offset & -offset
                wanted.setdefault(bit, []).append((m, offset))
        arrivals = {}
        for bit, keys in sorted(wanted.items()):
            sent = join([self.pieces[m, offset ^ bit] for m, offset in keys], self.rows)
            arrivals[bit] = swap(sent, "obs", bit)
        if beside is not None:
            arrivals, beside = lax.optimization_barrier((arrivals, beside()))
        new = [(0, 0), (1, 0)] if number == 0 else []
        for bit, keys in sorted(wanted.items()):
            self.pieces.update({key: (arrivals[bit], slot) for slot, key in enumerate(keys)})
            new += keys
        last = number == len(self.phases) - 1
        for part in [[key] for key in new] if last else [new]:
            group = join([self.pieces[key] for key in part], self.rows)
            self.groups.append((number, part, group, swap(group, "obs", 1)))
        return beside

    def of(self, m, number=None):
        arrays, places = [], []
        for at, new, *pair in self.groups:
            if number not in (None, at):
                continue
            slots = [(slot, offset) for slot, (owner, offset) in enumerate(new) if owner == m]
            for core, array in enumerate(pair):
                places += [(len(arrays), slot, offset ^ core) for slot, offset in slots]
                arrays += [array] if slots else []
        return arrays, places


def store_pieces(groups, places, whole):
    me = lax.axis_index("obs")
    rows = whole.shape[0] // len(places)
    for source, slot, offset in places:
        target = pl.ds(pl.multiple_of(rows * (me ^ offset), rows), rows)
        whole[target, :] = groups[source][rows * slot : rows * (slot + 1), :]


def stack_kernel(coords_in, codes_in, out, coords, codes, sems):
    fetch((coords_in, codes_in), (coords, codes), sems)
    out[0:2, :] = coords[...]
    out[2:3, :] = codes[...].astype(f32)


def fetch(sources, targets, sems):
    copies = [pltpu.make_async_copy(a, b, sems.at[i]) for i, (a, b) in enumerate(zip(sources, targets))]
    for copy in copies:
        copy.start()
    for copy in copies:
        copy.wait()


def cover_rows(nz, number, columns, table, mix, kt):
    me = lax.axis_index("obs")
    times, waves, bands = table[0:1, :], table[1:2, :], table[2:3, :]
    hot = (lax.broadcasted_iota(jnp.int32, (C, ROWS_DEV), 0).astype(f32) == bands).astype(f32)
    hots = jnp.concatenate([hot, hot, hot, jnp.zeros_like(hot)], axis=0).astype(bf16)
    offsets = pair_offsets(nz, number)
    step = kt.shape[0] // len(offsets)
    for i, offset in enumerate(offsets):
        here = columns[pl.ds(pl.multiple_of(step * ((me ^ offset) // 2), step), step), :]
        picked = jnp.zeros((step, C), f32)
        for kind in range(NB):
            picked = jnp.where(here[:, 2:3] == float(kind), mix[kind : kind + 1, :], picked)
        high = picked.astype(bf16).astype(f32)
        middle = (picked - high).astype(bf16).astype(f32)
        low = picked - high - middle
        split = jnp.concatenate([high, middle, low, jnp.zeros_like(low)], axis=1).astype(bf16)
        mixing = dot(split, hots)
        delta_t = times - here[:, 0:1]
        delta_w = waves - here[:, 1:2]
        value = jnp.exp2(-(delta_t * delta_t + delta_w * delta_w)) * mixing
        kt[step * i : step * (i + 1), :] = value.astype(bf16)


def first_rows_kernel(
    nz, arrived, points_in, bands_in, mix_in, lengthscales,
    kt, labels, self_cov, columns, table, mix, points, point_bands, band_mix, sems,
):
    fetch((points_in, bands_in, mix_in), (points, point_bands, band_mix), sems)
    codes = arrived[2:3, :]
    label = jnp.floor((codes + 0.5) * (1.0 / NB))
    labels[...] = label.astype(jnp.int32)
    bands = codes - NB * label
    hot = (lax.broadcasted_iota(jnp.int32, (C, ROWS_DEV), 0).astype(f32) == bands).astype(f32)
    eye = lax.broadcasted_iota(jnp.int32, (C, C), 0) == lax.broadcasted_iota(jnp.int32, (C, C), 1)
    factor = jnp.concatenate([band_mix[...], jnp.zeros((NB, C - NB), f32)], axis=1)
    factor = jnp.concatenate([factor, jnp.zeros((C - NB, C), f32)], axis=0)
    coupling = eye.astype(f32) + lax.dot_general(
        factor, factor, (((1,), (1,)), ((), ())), precision=precise, preferred_element_type=f32
    )
    mix[...] = coupling
    diagonal = jnp.sum(jnp.where(eye, coupling, 0.0), axis=1, keepdims=True)
    self_cov[...] = jnp.sum(hot * diagonal, axis=0, keepdims=True)
    scales = [SQRT_HALF_LOG2E / lengthscales[i] for i in range(2)]
    table[0:1, :] = arrived[0:1, :] * scales[0]
    table[1:2, :] = arrived[1:2, :] * scales[1]
    table[2:3, :] = bands
    width = points.shape[1]
    columns[...] = jnp.concatenate(
        [points[0:1, :] * scales[0], points[1:2, :] * scales[1], point_bands[...].astype(f32), jnp.zeros((C - 3, width), f32)],
        axis=0,
    ).T
    cover_rows(nz, 0, columns, table, mix, kt)


def more_rows_kernel(nz, columns, table, mix, *kts):
    for number, kt in enumerate(kts):
        cover_rows(nz, number + 1, columns, table, mix, kt)


def join_pairs(nz, number, places, groups, factor):
    me = lax.axis_index("obs")
    offsets = pair_offsets(nz, number)
    size = factor.shape[0] // len(offsets) // 2
    for source, slot, offset in places:
        base = 2 * size * offsets.index(offset & -2)
        target = pl.multiple_of(base + size * ((me ^ offset) & 1), size)
        factor[pl.ds(target, size), :] = groups[source][size * slot : size * (slot + 1), :]


def pair_offsets(nz, number):
    return ([0] if number == 0 else []) + phases_of(nz)[number]


def whiten_kernel(nz, number, places, kt, *refs):
    start = refs[0] if number > 0 else None
    groups, (total, factor, turned) = refs[(number > 0) : -3], refs[-3:]
    join_pairs(nz, number, places, groups, factor)
    turned[...] = factor[...].T

    @pl.loop(0, ROWS_DEV // COL)
    def _(step):
        columns = pl.ds(pl.multiple_of(step * COL, COL), COL)
        for k in range(0, turned.shape[0], 256):
            part = dot(turned[k : k + 256, :], kt[:, columns])
            if number > 0:
                part = part + start[k : k + 256, columns]
            total[k : k + 256, columns] = part


def covary_kernel(nz, last, last_places, places, kt, start, means, *refs):
    ab, bt, sums, factor, last_turned, whole, turned = refs[-7:]
    count = 1 + max(source for source, _, _ in last_places)
    last_groups, groups = refs[:count], refs[count:-7]
    width = whole.shape[0]
    join_pairs(nz, last, last_places, last_groups, factor)
    last_turned[...] = factor[...].T
    store_pieces(groups, places, whole)
    for j in range(0, width, 256):
        turned[:, j : j + 256] = whole[j : j + 256, :].T

    @pl.loop(0, ROWS_DEV // COL)
    def _(step):
        columns = pl.ds(pl.multiple_of(step * COL, COL), COL)
        square = jnp.zeros((1, COL), f32)
        for k in range(0, width, 256):
            part = start[k : k + 256, columns] + dot(last_turned[k : k + 256, :], kt[:, columns])
            square = square - jnp.sum(part * part, axis=0, keepdims=True)
            ab[k : k + 256, columns] = part.astype(bf16)
        sums[:, columns] = dot(means[...], ab[:, columns])
        for l in range(0, width, 256):
            part = dot(turned[l : l + 256, l:], ab[l:, columns])
            square = square + jnp.sum(part * part, axis=0, keepdims=True)
            bt[l : l + 256, columns] = part.astype(bf16)
        piece = ROWS_DEV // C
        for i in range(COL // piece):
            sums[pl.ds((COL // piece) * step + i, 1), ROWS_DEV:] = square[:, piece * i : piece * (i + 1)]


def outer_rows(nz, x, ab, heavy, picked, keep, send):
    core = lax.axis_index("obs") % 2
    block = ab.shape[0] // nz
    pair = block // 2
    for z in range(nz):
        picked[pair * z : pair * (z + 1), :] = ab[pl.ds(pl.multiple_of(block * z + pair * x, pair), pair), :]
    for chunk in range(nz):
        term = dot_nt(picked[pair * chunk :, :], heavy[block * chunk : block * (chunk + 1), :])
        for z in range(chunk, nz):
            left = block * (z * (z + 1) // 2 + chunk)
            top = pair * (z - chunk)
            even = term[top : top + pair // 2, :]
            odd = term[top + pair // 2 : top + pair, :]
            keep[:, left : left + block] = jnp.where(core == 0, even, odd)
            send[: pair // 2, left : left + block] = jnp.where(core == 0, odd, even).astype(bf16)


def blocks_at(values, bit, wanted):
    blocks = [i for i in range(values.shape[1] // SLOT) if bool(i & bit) == wanted]
    return {i: values[:, SLOT * i : SLOT * (i + 1)] for i in blocks}


def outgoing(state, width, bit):
    values = state[...]
    rows = [values[:, :width]]
    if values.shape[1] > width:
        rows.append(jnp.concatenate(list(blocks_at(values[:, width:], bit, True).values()), axis=1))
    return jnp.concatenate(rows, axis=0)


def absorbed(state, width, bit, arrived):
    values = state[...]
    mean = values[:, :width] + arrived[:C]
    if values.shape[1] == width:
        return mean
    blocks = blocks_at(values[:, width:], bit, False)
    came = blocks_at(values[:, width:], bit, True)
    blocks.update({i: arrived[C:, SLOT * at : SLOT * (at + 1)] for at, i in enumerate(came)})
    return jnp.concatenate([mean] + [blocks[i] for i in sorted(blocks)], axis=1)


def slope_kernel(nz, own, other, scales, labels, self_cov, ab, bt, chances_out, state, heavy, keep, send, picked):
    total = own[...] + other[...]
    variance = jnp.concatenate([total[i : i + 1, ROWS_DEV:] for i in range(C)], axis=1) + self_cov[...]
    classes = lax.broadcasted_iota(jnp.int32, (C, 1), 0)
    scale = jnp.zeros((C, 1), f32)
    for i in range(C):
        scale = jnp.where(classes == i, scales[i], scale)
    logits = total[:, :ROWS_DEV] + 0.5 * scale * variance
    weights = jnp.exp(logits)
    chances = weights / jnp.sum(weights, axis=0, keepdims=True)
    chances_out[...] = chances
    twice = -jnp.sum(chances * scale, axis=0, keepdims=True)
    slope = ((labels[...] == classes).astype(f32) - chances).astype(bf16)
    heavy[...] = (bt[...].astype(f32) * twice).astype(bf16)
    width = ab.shape[0]
    state[:, :width] = dot_nt(slope, ab[...])
    if state.shape[1] > width:
        for i in range(ROWS_DEV // SLOT):
            there = pl.ds(pl.multiple_of(SLOT * (lax.axis_index("obs") ^ i), SLOT), SLOT)
            state[:, width + SLOT * i : width + SLOT * (i + 1)] = chances_out[:, there]
    send[keep.shape[0] :, :width] = halves(outgoing(state, width, 1))
    outer_rows(nz, 1 - (lax.axis_index("obs") // 2) % 2, ab, heavy, picked, keep, send)


def near_kernel(nz, ab, heavy, keep, send, picked):
    outer_rows(nz, (lax.axis_index("obs") // 2) % 2, ab, heavy, picked, keep, send)


def halves(value):
    high = value.astype(bf16).astype(f32)
    return jnp.concatenate([high, value - high], axis=0).astype(bf16)


def joined(pair):
    rows = pair.shape[0] // 2
    return pair[:rows].astype(f32) + pair[rows:].astype(f32)


def pair_kernel(width, bit, state, keep, arrived, state_out, ahead, total):
    rows = keep.shape[0]
    total[...] = keep[...] + arrived[:rows, :].astype(f32)
    state_out[...] = absorbed(state, width, 1, joined(arrived[rows:, :width]))
    ahead[...] = outgoing(state_out, width, bit)


def near_pair_kernel(keep, arrived, total):
    total[...] = keep[...] + arrived[...].astype(f32)


def with_children(nz, totals, width, offset, children, refs):
    total = totals[(offset // 2) % 2]
    rows = total.shape[0]
    z = (lax.axis_index("obs") ^ offset) // 4
    start = pl.multiple_of(width // nz * (z * (z + 1) // 2), width // nz)
    value = total[:, pl.ds(start, width)]
    for source, slot in children:
        value = value + refs[source][rows * slot : rows * (slot + 1), :].astype(f32)
    return value


def state_of(state, refs, came, width):
    if came is None:
        return state[...]
    source, bit = came
    arrived = refs[source]
    if arrived.dtype == f32:
        return absorbed(state, width, bit, arrived[...])
    extra = 2 * C * (2 if state.shape[1] > width else 1)
    return absorbed(state, width, bit, joined(arrived[arrived.shape[0] - extra :, :]))


def level_kernel(nz, plan, came, bit, state, near, far, *refs):
    outs = refs[len(refs) - len(plan) - 1 :]
    rows = far.shape[0]
    width = outs[1].shape[1]
    outs[0][...] = state_of(state, refs, came, width)
    for out, (pieces, with_state) in zip(outs[1:], plan):
        for i, (offset, children) in enumerate(pieces):
            part = with_children(nz, (near, far), width, offset, children, refs)
            out[rows * i : rows * (i + 1), :] = part.astype(bf16)
        if with_state:
            out[rows * len(pieces) :, :] = halves(outgoing(outs[0], width, bit))


def index_in(arrays, array):
    for i, other in enumerate(arrays):
        if other is array:
            return i
    arrays.append(array)
    return len(arrays) - 1


class Scatter:
    def __init__(self, nz, width, state):
        self.nz, self.width, self.state = nz, width, state
        self.arrived = {}
        self.came = None

    def children(self, offset, arrays):
        return [
            (index_in(arrays, array), slot)
            for child, (array, slot) in self.arrived.items()
            if child ^ (child & -child) == offset
        ]

    def came_in(self, arrays):
        return None if self.came is None else (index_in(arrays, self.came[0]), self.came[1])

    def level(self, near, far, sends, bit):
        arrays = []
        plan = [
            ([(o, self.children(o, arrays)) for o in offsets], offsets[0] & -offsets[0] == bit)
            for offsets in sends
        ]
        came = self.came_in(arrays)
        rows = far.shape[0]
        extra = 2 * C * (2 if self.state.shape[1] > self.width else 1)
        self.state, *outs = pl.pallas_call(
            functools.partial(level_kernel, self.nz, plan, came, bit),
            out_shape=[jax.ShapeDtypeStruct(self.state.shape, f32)]
            + [jax.ShapeDtypeStruct((rows * len(pieces) + extra * m, self.width), bf16) for pieces, m in plan],
            in_specs=[VMEM] * (3 + len(arrays)),
            out_specs=[VMEM] * (1 + len(plan)),
            compiler_params=SMALL,
            name="add_level",
        )(self.state, near, far, *arrays)
        for (pieces, with_state), out in zip(plan, outs):
            offsets = [offset for offset, _ in pieces]
            out = swap(out, "obs", offsets[0] & -offsets[0])
            self.arrived.update({offset: (out, slot) for slot, offset in enumerate(offsets)})
            if with_state:
                self.came = (out, bit)


def finish_kernel(nz, children, came, state, near, chol, means, *refs):
    outs = refs[-3:] if state.shape[1] > chol.shape[1] else refs[-2:]
    grad_chol, grad_mean = outs[:2]
    rows, width = chol.shape
    value = with_children(nz, (near, near), width, 0, children, refs)
    row_ids = lax.axis_index("obs") * rows + lax.broadcasted_iota(jnp.int32, (rows, width), 0)
    column_ids = lax.broadcasted_iota(jnp.int32, (rows, width), 1)
    own = chol[...].astype(f32)
    on_diag = column_ids == row_ids
    inverse = 1.0 / jnp.where(on_diag, own, 1.0)
    grad_chol[...] = jnp.where(column_ids <= row_ids, value, 0.0) - own + jnp.where(on_diag, inverse, 0.0)
    values = state_of(state, refs, came, width)
    grad_mean[...] = values[:, :width] - means[...].astype(f32)
    for i in range((values.shape[1] - width) // SLOT):
        there = pl.ds(pl.multiple_of(SLOT * (lax.axis_index("obs") ^ i), SLOT), SLOT)
        outs[2][:, there] = values[:, width + SLOT * i : width + SLOT * (i + 1)]


def route(obs_coords, obs_codes, route_plan):
    devices = lax.axis_size("obs")
    stacked = pl.pallas_call(
        stack_kernel,
        out_shape=jax.ShapeDtypeStruct((3, obs_coords.shape[1]), f32),
        in_specs=[HBM, HBM],
        out_specs=VMEM,
        scratch_shapes=[
            pltpu.VMEM(obs_coords.shape, f32),
            pltpu.VMEM((1, obs_coords.shape[1]), jnp.int32),
            pltpu.SemaphoreType.DMA((2,)),
        ],
        compiler_params=SMALL,
        name="stack",
    )(obs_coords, obs_codes[None, :])
    if devices * SLOT == ROWS_DEV:
        return stacked
    me = lax.axis_index("obs")
    blocks = route_plan * SLOT
    send_start = jnp.cumsum(blocks, axis=1) - blocks
    recv_start = jnp.cumsum(blocks, axis=0) - blocks
    my_sends = lax.dynamic_index_in_dim(send_start, me, 0, keepdims=False)
    my_recvs = lax.dynamic_index_in_dim(recv_start, me, 1, keepdims=False)
    padded = jnp.concatenate([stacked, jnp.zeros((3, SLOT), f32)], axis=1)
    outgoing = jax.vmap(lambda offset: lax.dynamic_slice_in_dim(padded, offset, SLOT, 1))(my_sends)
    incoming = lax.all_to_all(outgoing, "obs", split_axis=0, concat_axis=0, tiled=True)
    position = jnp.arange(ROWS_DEV, dtype=jnp.int32)
    sources = jnp.arange(devices, dtype=jnp.int32)
    source = jnp.sum((my_recvs[None, :] <= position[:, None]).astype(jnp.int32), axis=1) - 1
    pick = (source[:, None] == sources[None, :]).astype(jnp.int32)
    begin_row = jnp.sum(pick * my_recvs[None, :], axis=1)
    return incoming[source, :, position - begin_row].T


def body(
    obs_coords,
    obs_codes,
    route_plan,
    inducing_coords,
    inducing_bands,
    band_mix,
    lengthscales,
    class_scales,
    prior_factor,
    variational_chol,
    variational_mean,
):
    n = lax.axis_size("obs")
    nz = n // 4
    rows, width = variational_chol.shape
    gather = Gather((prior_factor, variational_chol), nz)
    arrived = route(obs_coords, obs_codes, route_plan)
    big = pltpu.CompilerParams(vmem_limit_bytes=16 * 1024 * 1024)
    phases = range(len(gather.phases))
    covered = [
        jax.ShapeDtypeStruct((2 * rows * len(pair_offsets(nz, number)), ROWS_DEV), bf16) for number in phases
    ]
    cover = lambda: pl.pallas_call(
        functools.partial(first_rows_kernel, nz),
        out_shape=[
            covered[0],
            jax.ShapeDtypeStruct((1, ROWS_DEV), jnp.int32),
            jax.ShapeDtypeStruct((1, ROWS_DEV), f32),
            jax.ShapeDtypeStruct((width, C), f32),
            jax.ShapeDtypeStruct((C, ROWS_DEV), f32),
            jax.ShapeDtypeStruct((C, C), f32),
        ],
        in_specs=[VMEM, HBM, HBM, HBM, SMEM],
        out_specs=[VMEM] * 6,
        scratch_shapes=[
            pltpu.VMEM((2, width), f32),
            pltpu.VMEM((1, width), jnp.int32),
            pltpu.VMEM((NB, NB), f32),
            pltpu.SemaphoreType.DMA((3,)),
        ],
        compiler_params=big,
        cost_estimate=pl.CostEstimate(
            flops=10 * width * ROWS_DEV, bytes_accessed=2 * 1024 * 1024, transcendentals=width * ROWS_DEV // 2
        ),
        name="first_rows",
    )(arrived, inducing_coords, inducing_bands[None, :], band_mix, lengthscales)
    cover_more = lambda *given: pl.pallas_call(
        functools.partial(more_rows_kernel, nz),
        out_shape=covered[1:],
        in_specs=[VMEM] * 3,
        out_specs=[VMEM] * (len(covered) - 1),
        compiler_params=big,
        cost_estimate=pl.CostEstimate(
            flops=10 * width * ROWS_DEV, bytes_accessed=2 * 1024 * 1024, transcendentals=width * ROWS_DEV // 2
        ),
        name="more_rows",
    )(*given)

    def whiten(number, kt, *start):
        arrays, places = gather.of(0, number)
        inner = 2 * rows * len(pair_offsets(nz, number))
        return pl.pallas_call(
            functools.partial(whiten_kernel, nz, number, places),
            out_shape=jax.ShapeDtypeStruct((width, ROWS_DEV), f32),
            in_specs=[VMEM] * (1 + len(start) + len(arrays)),
            out_specs=VMEM,
            scratch_shapes=[
                pltpu.VMEM((inner, width), bf16),
                pltpu.VMEM((width, inner), bf16),
            ],
            input_output_aliases={1: 0} if start else {},
            compiler_params=big,
            cost_estimate=pl.CostEstimate(
                flops=2 * width * inner * ROWS_DEV, bytes_accessed=10 * 1024 * 1024, transcendentals=0
            ),
            name="whiten",
        )(kt, *start, *arrays)

    kt, labels, self_cov, *given = gather.phase(0, cover)
    last = len(gather.phases) - 1
    whitened, kts = gather.phase(1, lambda: (whiten(0, kt), cover_more(*given)))
    for number in range(2, last + 1):
        whitened = gather.phase(number, lambda: whiten(number - 1, kts[number - 2], whitened))
    last_arrays, last_places = gather.of(0, last)
    chol_arrays, chol_places = gather.of(1)
    ab, bt, sums = pl.pallas_call(
        functools.partial(covary_kernel, nz, last, last_places, chol_places),
        out_shape=(
            jax.ShapeDtypeStruct((width, ROWS_DEV), bf16),
            jax.ShapeDtypeStruct((width, ROWS_DEV), bf16),
            jax.ShapeDtypeStruct((C, ROWS_DEV + ROWS_DEV // C), f32),
        ),
        in_specs=[VMEM] * (3 + len(last_arrays) + len(chol_arrays)),
        out_specs=(VMEM, VMEM, VMEM),
        scratch_shapes=[
            pltpu.VMEM((2 * rows, width), bf16),
            pltpu.VMEM((width, 2 * rows), bf16),
            pltpu.VMEM((width, width), bf16),
            pltpu.VMEM((width, width), bf16),
        ],
        compiler_params=big,
        cost_estimate=pl.CostEstimate(
            flops=width * width * ROWS_DEV, bytes_accessed=10 * 1024 * 1024, transcendentals=0
        ),
        name="covary",
    )(kts[-1], whitened, variational_mean, *last_arrays, *chol_arrays)

    other = swap(sums, "ind", 1)
    bit = 2
    while bit < lax.axis_size("ind"):
        sums = sums + other
        other = swap(sums, "ind", bit)
        bit *= 2

    packed = width // nz * (nz * (nz + 1) // 2)
    kept = jax.ShapeDtypeStruct((rows, packed), f32)
    moving = n * SLOT == ROWS_DEV
    held = jax.ShapeDtypeStruct((C, width + ROWS_DEV * moving), f32)
    extra = C * (2 if moving else 1)
    chances, state, heavy, keep, send = pl.pallas_call(
        functools.partial(slope_kernel, nz),
        out_shape=[
            jax.ShapeDtypeStruct((C, ROWS_DEV), f32),
            held,
            jax.ShapeDtypeStruct((width, ROWS_DEV), bf16),
            kept,
            jax.ShapeDtypeStruct((rows + 2 * extra, packed), bf16),
        ],
        in_specs=[VMEM, VMEM, SMEM] + [VMEM] * 4,
        out_specs=[VMEM] * 5,
        scratch_shapes=[pltpu.VMEM((width // 2, ROWS_DEV), bf16)],
        compiler_params=big,
        name="slopes",
    )(sums, other, class_scales, labels, self_cov, ab, bt)
    near_keep, near_send = pl.pallas_call(
        functools.partial(near_kernel, nz),
        out_shape=[kept, jax.ShapeDtypeStruct((rows, packed), bf16)],
        in_specs=[VMEM] * 2,
        out_specs=[VMEM] * 2,
        scratch_shapes=[pltpu.VMEM((width // 2, ROWS_DEV), bf16)],
        compiler_params=big,
        name="near_outer",
    )(ab, heavy)
    state, ahead, far = pl.pallas_call(
        functools.partial(pair_kernel, width, 2 * nz),
        out_shape=[held, jax.ShapeDtypeStruct((extra, width), f32), kept],
        in_specs=[VMEM] * 3,
        out_specs=[VMEM] * 3,
        compiler_params=SMALL,
        name="add_pair",
    )(state, keep, swap(send, "obs", 1))
    near = pl.pallas_call(
        near_pair_kernel,
        out_shape=kept,
        in_specs=[VMEM] * 2,
        out_specs=VMEM,
        compiler_params=SMALL,
        name="add_near_pair",
    )(near_keep, swap(near_send, "obs", 1))
    scatter = Scatter(nz, width, state)
    ahead = swap(ahead, "obs", 2 * nz)
    along_x = [o for phase in reversed(gather.phases) for o in phase if o & 2]
    scatter.level(far, far, [along_x[:1], along_x[1:-1]], None)
    scatter.came = (ahead, 2 * nz)
    along_z = [[o for o in phase if not o & 2] for phase in gather.phases]
    along_z = [phase for phase in along_z if phase]
    for i, phase in enumerate(reversed(along_z)):
        bits = sorted({o & -o for o in phase}, reverse=True)
        sends = [[o for o in phase if o & -o == bit] for bit in bits]
        last_step = i == len(along_z) - 1
        scatter.level(near, far, sends + [along_x[-1:]] * last_step, 2 if last_step else 4 << i)
    arrays = []
    children = scatter.children(0, arrays)
    came = scatter.came_in(arrays)
    shapes = [jax.ShapeDtypeStruct((rows, width), f32), jax.ShapeDtypeStruct((C, width), f32)]
    if moving:
        shapes.append(jax.ShapeDtypeStruct((C, ROWS_DEV), f32))
    grad_chol, grad_mean, *moved = pl.pallas_call(
        functools.partial(finish_kernel, nz, children, came),
        out_shape=shapes,
        in_specs=[VMEM] * (4 + len(arrays)),
        out_specs=[VMEM] * len(shapes),
        compiler_params=SMALL,
        name="finish",
    )(scatter.state, near, variational_chol, variational_mean, *arrays)
    chances = moved[0] if moving else chances
    return (chances, grad_chol, grad_mean)


def solution(mesh):
    placed = (
        P(None, "obs"),
        P("obs"),
        P(),
        P(None, "ind"),
        P("ind"),
        P(),
        P(),
        P(),
        P(("ind", "obs"), None),
        P(("ind", "obs"), None),
        P(None, "ind"),
    )
    return jax.shard_map(
        body,
        mesh=mesh,
        in_specs=placed,
        out_specs=(P(None, "obs"), P(("ind", "obs"), None), P(None, "ind")),
        check_vma=False,
    )
```

```python
import functools

import jax
import jax.numpy as jnp
from jax import lax
from jax.experimental import pallas as pl
from jax.experimental.pallas import tpu as pltpu
from jax.sharding import PartitionSpec as P

C = 8
NB = 6
ROWS_DEV = 2048
SLOT = 128
COL = 2048
SQRT_HALF_LOG2E = 0.8493218002880191

precise = lax.Precision.HIGHEST
f32 = jnp.float32
bf16 = jnp.bfloat16
SMEM = pl.BlockSpec(memory_space=pltpu.SMEM)
VMEM = pl.BlockSpec(memory_space=pltpu.VMEM)
HBM = pl.BlockSpec(memory_space=pltpu.HBM)
SMALL = pltpu.CompilerParams(vmem_limit_bytes=4 * 1024 * 1024)


def dot(a, b):
    return jnp.dot(a, b, preferred_element_type=f32)


def dot_nt(a, b):
    return lax.dot_general(a, b, (((1,), (1,)), ((), ())), preferred_element_type=f32)


def swap(value, axis, bit):
    size = lax.axis_size(axis)
    return lax.ppermute(value, axis, [(i, i ^ bit) for i in range(size)])


def after(value, *earlier):
    return lax.optimization_barrier((value,) + earlier)[0]


def join_kernel(places, rows, *refs):
    out = refs[-1]
    for i, (source, slot) in enumerate(places):
        out[rows * i : rows * (i + 1), :] = refs[source][rows * slot : rows * (slot + 1), :]


def join(parts, rows):
    first = parts[0][0]
    if first.shape[0] == rows * len(parts) and parts == [(first, slot) for slot in range(len(parts))]:
        return first
    arrays = list({id(array): array for array, _ in parts}.values())
    places = [([array is other for other in arrays].index(True), slot) for array, slot in parts]
    return pl.pallas_call(
        functools.partial(join_kernel, places, rows),
        out_shape=jax.ShapeDtypeStruct((rows * len(parts), parts[0][0].shape[1]), parts[0][0].dtype),
        in_specs=[VMEM] * len(arrays),
        out_specs=VMEM,
        compiler_params=SMALL,
        name="join",
    )(*arrays)


def phases_of(nz):
    offsets = range(2, 4 * nz, 2)
    most = max(offset.bit_count() for offset in offsets)
    return [[o for o in reversed(offsets) if o.bit_count() == p] for p in range(1, most + 1)]


class Gather:
    def __init__(self, factors, nz):
        self.rows = factors[0].shape[0]
        own = join([(factor, 0) for factor in factors], self.rows)
        self.pieces = {(m, 0): (own, m) for m in range(2)}
        self.phases = phases_of(nz)
        self.groups = []

    def phase(self, number, beside=None):
        wanted = {}
        for offset in self.phases[number]:
            for m in range(2):
                bit = 4 if m == 1 and offset & 4 else offset & -offset
                wanted.setdefault(bit, []).append((m, offset))
        arrivals = {}
        for bit, keys in sorted(wanted.items()):
            sent = join([self.pieces[m, offset ^ bit] for m, offset in keys], self.rows)
            arrivals[bit] = swap(sent, "obs", bit)
        if beside is not None:
            arrivals, beside = lax.optimization_barrier((arrivals, beside()))
        new = [(0, 0), (1, 0)] if number == 0 else []
        for bit, keys in sorted(wanted.items()):
            self.pieces.update({key: (arrivals[bit], slot) for slot, key in enumerate(keys)})
            new += keys
        last = number == len(self.phases) - 1
        for part in [[key] for key in new] if last else [new]:
            group = join([self.pieces[key] for key in part], self.rows)
            self.groups.append((number, part, group, swap(group, "obs", 1)))
        return beside

    def of(self, m, number=None):
        arrays, places = [], []
        for at, new, *pair in self.groups:
            if number not in (None, at):
                continue
            slots = [(slot, offset) for slot, (owner, offset) in enumerate(new) if owner == m]
            for core, array in enumerate(pair):
                places += [(len(arrays), slot, offset ^ core) for slot, offset in slots]
                arrays += [array] if slots else []
        return arrays, places


def store_pieces(groups, places, whole):
    me = lax.axis_index("obs")
    rows = whole.shape[0] // len(places)
    for source, slot, offset in places:
        target = pl.ds(pl.multiple_of(rows * (me ^ offset), rows), rows)
        whole[target, :] = groups[source][rows * slot : rows * (slot + 1), :]


def stack_kernel(coords_in, codes_in, out, coords, codes, sems):
    fetch((coords_in, codes_in), (coords, codes), sems)
    out[0:2, :] = coords[...]
    out[2:3, :] = codes[...].astype(f32)


def fetch(sources, targets, sems):
    copies = [pltpu.make_async_copy(a, b, sems.at[i]) for i, (a, b) in enumerate(zip(sources, targets))]
    for copy in copies:
        copy.start()
    for copy in copies:
        copy.wait()


def cover_rows(nz, number, columns, table, mix, kt):
    me = lax.axis_index("obs")
    times, waves, bands = table[0:1, :], table[1:2, :], table[2:3, :]
    hot = (lax.broadcasted_iota(jnp.int32, (C, ROWS_DEV), 0).astype(f32) == bands).astype(f32)
    hots = jnp.concatenate([hot, hot, hot, jnp.zeros_like(hot)], axis=0).astype(bf16)
    offsets = pair_offsets(nz, number)
    step = kt.shape[0] // len(offsets)
    for i, offset in enumerate(offsets):
        here = columns[pl.ds(pl.multiple_of(step * ((me ^ offset) // 2), step), step), :]
        picked = jnp.zeros((step, C), f32)
        for kind in range(NB):
            picked = jnp.where(here[:, 2:3] == float(kind), mix[kind : kind + 1, :], picked)
        high = picked.astype(bf16).astype(f32)
        middle = (picked - high).astype(bf16).astype(f32)
        low = picked - high - middle
        split = jnp.concatenate([high, middle, low, jnp.zeros_like(low)], axis=1).astype(bf16)
        mixing = dot(split, hots)
        delta_t = times - here[:, 0:1]
        delta_w = waves - here[:, 1:2]
        value = jnp.exp2(-(delta_t * delta_t + delta_w * delta_w)) * mixing
        kt[step * i : step * (i + 1), :] = value.astype(bf16)


def first_rows_kernel(
    nz, arrived, points_in, bands_in, mix_in, lengthscales,
    kt, labels, self_cov, columns, table, mix, points, point_bands, band_mix, sems,
):
    fetch((points_in, bands_in, mix_in), (points, point_bands, band_mix), sems)
    codes = arrived[2:3, :]
    label = jnp.floor((codes + 0.5) * (1.0 / NB))
    labels[...] = label.astype(jnp.int32)
    bands = codes - NB * label
    hot = (lax.broadcasted_iota(jnp.int32, (C, ROWS_DEV), 0).astype(f32) == bands).astype(f32)
    eye = lax.broadcasted_iota(jnp.int32, (C, C), 0) == lax.broadcasted_iota(jnp.int32, (C, C), 1)
    factor = jnp.concatenate([band_mix[...], jnp.zeros((NB, C - NB), f32)], axis=1)
    factor = jnp.concatenate([factor, jnp.zeros((C - NB, C), f32)], axis=0)
    coupling = eye.astype(f32) + lax.dot_general(
        factor, factor, (((1,), (1,)), ((), ())), precision=precise, preferred_element_type=f32
    )
    mix[...] = coupling
    diagonal = jnp.sum(jnp.where(eye, coupling, 0.0), axis=1, keepdims=True)
    self_cov[...] = jnp.sum(hot * diagonal, axis=0, keepdims=True)
    scales = [SQRT_HALF_LOG2E / lengthscales[i] for i in range(2)]
    table[0:1, :] = arrived[0:1, :] * scales[0]
    table[1:2, :] = arrived[1:2, :] * scales[1]
    table[2:3, :] = bands
    width = points.shape[1]
    columns[...] = jnp.concatenate(
        [points[0:1, :] * scales[0], points[1:2, :] * scales[1], point_bands[...].astype(f32), jnp.zeros((C - 3, width), f32)],
        axis=0,
    ).T
    cover_rows(nz, 0, columns, table, mix, kt)


def more_rows_kernel(nz, columns, table, mix, *kts):
    for number, kt in enumerate(kts):
        cover_rows(nz, number + 1, columns, table, mix, kt)


def join_pairs(nz, number, places, groups, factor):
    me = lax.axis_index("obs")
    offsets = pair_offsets(nz, number)
    size = factor.shape[0] // len(offsets) // 2
    for source, slot, offset in places:
        base = 2 * size * offsets.index(offset & -2)
        target = pl.multiple_of(base + size * ((me ^ offset) & 1), size)
        factor[pl.ds(target, size), :] = groups[source][size * slot : size * (slot + 1), :]


def pair_offsets(nz, number):
    return ([0] if number == 0 else []) + phases_of(nz)[number]


def whiten_kernel(nz, number, places, kt, *refs):
    start = refs[0] if number > 0 else None
    groups, (total, factor, turned) = refs[(number > 0) : -3], refs[-3:]
    join_pairs(nz, number, places, groups, factor)
    turned[...] = factor[...].T

    @pl.loop(0, ROWS_DEV // COL)
    def _(step):
        columns = pl.ds(pl.multiple_of(step * COL, COL), COL)
        for k in range(0, turned.shape[0], 256):
            part = dot(turned[k : k + 256, :], kt[:, columns])
            if number > 0:
                part = part + start[k : k + 256, columns]
            total[k : k + 256, columns] = part


def covary_kernel(nz, last, last_places, places, kt, start, means, *refs):
    ab, bt, sums, factor, last_turned, whole, turned = refs[-7:]
    count = 1 + max(source for source, _, _ in last_places)
    last_groups, groups = refs[:count], refs[count:-7]
    width = whole.shape[0]
    join_pairs(nz, last, last_places, last_groups, factor)
    last_turned[...] = factor[...].T
    store_pieces(groups, places, whole)
    for j in range(0, width, 256):
        turned[:, j : j + 256] = whole[j : j + 256, :].T

    @pl.loop(0, ROWS_DEV // COL)
    def _(step):
        columns = pl.ds(pl.multiple_of(step * COL, COL), COL)
        square = jnp.zeros((1, COL), f32)
        for k in range(0, width, 256):
            part = start[k : k + 256, columns] + dot(last_turned[k : k + 256, :], kt[:, columns])
            square = square - jnp.sum(part * part, axis=0, keepdims=True)
            ab[k : k + 256, columns] = part.astype(bf16)
        for l in range(0, width, 256):
            rows = turned[l : l + 256, l:]
            if l == 0:
                rows = jnp.concatenate([rows, means[...], jnp.zeros_like(means)], axis=0)
            part = dot(rows, ab[l:, columns])
            if l == 0:
                sums[:, columns] = part[256 : 256 + C, :]
                part = part[:256, :]
            square = square + jnp.sum(part * part, axis=0, keepdims=True)
            bt[l : l + 256, columns] = part.astype(bf16)
        piece = ROWS_DEV // C
        for i in range(COL // piece):
            sums[pl.ds((COL // piece) * step + i, 1), ROWS_DEV:] = square[:, piece * i : piece * (i + 1)]


def outer_rows(nz, x, ab, heavy, picked, keep, send):
    core = lax.axis_index("obs") % 2
    block = ab.shape[0] // nz
    pair = block // 2
    for z in range(nz):
        picked[pair * z : pair * (z + 1), :] = ab[pl.ds(pl.multiple_of(block * z + pair * x, pair), pair), :]
    for chunk in range(nz):
        term = dot_nt(picked[pair * chunk :, :], heavy[block * chunk : block * (chunk + 1), :])
        for z in range(chunk, nz):
            left = block * (z * (z + 1) // 2 + chunk)
            top = pair * (z - chunk)
            even = term[top : top + pair // 2, :]
            odd = term[top + pair // 2 : top + pair, :]
            keep[:, left : left + block] = jnp.where(core == 0, even, odd)
            send[: pair // 2, left : left + block] = jnp.where(core == 0, odd, even).astype(bf16)


def blocks_at(values, bit, wanted):
    blocks = [i for i in range(values.shape[1] // SLOT) if bool(i & bit) == wanted]
    return {i: values[:, SLOT * i : SLOT * (i + 1)] for i in blocks}


def outgoing(state, width, bit):
    values = state[...]
    rows = [values[:, :width]]
    if values.shape[1] > width:
        rows.append(jnp.concatenate(list(blocks_at(values[:, width:], bit, True).values()), axis=1))
    return jnp.concatenate(rows, axis=0)


def absorbed(state, width, bit, arrived):
    values = state[...]
    mean = values[:, :width] + arrived[:C]
    if values.shape[1] == width:
        return mean
    blocks = blocks_at(values[:, width:], bit, False)
    came = blocks_at(values[:, width:], bit, True)
    blocks.update({i: arrived[C:, SLOT * at : SLOT * (at + 1)] for at, i in enumerate(came)})
    return jnp.concatenate([mean] + [blocks[i] for i in sorted(blocks)], axis=1)


def slope_kernel(nz, own, other, scales, labels, self_cov, ab, bt, chances_out, state, heavy, keep, send, picked):
    total = own[...] + other[...]
    variance = jnp.concatenate([total[i : i + 1, ROWS_DEV:] for i in range(C)], axis=1) + self_cov[...]
    classes = lax.broadcasted_iota(jnp.int32, (C, 1), 0)
    scale = jnp.zeros((C, 1), f32)
    for i in range(C):
        scale = jnp.where(classes == i, scales[i], scale)
    logits = total[:, :ROWS_DEV] + 0.5 * scale * variance
    weights = jnp.exp(logits)
    chances = weights / jnp.sum(weights, axis=0, keepdims=True)
    chances_out[...] = chances
    twice = -jnp.sum(chances * scale, axis=0, keepdims=True)
    slope = ((labels[...] == classes).astype(f32) - chances).astype(bf16)
    heavy[...] = (bt[...].astype(f32) * twice).astype(bf16)
    width = ab.shape[0]
    state[:, :width] = dot_nt(slope, ab[...])
    if state.shape[1] > width:
        for i in range(ROWS_DEV // SLOT):
            there = pl.ds(pl.multiple_of(SLOT * (lax.axis_index("obs") ^ i), SLOT), SLOT)
            state[:, width + SLOT * i : width + SLOT * (i + 1)] = chances_out[:, there]
    send[keep.shape[0] :, :width] = halves(outgoing(state, width, 1))
    outer_rows(nz, 1 - (lax.axis_index("obs") // 2) % 2, ab, heavy, picked, keep, send)


def near_kernel(nz, ab, heavy, keep, send, picked):
    outer_rows(nz, (lax.axis_index("obs") // 2) % 2, ab, heavy, picked, keep, send)


def halves(value):
    high = value.astype(bf16).astype(f32)
    return jnp.concatenate([high, value - high], axis=0).astype(bf16)


def joined(pair):
    rows = pair.shape[0] // 2
    return pair[:rows].astype(f32) + pair[rows:].astype(f32)


def pair_kernel(width, bit, state, keep, arrived, state_out, ahead, total):
    rows = keep.shape[0]
    total[...] = keep[...] + arrived[:rows, :].astype(f32)
    state_out[...] = absorbed(state, width, 1, joined(arrived[rows:, :width]))
    ahead[...] = outgoing(state_out, width, bit)


def near_pair_kernel(keep, arrived, total):
    total[...] = keep[...] + arrived[...].astype(f32)


def with_children(nz, totals, width, offset, children, refs):
    total = totals[(offset // 2) % 2]
    rows = total.shape[0]
    z = (lax.axis_index("obs") ^ offset) // 4
    start = pl.multiple_of(width // nz * (z * (z + 1) // 2), width // nz)
    value = total[:, pl.ds(start, width)]
    for source, slot in children:
        value = value + refs[source][rows * slot : rows * (slot + 1), :].astype(f32)
    return value


def state_of(state, refs, came, width):
    if came is None:
        return state[...]
    source, bit = came
    arrived = refs[source]
    if arrived.dtype == f32:
        return absorbed(state, width, bit, arrived[...])
    extra = 2 * C * (2 if state.shape[1] > width else 1)
    return absorbed(state, width, bit, joined(arrived[arrived.shape[0] - extra :, :]))


def level_kernel(nz, plan, came, bit, state, near, far, *refs):
    outs = refs[len(refs) - len(plan) - 1 :]
    rows = far.shape[0]
    width = outs[1].shape[1]
    outs[0][...] = state_of(state, refs, came, width)
    for out, (pieces, with_state) in zip(outs[1:], plan):
        for i, (offset, children) in enumerate(pieces):
            part = with_children(nz, (near, far), width, offset, children, refs)
            out[rows * i : rows * (i + 1), :] = part.astype(bf16)
        if with_state:
            out[rows * len(pieces) :, :] = halves(outgoing(outs[0], width, bit))


def index_in(arrays, array):
    for i, other in enumerate(arrays):
        if other is array:
            return i
    arrays.append(array)
    return len(arrays) - 1


class Scatter:
    def __init__(self, nz, width, state):
        self.nz, self.width, self.state = nz, width, state
        self.arrived = {}
        self.came = None

    def children(self, offset, arrays):
        return [
            (index_in(arrays, array), slot)
            for child, (array, slot) in self.arrived.items()
            if child ^ (child & -child) == offset
        ]

    def came_in(self, arrays):
        return None if self.came is None else (index_in(arrays, self.came[0]), self.came[1])

    def level(self, near, far, sends, bit):
        arrays = []
        plan = [
            ([(o, self.children(o, arrays)) for o in offsets], offsets[0] & -offsets[0] == bit)
            for offsets in sends
        ]
        came = self.came_in(arrays)
        rows = far.shape[0]
        extra = 2 * C * (2 if self.state.shape[1] > self.width else 1)
        self.state, *outs = pl.pallas_call(
            functools.partial(level_kernel, self.nz, plan, came, bit),
            out_shape=[jax.ShapeDtypeStruct(self.state.shape, f32)]
            + [jax.ShapeDtypeStruct((rows * len(pieces) + extra * m, self.width), bf16) for pieces, m in plan],
            in_specs=[VMEM] * (3 + len(arrays)),
            out_specs=[VMEM] * (1 + len(plan)),
            compiler_params=SMALL,
            name="add_level",
        )(self.state, near, far, *arrays)
        for (pieces, with_state), out in zip(plan, outs):
            offsets = [offset for offset, _ in pieces]
            out = swap(out, "obs", offsets[0] & -offsets[0])
            self.arrived.update({offset: (out, slot) for slot, offset in enumerate(offsets)})
            if with_state:
                self.came = (out, bit)


def finish_kernel(nz, children, came, state, near, chol, means, *refs):
    outs = refs[-3:] if state.shape[1] > chol.shape[1] else refs[-2:]
    grad_chol, grad_mean = outs[:2]
    rows, width = chol.shape
    value = with_children(nz, (near, near), width, 0, children, refs)
    row_ids = lax.axis_index("obs") * rows + lax.broadcasted_iota(jnp.int32, (rows, width), 0)
    column_ids = lax.broadcasted_iota(jnp.int32, (rows, width), 1)
    own = chol[...].astype(f32)
    on_diag = column_ids == row_ids
    inverse = 1.0 / jnp.where(on_diag, own, 1.0)
    grad_chol[...] = jnp.where(column_ids <= row_ids, value, 0.0) - own + jnp.where(on_diag, inverse, 0.0)
    values = state_of(state, refs, came, width)
    grad_mean[...] = values[:, :width] - means[...].astype(f32)
    for i in range((values.shape[1] - width) // SLOT):
        there = pl.ds(pl.multiple_of(SLOT * (lax.axis_index("obs") ^ i), SLOT), SLOT)
        outs[2][:, there] = values[:, width + SLOT * i : width + SLOT * (i + 1)]


def route(obs_coords, obs_codes, route_plan):
    devices = lax.axis_size("obs")
    stacked = pl.pallas_call(
        stack_kernel,
        out_shape=jax.ShapeDtypeStruct((3, obs_coords.shape[1]), f32),
        in_specs=[HBM, HBM],
        out_specs=VMEM,
        scratch_shapes=[
            pltpu.VMEM(obs_coords.shape, f32),
            pltpu.VMEM((1, obs_coords.shape[1]), jnp.int32),
            pltpu.SemaphoreType.DMA((2,)),
        ],
        compiler_params=SMALL,
        name="stack",
    )(obs_coords, obs_codes[None, :])
    if devices * SLOT == ROWS_DEV:
        return stacked
    me = lax.axis_index("obs")
    blocks = route_plan * SLOT
    send_start = jnp.cumsum(blocks, axis=1) - blocks
    recv_start = jnp.cumsum(blocks, axis=0) - blocks
    my_sends = lax.dynamic_index_in_dim(send_start, me, 0, keepdims=False)
    my_recvs = lax.dynamic_index_in_dim(recv_start, me, 1, keepdims=False)
    padded = jnp.concatenate([stacked, jnp.zeros((3, SLOT), f32)], axis=1)
    outgoing = jax.vmap(lambda offset: lax.dynamic_slice_in_dim(padded, offset, SLOT, 1))(my_sends)
    incoming = lax.all_to_all(outgoing, "obs", split_axis=0, concat_axis=0, tiled=True)
    position = jnp.arange(ROWS_DEV, dtype=jnp.int32)
    sources = jnp.arange(devices, dtype=jnp.int32)
    source = jnp.sum((my_recvs[None, :] <= position[:, None]).astype(jnp.int32), axis=1) - 1
    pick = (source[:, None] == sources[None, :]).astype(jnp.int32)
    begin_row = jnp.sum(pick * my_recvs[None, :], axis=1)
    return incoming[source, :, position - begin_row].T


def body(
    obs_coords,
    obs_codes,
    route_plan,
    inducing_coords,
    inducing_bands,
    band_mix,
    lengthscales,
    class_scales,
    prior_factor,
    variational_chol,
    variational_mean,
):
    n = lax.axis_size("obs")
    nz = n // 4
    rows, width = variational_chol.shape
    gather = Gather((prior_factor, variational_chol), nz)
    arrived = route(obs_coords, obs_codes, route_plan)
    big = pltpu.CompilerParams(vmem_limit_bytes=16 * 1024 * 1024)
    phases = range(len(gather.phases))
    covered = [
        jax.ShapeDtypeStruct((2 * rows * len(pair_offsets(nz, number)), ROWS_DEV), bf16) for number in phases
    ]
    cover = lambda: pl.pallas_call(
        functools.partial(first_rows_kernel, nz),
        out_shape=[
            covered[0],
            jax.ShapeDtypeStruct((1, ROWS_DEV), jnp.int32),
            jax.ShapeDtypeStruct((1, ROWS_DEV), f32),
            jax.ShapeDtypeStruct((width, C), f32),
            jax.ShapeDtypeStruct((C, ROWS_DEV), f32),
            jax.ShapeDtypeStruct((C, C), f32),
        ],
        in_specs=[VMEM, HBM, HBM, HBM, SMEM],
        out_specs=[VMEM] * 6,
        scratch_shapes=[
            pltpu.VMEM((2, width), f32),
            pltpu.VMEM((1, width), jnp.int32),
            pltpu.VMEM((NB, NB), f32),
            pltpu.SemaphoreType.DMA((3,)),
        ],
        compiler_params=big,
        cost_estimate=pl.CostEstimate(
            flops=10 * width * ROWS_DEV, bytes_accessed=2 * 1024 * 1024, transcendentals=width * ROWS_DEV // 2
        ),
        name="first_rows",
    )(arrived, inducing_coords, inducing_bands[None, :], band_mix, lengthscales)
    cover_more = lambda *given: pl.pallas_call(
        functools.partial(more_rows_kernel, nz),
        out_shape=covered[1:],
        in_specs=[VMEM] * 3,
        out_specs=[VMEM] * (len(covered) - 1),
        compiler_params=big,
        cost_estimate=pl.CostEstimate(
            flops=10 * width * ROWS_DEV, bytes_accessed=2 * 1024 * 1024, transcendentals=width * ROWS_DEV // 2
        ),
        name="more_rows",
    )(*given)

    def whiten(number, kt, *start):
        arrays, places = gather.of(0, number)
        inner = 2 * rows * len(pair_offsets(nz, number))
        return pl.pallas_call(
            functools.partial(whiten_kernel, nz, number, places),
            out_shape=jax.ShapeDtypeStruct((width, ROWS_DEV), f32),
            in_specs=[VMEM] * (1 + len(start) + len(arrays)),
            out_specs=VMEM,
            scratch_shapes=[
                pltpu.VMEM((inner, width), bf16),
                pltpu.VMEM((width, inner), bf16),
            ],
            input_output_aliases={1: 0} if start else {},
            compiler_params=big,
            cost_estimate=pl.CostEstimate(
                flops=2 * width * inner * ROWS_DEV, bytes_accessed=10 * 1024 * 1024, transcendentals=0
            ),
            name="whiten",
        )(kt, *start, *arrays)

    kt, labels, self_cov, *given = gather.phase(0, cover)
    last = len(gather.phases) - 1
    whitened, kts = gather.phase(1, lambda: (whiten(0, kt), cover_more(*given)))
    for number in range(2, last + 1):
        whitened = gather.phase(number, lambda: whiten(number - 1, kts[number - 2], whitened))
    last_arrays, last_places = gather.of(0, last)
    chol_arrays, chol_places = gather.of(1)
    ab, bt, sums = pl.pallas_call(
        functools.partial(covary_kernel, nz, last, last_places, chol_places),
        out_shape=(
            jax.ShapeDtypeStruct((width, ROWS_DEV), bf16),
            jax.ShapeDtypeStruct((width, ROWS_DEV), bf16),
            jax.ShapeDtypeStruct((C, ROWS_DEV + ROWS_DEV // C), f32),
        ),
        in_specs=[VMEM] * (3 + len(last_arrays) + len(chol_arrays)),
        out_specs=(VMEM, VMEM, VMEM),
        scratch_shapes=[
            pltpu.VMEM((2 * rows, width), bf16),
            pltpu.VMEM((width, 2 * rows), bf16),
            pltpu.VMEM((width, width), bf16),
            pltpu.VMEM((width, width), bf16),
        ],
        compiler_params=big,
        cost_estimate=pl.CostEstimate(
            flops=width * width * ROWS_DEV, bytes_accessed=10 * 1024 * 1024, transcendentals=0
        ),
        name="covary",
    )(kts[-1], whitened, variational_mean, *last_arrays, *chol_arrays)

    other = swap(sums, "ind", 1)
    bit = 2
    while bit < lax.axis_size("ind"):
        sums = sums + other
        other = swap(sums, "ind", bit)
        bit *= 2

    packed = width // nz * (nz * (nz + 1) // 2)
    kept = jax.ShapeDtypeStruct((rows, packed), f32)
    moving = n * SLOT == ROWS_DEV
    held = jax.ShapeDtypeStruct((C, width + ROWS_DEV * moving), f32)
    extra = C * (2 if moving else 1)
    chances, state, heavy, keep, send = pl.pallas_call(
        functools.partial(slope_kernel, nz),
        out_shape=[
            jax.ShapeDtypeStruct((C, ROWS_DEV), f32),
            held,
            jax.ShapeDtypeStruct((width, ROWS_DEV), bf16),
            kept,
            jax.ShapeDtypeStruct((rows + 2 * extra, packed), bf16),
        ],
        in_specs=[VMEM, VMEM, SMEM] + [VMEM] * 4,
        out_specs=[VMEM] * 5,
        scratch_shapes=[pltpu.VMEM((width // 2, ROWS_DEV), bf16)],
        compiler_params=big,
        name="slopes",
    )(sums, other, class_scales, labels, self_cov, ab, bt)
    near_keep, near_send = pl.pallas_call(
        functools.partial(near_kernel, nz),
        out_shape=[kept, jax.ShapeDtypeStruct((rows, packed), bf16)],
        in_specs=[VMEM] * 2,
        out_specs=[VMEM] * 2,
        scratch_shapes=[pltpu.VMEM((width // 2, ROWS_DEV), bf16)],
        compiler_params=big,
        name="near_outer",
    )(ab, heavy)
    state, ahead, far = pl.pallas_call(
        functools.partial(pair_kernel, width, 2 * nz),
        out_shape=[held, jax.ShapeDtypeStruct((extra, width), f32), kept],
        in_specs=[VMEM] * 3,
        out_specs=[VMEM] * 3,
        compiler_params=SMALL,
        name="add_pair",
    )(state, keep, swap(send, "obs", 1))
    near = pl.pallas_call(
        near_pair_kernel,
        out_shape=kept,
        in_specs=[VMEM] * 2,
        out_specs=VMEM,
        compiler_params=SMALL,
        name="add_near_pair",
    )(near_keep, swap(near_send, "obs", 1))
    scatter = Scatter(nz, width, state)
    ahead = swap(ahead, "obs", 2 * nz)
    along_x = [o for phase in reversed(gather.phases) for o in phase if o & 2]
    scatter.level(far, far, [along_x[:1], along_x[1:-1]], None)
    scatter.came = (ahead, 2 * nz)
    along_z = [[o for o in phase if not o & 2] for phase in gather.phases]
    along_z = [phase for phase in along_z if phase]
    for i, phase in enumerate(reversed(along_z)):
        bits = sorted({o & -o for o in phase}, reverse=True)
        sends = [[o for o in phase if o & -o == bit] for bit in bits]
        last_step = i == len(along_z) - 1
        scatter.level(near, far, sends + [along_x[-1:]] * last_step, 2 if last_step else 4 << i)
    arrays = []
    children = scatter.children(0, arrays)
    came = scatter.came_in(arrays)
    shapes = [jax.ShapeDtypeStruct((rows, width), f32), jax.ShapeDtypeStruct((C, width), f32)]
    if moving:
        shapes.append(jax.ShapeDtypeStruct((C, ROWS_DEV), f32))
    grad_chol, grad_mean, *moved = pl.pallas_call(
        functools.partial(finish_kernel, nz, children, came),
        out_shape=shapes,
        in_specs=[VMEM] * (4 + len(arrays)),
        out_specs=[VMEM] * len(shapes),
        compiler_params=SMALL,
        name="finish",
    )(scatter.state, near, variational_chol, variational_mean, *arrays)
    chances = moved[0] if moving else chances
    return (chances, grad_chol, grad_mean)


def solution(mesh):
    placed = (
        P(None, "obs"),
        P("obs"),
        P(),
        P(None, "ind"),
        P("ind"),
        P(),
        P(),
        P(),
        P(("ind", "obs"), None),
        P(("ind", "obs"), None),
        P(None, "ind"),
    )
    return jax.shard_map(
        body,
        mesh=mesh,
        in_specs=placed,
        out_specs=(P(None, "obs"), P(("ind", "obs"), None), P(None, "ind")),
        check_vma=False,
    )
```

```python
import functools

import jax
import jax.numpy as jnp
from jax import lax
from jax.experimental import pallas as pl
from jax.experimental.pallas import tpu as pltpu
from jax.sharding import PartitionSpec as P

C = 8
NB = 6
ROWS_DEV = 2048
SLOT = 128
COL = 2048
SQRT_HALF_LOG2E = 0.8493218002880191

precise = lax.Precision.HIGHEST
f32 = jnp.float32
bf16 = jnp.bfloat16
SMEM = pl.BlockSpec(memory_space=pltpu.SMEM)
VMEM = pl.BlockSpec(memory_space=pltpu.VMEM)
HBM = pl.BlockSpec(memory_space=pltpu.HBM)
SMALL = pltpu.CompilerParams(vmem_limit_bytes=4 * 1024 * 1024)


def dot(a, b):
    return jnp.dot(a, b, preferred_element_type=f32)


def dot_nt(a, b):
    return lax.dot_general(a, b, (((1,), (1,)), ((), ())), preferred_element_type=f32)


def swap(value, axis, bit):
    size = lax.axis_size(axis)
    return lax.ppermute(value, axis, [(i, i ^ bit) for i in range(size)])


def after(value, *earlier):
    return lax.optimization_barrier((value,) + earlier)[0]


def join_kernel(places, rows, *refs):
    out = refs[-1]
    for i, (source, slot) in enumerate(places):
        out[rows * i : rows * (i + 1), :] = refs[source][rows * slot : rows * (slot + 1), :]


def join(parts, rows):
    first = parts[0][0]
    if first.shape[0] == rows * len(parts) and parts == [(first, slot) for slot in range(len(parts))]:
        return first
    arrays = list({id(array): array for array, _ in parts}.values())
    places = [([array is other for other in arrays].index(True), slot) for array, slot in parts]
    return pl.pallas_call(
        functools.partial(join_kernel, places, rows),
        out_shape=jax.ShapeDtypeStruct((rows * len(parts), parts[0][0].shape[1]), parts[0][0].dtype),
        in_specs=[VMEM] * len(arrays),
        out_specs=VMEM,
        compiler_params=SMALL,
        name="join",
    )(*arrays)


def phases_of(nz):
    offsets = range(2, 4 * nz, 2)
    most = max(offset.bit_count() for offset in offsets)
    return [[o for o in reversed(offsets) if o.bit_count() == p] for p in range(1, most + 1)]


class Gather:
    def __init__(self, factors, nz):
        self.rows = factors[0].shape[0]
        own = join([(factor, 0) for factor in factors], self.rows)
        self.pieces = {(m, 0): (own, m) for m in range(2)}
        self.phases = phases_of(nz)
        self.groups = []

    def phase(self, number, beside=None):
        wanted = {}
        for offset in self.phases[number]:
            for m in range(2):
                bit = 4 if m == 1 and offset & 4 else offset & -offset
                wanted.setdefault(bit, []).append((m, offset))
        arrivals = {}
        for bit, keys in sorted(wanted.items()):
            sent = join([self.pieces[m, offset ^ bit] for m, offset in keys], self.rows)
            arrivals[bit] = swap(sent, "obs", bit)
        if beside is not None:
            arrivals, beside = lax.optimization_barrier((arrivals, beside()))
        new = [(0, 0), (1, 0)] if number == 0 else []
        for bit, keys in sorted(wanted.items()):
            self.pieces.update({key: (arrivals[bit], slot) for slot, key in enumerate(keys)})
            new += keys
        last = number == len(self.phases) - 1
        for part in [[key] for key in new] if last else [new]:
            group = join([self.pieces[key] for key in part], self.rows)
            self.groups.append((number, part, group, swap(group, "obs", 1)))
        return beside

    def of(self, m, number=None):
        arrays, places = [], []
        for at, new, *pair in self.groups:
            if number not in (None, at):
                continue
            slots = [(slot, offset) for slot, (owner, offset) in enumerate(new) if owner == m]
            for core, array in enumerate(pair):
                places += [(len(arrays), slot, offset ^ core) for slot, offset in slots]
                arrays += [array] if slots else []
        return arrays, places


def store_pieces(groups, places, whole):
    me = lax.axis_index("obs")
    rows = whole.shape[0] // len(places)
    for source, slot, offset in places:
        target = pl.ds(pl.multiple_of(rows * (me ^ offset), rows), rows)
        whole[target, :] = groups[source][rows * slot : rows * (slot + 1), :]


def stack_kernel(coords_in, codes_in, out, coords, codes, sems):
    fetch((coords_in, codes_in), (coords, codes), sems)
    out[0:2, :] = coords[...]
    out[2:3, :] = codes[...].astype(f32)


def fetch(sources, targets, sems):
    copies = [pltpu.make_async_copy(a, b, sems.at[i]) for i, (a, b) in enumerate(zip(sources, targets))]
    for copy in copies:
        copy.start()
    for copy in copies:
        copy.wait()


def cover_rows(nz, number, columns, table, mix, kt):
    me = lax.axis_index("obs")
    times, waves, bands = table[0:1, :], table[1:2, :], table[2:3, :]
    hot = (lax.broadcasted_iota(jnp.int32, (C, ROWS_DEV), 0).astype(f32) == bands).astype(f32)
    hots = jnp.concatenate([hot, hot, hot, jnp.zeros_like(hot)], axis=0).astype(bf16)
    offsets = pair_offsets(nz, number)
    step = kt.shape[0] // len(offsets)
    for i, offset in enumerate(offsets):
        here = columns[pl.ds(pl.multiple_of(step * ((me ^ offset) // 2), step), step), :]
        picked = jnp.zeros((step, C), f32)
        for kind in range(NB):
            picked = jnp.where(here[:, 2:3] == float(kind), mix[kind : kind + 1, :], picked)
        high = picked.astype(bf16).astype(f32)
        middle = (picked - high).astype(bf16).astype(f32)
        low = picked - high - middle
        split = jnp.concatenate([high, middle, low, jnp.zeros_like(low)], axis=1).astype(bf16)
        mixing = dot(split, hots)
        delta_t = times - here[:, 0:1]
        delta_w = waves - here[:, 1:2]
        value = jnp.exp2(-(delta_t * delta_t + delta_w * delta_w)) * mixing
        kt[step * i : step * (i + 1), :] = value.astype(bf16)


def first_rows_kernel(
    nz, arrived, points_in, bands_in, mix_in, lengthscales,
    kt, labels, self_cov, columns, table, mix, points, point_bands, band_mix, sems,
):
    fetch((points_in, bands_in, mix_in), (points, point_bands, band_mix), sems)
    codes = arrived[2:3, :]
    label = jnp.floor((codes + 0.5) * (1.0 / NB))
    labels[...] = label.astype(jnp.int32)
    bands = codes - NB * label
    hot = (lax.broadcasted_iota(jnp.int32, (C, ROWS_DEV), 0).astype(f32) == bands).astype(f32)
    eye = lax.broadcasted_iota(jnp.int32, (C, C), 0) == lax.broadcasted_iota(jnp.int32, (C, C), 1)
    factor = jnp.concatenate([band_mix[...], jnp.zeros((NB, C - NB), f32)], axis=1)
    factor = jnp.concatenate([factor, jnp.zeros((C - NB, C), f32)], axis=0)
    coupling = eye.astype(f32) + lax.dot_general(
        factor, factor, (((1,), (1,)), ((), ())), precision=precise, preferred_element_type=f32
    )
    mix[...] = coupling
    diagonal = jnp.sum(jnp.where(eye, coupling, 0.0), axis=1, keepdims=True)
    self_cov[...] = jnp.sum(hot * diagonal, axis=0, keepdims=True)
    scales = [SQRT_HALF_LOG2E / lengthscales[i] for i in range(2)]
    table[0:1, :] = arrived[0:1, :] * scales[0]
    table[1:2, :] = arrived[1:2, :] * scales[1]
    table[2:3, :] = bands
    width = points.shape[1]
    columns[...] = jnp.concatenate(
        [points[0:1, :] * scales[0], points[1:2, :] * scales[1], point_bands[...].astype(f32), jnp.zeros((C - 3, width), f32)],
        axis=0,
    ).T
    cover_rows(nz, 0, columns, table, mix, kt)


def more_rows_kernel(nz, columns, table, mix, *kts):
    for number, kt in enumerate(kts):
        cover_rows(nz, number + 1, columns, table, mix, kt)


def join_pairs(nz, number, places, groups, factor):
    me = lax.axis_index("obs")
    offsets = pair_offsets(nz, number)
    size = factor.shape[0] // len(offsets) // 2
    for source, slot, offset in places:
        base = 2 * size * offsets.index(offset & -2)
        target = pl.multiple_of(base + size * ((me ^ offset) & 1), size)
        factor[pl.ds(target, size), :] = groups[source][size * slot : size * (slot + 1), :]


def pair_offsets(nz, number):
    return ([0] if number == 0 else []) + phases_of(nz)[number]


def whiten_kernel(nz, number, places, kt, *refs):
    start = refs[0] if number > 0 else None
    groups, (total, factor, turned) = refs[(number > 0) : -3], refs[-3:]
    join_pairs(nz, number, places, groups, factor)
    turned[...] = factor[...].T

    @pl.loop(0, ROWS_DEV // COL)
    def _(step):
        columns = pl.ds(pl.multiple_of(step * COL, COL), COL)
        for k in range(0, turned.shape[0], 256):
            part = dot(turned[k : k + 256, :], kt[:, columns])
            if number > 0:
                part = part + start[k : k + 256, columns]
            total[k : k + 256, columns] = part


def covary_kernel(nz, last, last_places, places, kt, start, means, *refs):
    ab, bt, sums, factor, last_turned, whole, turned = refs[-7:]
    count = 1 + max(source for source, _, _ in last_places)
    last_groups, groups = refs[:count], refs[count:-7]
    width = whole.shape[0]
    join_pairs(nz, last, last_places, last_groups, factor)
    last_turned[...] = factor[...].T
    store_pieces(groups, places, whole)
    for j in range(0, width, 256):
        turned[:, j : j + 256] = whole[j : j + 256, :].T

    @pl.loop(0, ROWS_DEV // COL)
    def _(step):
        columns = pl.ds(pl.multiple_of(step * COL, COL), COL)
        square = jnp.zeros((1, COL), f32)
        for k in range(0, width, 512):
            part = start[k : k + 512, columns] + dot(last_turned[k : k + 512, :], kt[:, columns])
            square = square - jnp.sum(part * part, axis=0, keepdims=True)
            ab[k : k + 512, columns] = part.astype(bf16)
        for l in range(0, width, 256):
            rows = turned[l : l + 256, l:]
            if l == 0:
                rows = jnp.concatenate([rows, means[...], jnp.zeros_like(means)], axis=0)
            part = dot(rows, ab[l:, columns])
            if l == 0:
                sums[:, columns] = part[256 : 256 + C, :]
                part = part[:256, :]
            square = square + jnp.sum(part * part, axis=0, keepdims=True)
            bt[l : l + 256, columns] = part.astype(bf16)
        piece = ROWS_DEV // C
        for i in range(COL // piece):
            sums[pl.ds((COL // piece) * step + i, 1), ROWS_DEV:] = square[:, piece * i : piece * (i + 1)]


def outer_rows(nz, x, ab, heavy, picked, keep, send):
    core = lax.axis_index("obs") % 2
    block = ab.shape[0] // nz
    pair = block // 2
    for z in range(nz):
        picked[pair * z : pair * (z + 1), :] = ab[pl.ds(pl.multiple_of(block * z + pair * x, pair), pair), :]
    for chunk in range(nz):
        term = dot_nt(picked[pair * chunk :, :], heavy[block * chunk : block * (chunk + 1), :])
        for z in range(chunk, nz):
            left = block * (z * (z + 1) // 2 + chunk)
            top = pair * (z - chunk)
            even = term[top : top + pair // 2, :]
            odd = term[top + pair // 2 : top + pair, :]
            keep[:, left : left + block] = jnp.where(core == 0, even, odd)
            send[: pair // 2, left : left + block] = jnp.where(core == 0, odd, even).astype(bf16)


def blocks_at(values, bit, wanted):
    blocks = [i for i in range(values.shape[1] // SLOT) if bool(i & bit) == wanted]
    return {i: values[:, SLOT * i : SLOT * (i + 1)] for i in blocks}


def outgoing(state, width, bit):
    values = state[...]
    rows = [values[:, :width]]
    if values.shape[1] > width:
        rows.append(jnp.concatenate(list(blocks_at(values[:, width:], bit, True).values()), axis=1))
    return jnp.concatenate(rows, axis=0)


def absorbed(state, width, bit, arrived):
    values = state[...]
    mean = values[:, :width] + arrived[:C]
    if values.shape[1] == width:
        return mean
    blocks = blocks_at(values[:, width:], bit, False)
    came = blocks_at(values[:, width:], bit, True)
    blocks.update({i: arrived[C:, SLOT * at : SLOT * (at + 1)] for at, i in enumerate(came)})
    return jnp.concatenate([mean] + [blocks[i] for i in sorted(blocks)], axis=1)


def slope_kernel(nz, own, other, scales, labels, self_cov, ab, bt, chances_out, state, heavy, keep, send, picked):
    total = own[...] + other[...]
    variance = jnp.concatenate([total[i : i + 1, ROWS_DEV:] for i in range(C)], axis=1) + self_cov[...]
    classes = lax.broadcasted_iota(jnp.int32, (C, 1), 0)
    scale = jnp.zeros((C, 1), f32)
    for i in range(C):
        scale = jnp.where(classes == i, scales[i], scale)
    logits = total[:, :ROWS_DEV] + 0.5 * scale * variance
    weights = jnp.exp(logits)
    chances = weights / jnp.sum(weights, axis=0, keepdims=True)
    chances_out[...] = chances
    twice = -jnp.sum(chances * scale, axis=0, keepdims=True)
    slope = ((labels[...] == classes).astype(f32) - chances).astype(bf16)
    heavy[...] = (bt[...].astype(f32) * twice).astype(bf16)
    width = ab.shape[0]
    state[:, :width] = dot_nt(ab[...], slope).T
    if state.shape[1] > width:
        for i in range(ROWS_DEV // SLOT):
            there = pl.ds(pl.multiple_of(SLOT * (lax.axis_index("obs") ^ i), SLOT), SLOT)
            state[:, width + SLOT * i : width + SLOT * (i + 1)] = chances_out[:, there]
    send[keep.shape[0] :, :width] = halves(outgoing(state, width, 1))
    outer_rows(nz, 1 - (lax.axis_index("obs") // 2) % 2, ab, heavy, picked, keep, send)


def near_kernel(nz, ab, heavy, keep, send, picked):
    outer_rows(nz, (lax.axis_index("obs") // 2) % 2, ab, heavy, picked, keep, send)


def halves(value):
    high = value.astype(bf16).astype(f32)
    return jnp.concatenate([high, value - high], axis=0).astype(bf16)


def joined(pair):
    rows = pair.shape[0] // 2
    return pair[:rows].astype(f32) + pair[rows:].astype(f32)


def pair_kernel(width, bit, state, keep, arrived, state_out, ahead, total):
    rows = keep.shape[0]
    total[...] = keep[...] + arrived[:rows, :].astype(f32)
    state_out[...] = absorbed(state, width, 1, joined(arrived[rows:, :width]))
    ahead[...] = outgoing(state_out, width, bit)


def near_pair_kernel(keep, arrived, total):
    total[...] = keep[...] + arrived[...].astype(f32)


def with_children(nz, totals, width, offset, children, refs):
    total = totals[(offset // 2) % 2]
    rows = total.shape[0]
    z = (lax.axis_index("obs") ^ offset) // 4
    start = pl.multiple_of(width // nz * (z * (z + 1) // 2), width // nz)
    value = total[:, pl.ds(start, width)]
    for source, slot in children:
        value = value + refs[source][rows * slot : rows * (slot + 1), :].astype(f32)
    return value


def state_of(state, refs, came, width):
    if came is None:
        return state[...]
    source, bit = came
    arrived = refs[source]
    if arrived.dtype == f32:
        return absorbed(state, width, bit, arrived[...])
    extra = 2 * C * (2 if state.shape[1] > width else 1)
    return absorbed(state, width, bit, joined(arrived[arrived.shape[0] - extra :, :]))


def level_kernel(nz, plan, came, bit, state, near, far, *refs):
    outs = refs[len(refs) - len(plan) - 1 :]
    rows = far.shape[0]
    width = outs[1].shape[1]
    outs[0][...] = state_of(state, refs, came, width)
    for out, (pieces, with_state) in zip(outs[1:], plan):
        for i, (offset, children) in enumerate(pieces):
            part = with_children(nz, (near, far), width, offset, children, refs)
            out[rows * i : rows * (i + 1), :] = part.astype(bf16)
        if with_state:
            out[rows * len(pieces) :, :] = halves(outgoing(outs[0], width, bit))


def index_in(arrays, array):
    for i, other in enumerate(arrays):
        if other is array:
            return i
    arrays.append(array)
    return len(arrays) - 1


class Scatter:
    def __init__(self, nz, width, state):
        self.nz, self.width, self.state = nz, width, state
        self.arrived = {}
        self.came = None

    def children(self, offset, arrays):
        return [
            (index_in(arrays, array), slot)
            for child, (array, slot) in self.arrived.items()
            if child ^ (child & -child) == offset
        ]

    def came_in(self, arrays):
        return None if self.came is None else (index_in(arrays, self.came[0]), self.came[1])

    def level(self, near, far, sends, bit):
        arrays = []
        plan = [
            ([(o, self.children(o, arrays)) for o in offsets], offsets[0] & -offsets[0] == bit)
            for offsets in sends
        ]
        came = self.came_in(arrays)
        rows = far.shape[0]
        extra = 2 * C * (2 if self.state.shape[1] > self.width else 1)
        self.state, *outs = pl.pallas_call(
            functools.partial(level_kernel, self.nz, plan, came, bit),
            out_shape=[jax.ShapeDtypeStruct(self.state.shape, f32)]
            + [jax.ShapeDtypeStruct((rows * len(pieces) + extra * m, self.width), bf16) for pieces, m in plan],
            in_specs=[VMEM] * (3 + len(arrays)),
            out_specs=[VMEM] * (1 + len(plan)),
            compiler_params=SMALL,
            name="add_level",
        )(self.state, near, far, *arrays)
        for (pieces, with_state), out in zip(plan, outs):
            offsets = [offset for offset, _ in pieces]
            out = swap(out, "obs", offsets[0] & -offsets[0])
            self.arrived.update({offset: (out, slot) for slot, offset in enumerate(offsets)})
            if with_state:
                self.came = (out, bit)


def finish_kernel(nz, children, came, state, near, chol, means, *refs):
    outs = refs[-3:] if state.shape[1] > chol.shape[1] else refs[-2:]
    grad_chol, grad_mean = outs[:2]
    rows, width = chol.shape
    value = with_children(nz, (near, near), width, 0, children, refs)
    row_ids = lax.axis_index("obs") * rows + lax.broadcasted_iota(jnp.int32, (rows, width), 0)
    column_ids = lax.broadcasted_iota(jnp.int32, (rows, width), 1)
    own = chol[...].astype(f32)
    on_diag = column_ids == row_ids
    inverse = 1.0 / jnp.where(on_diag, own, 1.0)
    grad_chol[...] = jnp.where(column_ids <= row_ids, value, 0.0) - own + jnp.where(on_diag, inverse, 0.0)
    values = state_of(state, refs, came, width)
    grad_mean[...] = values[:, :width] - means[...].astype(f32)
    for i in range((values.shape[1] - width) // SLOT):
        there = pl.ds(pl.multiple_of(SLOT * (lax.axis_index("obs") ^ i), SLOT), SLOT)
        outs[2][:, there] = values[:, width + SLOT * i : width + SLOT * (i + 1)]


def route(obs_coords, obs_codes, route_plan):
    devices = lax.axis_size("obs")
    stacked = pl.pallas_call(
        stack_kernel,
        out_shape=jax.ShapeDtypeStruct((3, obs_coords.shape[1]), f32),
        in_specs=[HBM, HBM],
        out_specs=VMEM,
        scratch_shapes=[
            pltpu.VMEM(obs_coords.shape, f32),
            pltpu.VMEM((1, obs_coords.shape[1]), jnp.int32),
            pltpu.SemaphoreType.DMA((2,)),
        ],
        compiler_params=SMALL,
        name="stack",
    )(obs_coords, obs_codes[None, :])
    if devices * SLOT == ROWS_DEV:
        return stacked
    me = lax.axis_index("obs")
    blocks = route_plan * SLOT
    send_start = jnp.cumsum(blocks, axis=1) - blocks
    recv_start = jnp.cumsum(blocks, axis=0) - blocks
    my_sends = lax.dynamic_index_in_dim(send_start, me, 0, keepdims=False)
    my_recvs = lax.dynamic_index_in_dim(recv_start, me, 1, keepdims=False)
    padded = jnp.concatenate([stacked, jnp.zeros((3, SLOT), f32)], axis=1)
    outgoing = jax.vmap(lambda offset: lax.dynamic_slice_in_dim(padded, offset, SLOT, 1))(my_sends)
    incoming = lax.all_to_all(outgoing, "obs", split_axis=0, concat_axis=0, tiled=True)
    position = jnp.arange(ROWS_DEV, dtype=jnp.int32)
    sources = jnp.arange(devices, dtype=jnp.int32)
    source = jnp.sum((my_recvs[None, :] <= position[:, None]).astype(jnp.int32), axis=1) - 1
    pick = (source[:, None] == sources[None, :]).astype(jnp.int32)
    begin_row = jnp.sum(pick * my_recvs[None, :], axis=1)
    return incoming[source, :, position - begin_row].T


def body(
    obs_coords,
    obs_codes,
    route_plan,
    inducing_coords,
    inducing_bands,
    band_mix,
    lengthscales,
    class_scales,
    prior_factor,
    variational_chol,
    variational_mean,
):
    n = lax.axis_size("obs")
    nz = n // 4
    rows, width = variational_chol.shape
    gather = Gather((prior_factor, variational_chol), nz)
    arrived = route(obs_coords, obs_codes, route_plan)
    big = pltpu.CompilerParams(vmem_limit_bytes=16 * 1024 * 1024)
    phases = range(len(gather.phases))
    covered = [
        jax.ShapeDtypeStruct((2 * rows * len(pair_offsets(nz, number)), ROWS_DEV), bf16) for number in phases
    ]
    cover = lambda: pl.pallas_call(
        functools.partial(first_rows_kernel, nz),
        out_shape=[
            covered[0],
            jax.ShapeDtypeStruct((1, ROWS_DEV), jnp.int32),
            jax.ShapeDtypeStruct((1, ROWS_DEV), f32),
            jax.ShapeDtypeStruct((width, C), f32),
            jax.ShapeDtypeStruct((C, ROWS_DEV), f32),
            jax.ShapeDtypeStruct((C, C), f32),
        ],
        in_specs=[VMEM, HBM, HBM, HBM, SMEM],
        out_specs=[VMEM] * 6,
        scratch_shapes=[
            pltpu.VMEM((2, width), f32),
            pltpu.VMEM((1, width), jnp.int32),
            pltpu.VMEM((NB, NB), f32),
            pltpu.SemaphoreType.DMA((3,)),
        ],
        compiler_params=big,
        cost_estimate=pl.CostEstimate(
            flops=10 * width * ROWS_DEV, bytes_accessed=2 * 1024 * 1024, transcendentals=width * ROWS_DEV // 2
        ),
        name="first_rows",
    )(arrived, inducing_coords, inducing_bands[None, :], band_mix, lengthscales)
    cover_more = lambda *given: pl.pallas_call(
        functools.partial(more_rows_kernel, nz),
        out_shape=covered[1:],
        in_specs=[VMEM] * 3,
        out_specs=[VMEM] * (len(covered) - 1),
        compiler_params=big,
        cost_estimate=pl.CostEstimate(
            flops=10 * width * ROWS_DEV, bytes_accessed=2 * 1024 * 1024, transcendentals=width * ROWS_DEV // 2
        ),
        name="more_rows",
    )(*given)

    def whiten(number, kt, *start):
        arrays, places = gather.of(0, number)
        inner = 2 * rows * len(pair_offsets(nz, number))
        return pl.pallas_call(
            functools.partial(whiten_kernel, nz, number, places),
            out_shape=jax.ShapeDtypeStruct((width, ROWS_DEV), f32),
            in_specs=[VMEM] * (1 + len(start) + len(arrays)),
            out_specs=VMEM,
            scratch_shapes=[
                pltpu.VMEM((inner, width), bf16),
                pltpu.VMEM((width, inner), bf16),
            ],
            input_output_aliases={1: 0} if start else {},
            compiler_params=big,
            cost_estimate=pl.CostEstimate(
                flops=2 * width * inner * ROWS_DEV, bytes_accessed=10 * 1024 * 1024, transcendentals=0
            ),
            name="whiten",
        )(kt, *start, *arrays)

    kt, labels, self_cov, *given = gather.phase(0, cover)
    last = len(gather.phases) - 1
    whitened, kts = gather.phase(1, lambda: (whiten(0, kt), cover_more(*given)))
    for number in range(2, last + 1):
        whitened = gather.phase(number, lambda: whiten(number - 1, kts[number - 2], whitened))
    last_arrays, last_places = gather.of(0, last)
    chol_arrays, chol_places = gather.of(1)
    ab, bt, sums = pl.pallas_call(
        functools.partial(covary_kernel, nz, last, last_places, chol_places),
        out_shape=(
            jax.ShapeDtypeStruct((width, ROWS_DEV), bf16),
            jax.ShapeDtypeStruct((width, ROWS_DEV), bf16),
            jax.ShapeDtypeStruct((C, ROWS_DEV + ROWS_DEV // C), f32),
        ),
        in_specs=[VMEM] * (3 + len(last_arrays) + len(chol_arrays)),
        out_specs=(VMEM, VMEM, VMEM),
        scratch_shapes=[
            pltpu.VMEM((2 * rows, width), bf16),
            pltpu.VMEM((width, 2 * rows), bf16),
            pltpu.VMEM((width, width), bf16),
            pltpu.VMEM((width, width), bf16),
        ],
        compiler_params=big,
        cost_estimate=pl.CostEstimate(
            flops=width * width * ROWS_DEV, bytes_accessed=10 * 1024 * 1024, transcendentals=0
        ),
        name="covary",
    )(kts[-1], whitened, variational_mean, *last_arrays, *chol_arrays)

    other = swap(sums, "ind", 1)
    bit = 2
    while bit < lax.axis_size("ind"):
        sums = sums + other
        other = swap(sums, "ind", bit)
        bit *= 2

    packed = width // nz * (nz * (nz + 1) // 2)
    kept = jax.ShapeDtypeStruct((rows, packed), f32)
    moving = n * SLOT == ROWS_DEV
    held = jax.ShapeDtypeStruct((C, width + ROWS_DEV * moving), f32)
    extra = C * (2 if moving else 1)
    chances, state, heavy, keep, send = pl.pallas_call(
        functools.partial(slope_kernel, nz),
        out_shape=[
            jax.ShapeDtypeStruct((C, ROWS_DEV), f32),
            held,
            jax.ShapeDtypeStruct((width, ROWS_DEV), bf16),
            kept,
            jax.ShapeDtypeStruct((rows + 2 * extra, packed), bf16),
        ],
        in_specs=[VMEM, VMEM, SMEM] + [VMEM] * 4,
        out_specs=[VMEM] * 5,
        scratch_shapes=[pltpu.VMEM((width // 2, ROWS_DEV), bf16)],
        compiler_params=big,
        name="slopes",
    )(sums, other, class_scales, labels, self_cov, ab, bt)
    near_keep, near_send = pl.pallas_call(
        functools.partial(near_kernel, nz),
        out_shape=[kept, jax.ShapeDtypeStruct((rows, packed), bf16)],
        in_specs=[VMEM] * 2,
        out_specs=[VMEM] * 2,
        scratch_shapes=[pltpu.VMEM((width // 2, ROWS_DEV), bf16)],
        compiler_params=big,
        name="near_outer",
    )(ab, heavy)
    state, ahead, far = pl.pallas_call(
        functools.partial(pair_kernel, width, 2 * nz),
        out_shape=[held, jax.ShapeDtypeStruct((extra, width), f32), kept],
        in_specs=[VMEM] * 3,
        out_specs=[VMEM] * 3,
        compiler_params=SMALL,
        name="add_pair",
    )(state, keep, swap(send, "obs", 1))
    near = pl.pallas_call(
        near_pair_kernel,
        out_shape=kept,
        in_specs=[VMEM] * 2,
        out_specs=VMEM,
        compiler_params=SMALL,
        name="add_near_pair",
    )(near_keep, swap(near_send, "obs", 1))
    scatter = Scatter(nz, width, state)
    ahead = swap(ahead, "obs", 2 * nz)
    along_x = [o for phase in reversed(gather.phases) for o in phase if o & 2]
    scatter.level(far, far, [along_x[:1], along_x[1:-1]], None)
    scatter.came = (ahead, 2 * nz)
    along_z = [[o for o in phase if not o & 2] for phase in gather.phases]
    along_z = [phase for phase in along_z if phase]
    for i, phase in enumerate(reversed(along_z)):
        bits = sorted({o & -o for o in phase}, reverse=True)
        sends = [[o for o in phase if o & -o == bit] for bit in bits]
        last_step = i == len(along_z) - 1
        scatter.level(near, far, sends + [along_x[-1:]] * last_step, 2 if last_step else 4 << i)
    arrays = []
    children = scatter.children(0, arrays)
    came = scatter.came_in(arrays)
    shapes = [jax.ShapeDtypeStruct((rows, width), f32), jax.ShapeDtypeStruct((C, width), f32)]
    if moving:
        shapes.append(jax.ShapeDtypeStruct((C, ROWS_DEV), f32))
    grad_chol, grad_mean, *moved = pl.pallas_call(
        functools.partial(finish_kernel, nz, children, came),
        out_shape=shapes,
        in_specs=[VMEM] * (4 + len(arrays)),
        out_specs=[VMEM] * len(shapes),
        compiler_params=SMALL,
        name="finish",
    )(scatter.state, near, variational_chol, variational_mean, *arrays)
    chances = moved[0] if moving else chances
    return (chances, grad_chol, grad_mean)


def solution(mesh):
    placed = (
        P(None, "obs"),
        P("obs"),
        P(),
        P(None, "ind"),
        P("ind"),
        P(),
        P(),
        P(),
        P(("ind", "obs"), None),
        P(("ind", "obs"), None),
        P(None, "ind"),
    )
    return jax.shard_map(
        body,
        mesh=mesh,
        in_specs=placed,
        out_specs=(P(None, "obs"), P(("ind", "obs"), None), P(None, "ind")),
        check_vma=False,
    )
```

```python
import functools

import jax
import jax.numpy as jnp
from jax import lax
from jax.experimental import pallas as pl
from jax.experimental.pallas import tpu as pltpu
from jax.sharding import PartitionSpec as P

C = 8
NB = 6
ROWS_DEV = 2048
SLOT = 128
COL = 2048
SQRT_HALF_LOG2E = 0.8493218002880191

precise = lax.Precision.HIGHEST
f32 = jnp.float32
bf16 = jnp.bfloat16
SMEM = pl.BlockSpec(memory_space=pltpu.SMEM)
VMEM = pl.BlockSpec(memory_space=pltpu.VMEM)
HBM = pl.BlockSpec(memory_space=pltpu.HBM)
SMALL = pltpu.CompilerParams(vmem_limit_bytes=4 * 1024 * 1024)


def dot(a, b):
    return jnp.dot(a, b, preferred_element_type=f32)


def dot_nt(a, b):
    return lax.dot_general(a, b, (((1,), (1,)), ((), ())), preferred_element_type=f32)


def swap(value, axis, bit):
    size = lax.axis_size(axis)
    return lax.ppermute(value, axis, [(i, i ^ bit) for i in range(size)])


def after(value, *earlier):
    return lax.optimization_barrier((value,) + earlier)[0]


def join_kernel(places, rows, *refs):
    out = refs[-1]
    for i, (source, slot) in enumerate(places):
        out[rows * i : rows * (i + 1), :] = refs[source][rows * slot : rows * (slot + 1), :]


def join(parts, rows):
    first = parts[0][0]
    if first.shape[0] == rows * len(parts) and parts == [(first, slot) for slot in range(len(parts))]:
        return first
    arrays = list({id(array): array for array, _ in parts}.values())
    places = [([array is other for other in arrays].index(True), slot) for array, slot in parts]
    return pl.pallas_call(
        functools.partial(join_kernel, places, rows),
        out_shape=jax.ShapeDtypeStruct((rows * len(parts), parts[0][0].shape[1]), parts[0][0].dtype),
        in_specs=[VMEM] * len(arrays),
        out_specs=VMEM,
        compiler_params=SMALL,
        name="join",
    )(*arrays)


def phases_of(nz):
    offsets = range(2, 4 * nz, 2)
    most = max(offset.bit_count() for offset in offsets)
    return [[o for o in reversed(offsets) if o.bit_count() == p] for p in range(1, most + 1)]


class Gather:
    def __init__(self, factors, nz):
        self.rows = factors[0].shape[0]
        own = join([(factor, 0) for factor in factors], self.rows)
        self.pieces = {(m, 0): (own, m) for m in range(2)}
        self.phases = phases_of(nz)
        self.groups = []

    def phase(self, number, beside=None):
        wanted = {}
        for offset in self.phases[number]:
            for m in range(2):
                bit = 4 if m == 1 and offset & 4 else offset & -offset
                wanted.setdefault(bit, []).append((m, offset))
        arrivals = {}
        for bit, keys in sorted(wanted.items()):
            sent = join([self.pieces[m, offset ^ bit] for m, offset in keys], self.rows)
            arrivals[bit] = swap(sent, "obs", bit)
        if beside is not None:
            arrivals, beside = lax.optimization_barrier((arrivals, beside()))
        new = [(0, 0), (1, 0)] if number == 0 else []
        for bit, keys in sorted(wanted.items()):
            self.pieces.update({key: (arrivals[bit], slot) for slot, key in enumerate(keys)})
            new += keys
        last = number == len(self.phases) - 1
        for part in [[key] for key in new] if last else [new]:
            group = join([self.pieces[key] for key in part], self.rows)
            self.groups.append((number, part, group, swap(group, "obs", 1)))
        return beside

    def of(self, m, number=None):
        arrays, places = [], []
        for at, new, *pair in self.groups:
            if number not in (None, at):
                continue
            slots = [(slot, offset) for slot, (owner, offset) in enumerate(new) if owner == m]
            for core, array in enumerate(pair):
                places += [(len(arrays), slot, offset ^ core) for slot, offset in slots]
                arrays += [array] if slots else []
        return arrays, places


def store_pieces(groups, places, whole):
    me = lax.axis_index("obs")
    rows = whole.shape[0] // len(places)
    for source, slot, offset in places:
        target = pl.ds(pl.multiple_of(rows * (me ^ offset), rows), rows)
        whole[target, :] = groups[source][rows * slot : rows * (slot + 1), :]


def stack_kernel(coords_in, codes_in, out, coords, codes, sems):
    fetch((coords_in, codes_in), (coords, codes), sems)
    out[0:2, :] = coords[...]
    out[2:3, :] = codes[...].astype(f32)


def fetch(sources, targets, sems):
    copies = [pltpu.make_async_copy(a, b, sems.at[i]) for i, (a, b) in enumerate(zip(sources, targets))]
    for copy in copies:
        copy.start()
    for copy in copies:
        copy.wait()


def cover_rows(nz, number, columns, table, mix, kt):
    me = lax.axis_index("obs")
    times, waves, bands = table[0:1, :], table[1:2, :], table[2:3, :]
    hot = (lax.broadcasted_iota(jnp.int32, (C, ROWS_DEV), 0).astype(f32) == bands).astype(f32)
    hots = jnp.concatenate([hot, hot, hot, jnp.zeros_like(hot)], axis=0).astype(bf16)
    offsets = pair_offsets(nz, number)
    step = kt.shape[0] // len(offsets)
    for i, offset in enumerate(offsets):
        here = columns[pl.ds(pl.multiple_of(step * ((me ^ offset) // 2), step), step), :]
        picked = jnp.zeros((step, C), f32)
        for kind in range(NB):
            picked = jnp.where(here[:, 2:3] == float(kind), mix[kind : kind + 1, :], picked)
        high = picked.astype(bf16).astype(f32)
        middle = (picked - high).astype(bf16).astype(f32)
        low = picked - high - middle
        split = jnp.concatenate([high, middle, low, jnp.zeros_like(low)], axis=1).astype(bf16)
        mixing = dot(split, hots)
        delta_t = times - here[:, 0:1]
        delta_w = waves - here[:, 1:2]
        value = jnp.exp2(-(delta_t * delta_t + delta_w * delta_w)) * mixing
        kt[step * i : step * (i + 1), :] = value.astype(bf16)


def first_rows_kernel(
    nz, arrived, points_in, bands_in, mix_in, lengthscales,
    kt, labels, self_cov, columns, table, mix, points, point_bands, band_mix, sems,
):
    fetch((points_in, bands_in, mix_in), (points, point_bands, band_mix), sems)
    codes = arrived[2:3, :]
    label = jnp.floor((codes + 0.5) * (1.0 / NB))
    labels[...] = label.astype(jnp.int32)
    bands = codes - NB * label
    hot = (lax.broadcasted_iota(jnp.int32, (C, ROWS_DEV), 0).astype(f32) == bands).astype(f32)
    eye = lax.broadcasted_iota(jnp.int32, (C, C), 0) == lax.broadcasted_iota(jnp.int32, (C, C), 1)
    factor = jnp.concatenate([band_mix[...], jnp.zeros((NB, C - NB), f32)], axis=1)
    factor = jnp.concatenate([factor, jnp.zeros((C - NB, C), f32)], axis=0)
    coupling = eye.astype(f32) + lax.dot_general(
        factor, factor, (((1,), (1,)), ((), ())), precision=precise, preferred_element_type=f32
    )
    mix[...] = coupling
    diagonal = jnp.sum(jnp.where(eye, coupling, 0.0), axis=1, keepdims=True)
    self_cov[...] = jnp.sum(hot * diagonal, axis=0, keepdims=True)
    scales = [SQRT_HALF_LOG2E / lengthscales[i] for i in range(2)]
    table[0:1, :] = arrived[0:1, :] * scales[0]
    table[1:2, :] = arrived[1:2, :] * scales[1]
    table[2:3, :] = bands
    width = points.shape[1]
    columns[...] = jnp.concatenate(
        [points[0:1, :] * scales[0], points[1:2, :] * scales[1], point_bands[...].astype(f32), jnp.zeros((C - 3, width), f32)],
        axis=0,
    ).T
    cover_rows(nz, 0, columns, table, mix, kt)


def more_rows_kernel(nz, columns, table, mix, *kts):
    for number, kt in enumerate(kts):
        cover_rows(nz, number + 1, columns, table, mix, kt)


def join_pairs(nz, number, places, groups, factor):
    me = lax.axis_index("obs")
    offsets = pair_offsets(nz, number)
    size = factor.shape[0] // len(offsets) // 2
    for source, slot, offset in places:
        base = 2 * size * offsets.index(offset & -2)
        target = pl.multiple_of(base + size * ((me ^ offset) & 1), size)
        factor[pl.ds(target, size), :] = groups[source][size * slot : size * (slot + 1), :]


def pair_offsets(nz, number):
    return ([0] if number == 0 else []) + phases_of(nz)[number]


def whiten_kernel(nz, number, places, kt, *refs):
    start = refs[0] if number > 0 else None
    groups, (total, factor, turned) = refs[(number > 0) : -3], refs[-3:]
    join_pairs(nz, number, places, groups, factor)
    turned[...] = factor[...].T

    @pl.loop(0, ROWS_DEV // COL)
    def _(step):
        columns = pl.ds(pl.multiple_of(step * COL, COL), COL)
        for k in range(0, turned.shape[0], 512):
            part = dot(turned[k : k + 512, :], kt[:, columns])
            if number > 0:
                part = part + start[k : k + 512, columns]
            total[k : k + 512, columns] = part


def covary_kernel(nz, last, last_places, places, kt, start, means, *refs):
    ab, bt, sums, factor, last_turned, whole, turned = refs[-7:]
    count = 1 + max(source for source, _, _ in last_places)
    last_groups, groups = refs[:count], refs[count:-7]
    width = whole.shape[0]
    join_pairs(nz, last, last_places, last_groups, factor)
    last_turned[...] = factor[...].T
    store_pieces(groups, places, whole)
    for j in range(0, width, 256):
        turned[:, j : j + 256] = whole[j : j + 256, :].T

    @pl.loop(0, ROWS_DEV // COL)
    def _(step):
        columns = pl.ds(pl.multiple_of(step * COL, COL), COL)
        square = jnp.zeros((1, COL), f32)
        for k in range(0, width, 1024):
            part = start[k : k + 1024, columns] + dot(last_turned[k : k + 1024, :], kt[:, columns])
            square = square - jnp.sum(part * part, axis=0, keepdims=True)
            ab[k : k + 1024, columns] = part.astype(bf16)
        for l in range(0, width, 256):
            rows = turned[l : l + 256, l:]
            if l == 0:
                rows = jnp.concatenate([rows, means[...], jnp.zeros_like(means)], axis=0)
            part = dot(rows, ab[l:, columns])
            if l == 0:
                sums[:, columns] = part[256 : 256 + C, :]
                part = part[:256, :]
            square = square + jnp.sum(part * part, axis=0, keepdims=True)
            bt[l : l + 256, columns] = part.astype(bf16)
        piece = ROWS_DEV // C
        for i in range(COL // piece):
            sums[pl.ds((COL // piece) * step + i, 1), ROWS_DEV:] = square[:, piece * i : piece * (i + 1)]


def outer_rows(nz, x, ab, heavy, picked, keep, send):
    core = lax.axis_index("obs") % 2
    block = ab.shape[0] // nz
    pair = block // 2
    for z in range(nz):
        picked[pair * z : pair * (z + 1), :] = ab[pl.ds(pl.multiple_of(block * z + pair * x, pair), pair), :]
    for chunk in range(nz):
        term = dot_nt(picked[pair * chunk :, :], heavy[block * chunk : block * (chunk + 1), :])
        for z in range(chunk, nz):
            left = block * (z * (z + 1) // 2 + chunk)
            top = pair * (z - chunk)
            even = term[top : top + pair // 2, :]
            odd = term[top + pair // 2 : top + pair, :]
            keep[:, left : left + block] = jnp.where(core == 0, even, odd)
            send[: pair // 2, left : left + block] = jnp.where(core == 0, odd, even).astype(bf16)


def blocks_at(values, bit, wanted):
    blocks = [i for i in range(values.shape[1] // SLOT) if bool(i & bit) == wanted]
    return {i: values[:, SLOT * i : SLOT * (i + 1)] for i in blocks}


def outgoing(state, width, bit):
    values = state[...]
    rows = [values[:, :width]]
    if values.shape[1] > width:
        rows.append(jnp.concatenate(list(blocks_at(values[:, width:], bit, True).values()), axis=1))
    return jnp.concatenate(rows, axis=0)


def absorbed(state, width, bit, arrived):
    values = state[...]
    mean = values[:, :width] + arrived[:C]
    if values.shape[1] == width:
        return mean
    blocks = blocks_at(values[:, width:], bit, False)
    came = blocks_at(values[:, width:], bit, True)
    blocks.update({i: arrived[C:, SLOT * at : SLOT * (at + 1)] for at, i in enumerate(came)})
    return jnp.concatenate([mean] + [blocks[i] for i in sorted(blocks)], axis=1)


def slope_kernel(nz, own, other, scales, labels, self_cov, ab, bt, chances_out, state, heavy, keep, send, picked):
    total = own[...] + other[...]
    variance = jnp.concatenate([total[i : i + 1, ROWS_DEV:] for i in range(C)], axis=1) + self_cov[...]
    classes = lax.broadcasted_iota(jnp.int32, (C, 1), 0)
    scale = jnp.zeros((C, 1), f32)
    for i in range(C):
        scale = jnp.where(classes == i, scales[i], scale)
    logits = total[:, :ROWS_DEV] + 0.5 * scale * variance
    weights = jnp.exp(logits)
    chances = weights / jnp.sum(weights, axis=0, keepdims=True)
    chances_out[...] = chances
    twice = -jnp.sum(chances * scale, axis=0, keepdims=True)
    slope = ((labels[...] == classes).astype(f32) - chances).astype(bf16)
    heavy[...] = (bt[...].astype(f32) * twice).astype(bf16)
    width = ab.shape[0]
    state[:, :width] = dot_nt(ab[...], slope).T
    if state.shape[1] > width:
        for i in range(ROWS_DEV // SLOT):
            there = pl.ds(pl.multiple_of(SLOT * (lax.axis_index("obs") ^ i), SLOT), SLOT)
            state[:, width + SLOT * i : width + SLOT * (i + 1)] = chances_out[:, there]
    send[keep.shape[0] :, :width] = halves(outgoing(state, width, 1))
    outer_rows(nz, 1 - (lax.axis_index("obs") // 2) % 2, ab, heavy, picked, keep, send)


def near_kernel(nz, ab, heavy, keep, send, picked):
    outer_rows(nz, (lax.axis_index("obs") // 2) % 2, ab, heavy, picked, keep, send)


def halves(value):
    high = value.astype(bf16).astype(f32)
    return jnp.concatenate([high, value - high], axis=0).astype(bf16)


def joined(pair):
    rows = pair.shape[0] // 2
    return pair[:rows].astype(f32) + pair[rows:].astype(f32)


def pair_kernel(width, bit, state, keep, arrived, state_out, ahead, total):
    rows = keep.shape[0]
    total[...] = keep[...] + arrived[:rows, :].astype(f32)
    state_out[...] = absorbed(state, width, 1, joined(arrived[rows:, :width]))
    ahead[...] = outgoing(state_out, width, bit)


def near_pair_kernel(keep, arrived, total):
    total[...] = keep[...] + arrived[...].astype(f32)


def with_children(nz, totals, width, offset, children, refs):
    total = totals[(offset // 2) % 2]
    rows = total.shape[0]
    z = (lax.axis_index("obs") ^ offset) // 4
    start = pl.multiple_of(width // nz * (z * (z + 1) // 2), width // nz)
    value = total[:, pl.ds(start, width)]
    for source, slot in children:
        value = value + refs[source][rows * slot : rows * (slot + 1), :].astype(f32)
    return value


def state_of(state, refs, came, width):
    if came is None:
        return state[...]
    source, bit = came
    arrived = refs[source]
    if arrived.dtype == f32:
        return absorbed(state, width, bit, arrived[...])
    extra = 2 * C * (2 if state.shape[1] > width else 1)
    return absorbed(state, width, bit, joined(arrived[arrived.shape[0] - extra :, :]))


def level_kernel(nz, plan, came, bit, state, near, far, *refs):
    outs = refs[len(refs) - len(plan) - 1 :]
    rows = far.shape[0]
    width = outs[1].shape[1]
    outs[0][...] = state_of(state, refs, came, width)
    for out, (pieces, with_state) in zip(outs[1:], plan):
        for i, (offset, children) in enumerate(pieces):
            part = with_children(nz, (near, far), width, offset, children, refs)
            out[rows * i : rows * (i + 1), :] = part.astype(bf16)
        if with_state:
            out[rows * len(pieces) :, :] = halves(outgoing(outs[0], width, bit))


def index_in(arrays, array):
    for i, other in enumerate(arrays):
        if other is array:
            return i
    arrays.append(array)
    return len(arrays) - 1


class Scatter:
    def __init__(self, nz, width, state):
        self.nz, self.width, self.state = nz, width, state
        self.arrived = {}
        self.came = None

    def children(self, offset, arrays):
        return [
            (index_in(arrays, array), slot)
            for child, (array, slot) in self.arrived.items()
            if child ^ (child & -child) == offset
        ]

    def came_in(self, arrays):
        return None if self.came is None else (index_in(arrays, self.came[0]), self.came[1])

    def level(self, near, far, sends, bit):
        arrays = []
        plan = [
            ([(o, self.children(o, arrays)) for o in offsets], offsets[0] & -offsets[0] == bit)
            for offsets in sends
        ]
        came = self.came_in(arrays)
        rows = far.shape[0]
        extra = 2 * C * (2 if self.state.shape[1] > self.width else 1)
        self.state, *outs = pl.pallas_call(
            functools.partial(level_kernel, self.nz, plan, came, bit),
            out_shape=[jax.ShapeDtypeStruct(self.state.shape, f32)]
            + [jax.ShapeDtypeStruct((rows * len(pieces) + extra * m, self.width), bf16) for pieces, m in plan],
            in_specs=[VMEM] * (3 + len(arrays)),
            out_specs=[VMEM] * (1 + len(plan)),
            compiler_params=SMALL,
            name="add_level",
        )(self.state, near, far, *arrays)
        for (pieces, with_state), out in zip(plan, outs):
            offsets = [offset for offset, _ in pieces]
            out = swap(out, "obs", offsets[0] & -offsets[0])
            self.arrived.update({offset: (out, slot) for slot, offset in enumerate(offsets)})
            if with_state:
                self.came = (out, bit)


def finish_kernel(nz, children, came, state, near, chol, means, *refs):
    outs = refs[-3:] if state.shape[1] > chol.shape[1] else refs[-2:]
    grad_chol, grad_mean = outs[:2]
    rows, width = chol.shape
    value = with_children(nz, (near, near), width, 0, children, refs)
    row_ids = lax.axis_index("obs") * rows + lax.broadcasted_iota(jnp.int32, (rows, width), 0)
    column_ids = lax.broadcasted_iota(jnp.int32, (rows, width), 1)
    own = chol[...].astype(f32)
    on_diag = column_ids == row_ids
    inverse = 1.0 / jnp.where(on_diag, own, 1.0)
    grad_chol[...] = jnp.where(column_ids <= row_ids, value, 0.0) - own + jnp.where(on_diag, inverse, 0.0)
    values = state_of(state, refs, came, width)
    grad_mean[...] = values[:, :width] - means[...].astype(f32)
    for i in range((values.shape[1] - width) // SLOT):
        there = pl.ds(pl.multiple_of(SLOT * (lax.axis_index("obs") ^ i), SLOT), SLOT)
        outs[2][:, there] = values[:, width + SLOT * i : width + SLOT * (i + 1)]


def route(obs_coords, obs_codes, route_plan):
    devices = lax.axis_size("obs")
    stacked = pl.pallas_call(
        stack_kernel,
        out_shape=jax.ShapeDtypeStruct((3, obs_coords.shape[1]), f32),
        in_specs=[HBM, HBM],
        out_specs=VMEM,
        scratch_shapes=[
            pltpu.VMEM(obs_coords.shape, f32),
            pltpu.VMEM((1, obs_coords.shape[1]), jnp.int32),
            pltpu.SemaphoreType.DMA((2,)),
        ],
        compiler_params=SMALL,
        name="stack",
    )(obs_coords, obs_codes[None, :])
    if devices * SLOT == ROWS_DEV:
        return stacked
    me = lax.axis_index("obs")
    blocks = route_plan * SLOT
    send_start = jnp.cumsum(blocks, axis=1) - blocks
    recv_start = jnp.cumsum(blocks, axis=0) - blocks
    my_sends = lax.dynamic_index_in_dim(send_start, me, 0, keepdims=False)
    my_recvs = lax.dynamic_index_in_dim(recv_start, me, 1, keepdims=False)
    padded = jnp.concatenate([stacked, jnp.zeros((3, SLOT), f32)], axis=1)
    outgoing = jax.vmap(lambda offset: lax.dynamic_slice_in_dim(padded, offset, SLOT, 1))(my_sends)
    incoming = lax.all_to_all(outgoing, "obs", split_axis=0, concat_axis=0, tiled=True)
    position = jnp.arange(ROWS_DEV, dtype=jnp.int32)
    sources = jnp.arange(devices, dtype=jnp.int32)
    source = jnp.sum((my_recvs[None, :] <= position[:, None]).astype(jnp.int32), axis=1) - 1
    pick = (source[:, None] == sources[None, :]).astype(jnp.int32)
    begin_row = jnp.sum(pick * my_recvs[None, :], axis=1)
    return incoming[source, :, position - begin_row].T


def body(
    obs_coords,
    obs_codes,
    route_plan,
    inducing_coords,
    inducing_bands,
    band_mix,
    lengthscales,
    class_scales,
    prior_factor,
    variational_chol,
    variational_mean,
):
    n = lax.axis_size("obs")
    nz = n // 4
    rows, width = variational_chol.shape
    gather = Gather((prior_factor, variational_chol), nz)
    arrived = route(obs_coords, obs_codes, route_plan)
    big = pltpu.CompilerParams(vmem_limit_bytes=16 * 1024 * 1024)
    phases = range(len(gather.phases))
    covered = [
        jax.ShapeDtypeStruct((2 * rows * len(pair_offsets(nz, number)), ROWS_DEV), bf16) for number in phases
    ]
    cover = lambda: pl.pallas_call(
        functools.partial(first_rows_kernel, nz),
        out_shape=[
            covered[0],
            jax.ShapeDtypeStruct((1, ROWS_DEV), jnp.int32),
            jax.ShapeDtypeStruct((1, ROWS_DEV), f32),
            jax.ShapeDtypeStruct((width, C), f32),
            jax.ShapeDtypeStruct((C, ROWS_DEV), f32),
            jax.ShapeDtypeStruct((C, C), f32),
        ],
        in_specs=[VMEM, HBM, HBM, HBM, SMEM],
        out_specs=[VMEM] * 6,
        scratch_shapes=[
            pltpu.VMEM((2, width), f32),
            pltpu.VMEM((1, width), jnp.int32),
            pltpu.VMEM((NB, NB), f32),
            pltpu.SemaphoreType.DMA((3,)),
        ],
        compiler_params=big,
        cost_estimate=pl.CostEstimate(
            flops=10 * width * ROWS_DEV, bytes_accessed=2 * 1024 * 1024, transcendentals=width * ROWS_DEV // 2
        ),
        name="first_rows",
    )(arrived, inducing_coords, inducing_bands[None, :], band_mix, lengthscales)
    cover_more = lambda *given: pl.pallas_call(
        functools.partial(more_rows_kernel, nz),
        out_shape=covered[1:],
        in_specs=[VMEM] * 3,
        out_specs=[VMEM] * (len(covered) - 1),
        compiler_params=big,
        cost_estimate=pl.CostEstimate(
            flops=10 * width * ROWS_DEV, bytes_accessed=2 * 1024 * 1024, transcendentals=width * ROWS_DEV // 2
        ),
        name="more_rows",
    )(*given)

    def whiten(number, kt, *start):
        arrays, places = gather.of(0, number)
        inner = 2 * rows * len(pair_offsets(nz, number))
        return pl.pallas_call(
            functools.partial(whiten_kernel, nz, number, places),
            out_shape=jax.ShapeDtypeStruct((width, ROWS_DEV), f32),
            in_specs=[VMEM] * (1 + len(start) + len(arrays)),
            out_specs=VMEM,
            scratch_shapes=[
                pltpu.VMEM((inner, width), bf16),
                pltpu.VMEM((width, inner), bf16),
            ],
            input_output_aliases={1: 0} if start else {},
            compiler_params=big,
            cost_estimate=pl.CostEstimate(
                flops=2 * width * inner * ROWS_DEV, bytes_accessed=10 * 1024 * 1024, transcendentals=0
            ),
            name="whiten",
        )(kt, *start, *arrays)

    kt, labels, self_cov, *given = gather.phase(0, cover)
    last = len(gather.phases) - 1
    whitened, kts = gather.phase(1, lambda: (whiten(0, kt), cover_more(*given)))
    for number in range(2, last + 1):
        whitened = gather.phase(number, lambda: whiten(number - 1, kts[number - 2], whitened))
    last_arrays, last_places = gather.of(0, last)
    chol_arrays, chol_places = gather.of(1)
    ab, bt, sums = pl.pallas_call(
        functools.partial(covary_kernel, nz, last, last_places, chol_places),
        out_shape=(
            jax.ShapeDtypeStruct((width, ROWS_DEV), bf16),
            jax.ShapeDtypeStruct((width, ROWS_DEV), bf16),
            jax.ShapeDtypeStruct((C, ROWS_DEV + ROWS_DEV // C), f32),
        ),
        in_specs=[VMEM] * (3 + len(last_arrays) + len(chol_arrays)),
        out_specs=(VMEM, VMEM, VMEM),
        scratch_shapes=[
            pltpu.VMEM((2 * rows, width), bf16),
            pltpu.VMEM((width, 2 * rows), bf16),
            pltpu.VMEM((width, width), bf16),
            pltpu.VMEM((width, width), bf16),
        ],
        compiler_params=big,
        cost_estimate=pl.CostEstimate(
            flops=width * width * ROWS_DEV, bytes_accessed=10 * 1024 * 1024, transcendentals=0
        ),
        name="covary",
    )(kts[-1], whitened, variational_mean, *last_arrays, *chol_arrays)

    other = swap(sums, "ind", 1)
    bit = 2
    while bit < lax.axis_size("ind"):
        sums = sums + other
        other = swap(sums, "ind", bit)
        bit *= 2

    packed = width // nz * (nz * (nz + 1) // 2)
    kept = jax.ShapeDtypeStruct((rows, packed), f32)
    moving = n * SLOT == ROWS_DEV
    held = jax.ShapeDtypeStruct((C, width + ROWS_DEV * moving), f32)
    extra = C * (2 if moving else 1)
    chances, state, heavy, keep, send = pl.pallas_call(
        functools.partial(slope_kernel, nz),
        out_shape=[
            jax.ShapeDtypeStruct((C, ROWS_DEV), f32),
            held,
            jax.ShapeDtypeStruct((width, ROWS_DEV), bf16),
            kept,
            jax.ShapeDtypeStruct((rows + 2 * extra, packed), bf16),
        ],
        in_specs=[VMEM, VMEM, SMEM] + [VMEM] * 4,
        out_specs=[VMEM] * 5,
        scratch_shapes=[pltpu.VMEM((width // 2, ROWS_DEV), bf16)],
        compiler_params=big,
        name="slopes",
    )(sums, other, class_scales, labels, self_cov, ab, bt)
    near_keep, near_send = pl.pallas_call(
        functools.partial(near_kernel, nz),
        out_shape=[kept, jax.ShapeDtypeStruct((rows, packed), bf16)],
        in_specs=[VMEM] * 2,
        out_specs=[VMEM] * 2,
        scratch_shapes=[pltpu.VMEM((width // 2, ROWS_DEV), bf16)],
        compiler_params=big,
        name="near_outer",
    )(ab, heavy)
    state, ahead, far = pl.pallas_call(
        functools.partial(pair_kernel, width, 2 * nz),
        out_shape=[held, jax.ShapeDtypeStruct((extra, width), f32), kept],
        in_specs=[VMEM] * 3,
        out_specs=[VMEM] * 3,
        compiler_params=SMALL,
        name="add_pair",
    )(state, keep, swap(send, "obs", 1))
    near = pl.pallas_call(
        near_pair_kernel,
        out_shape=kept,
        in_specs=[VMEM] * 2,
        out_specs=VMEM,
        compiler_params=SMALL,
        name="add_near_pair",
    )(near_keep, swap(near_send, "obs", 1))
    scatter = Scatter(nz, width, state)
    ahead = swap(ahead, "obs", 2 * nz)
    along_x = [o for phase in reversed(gather.phases) for o in phase if o & 2]
    scatter.level(far, far, [along_x[:1], along_x[1:-1]], None)
    scatter.came = (ahead, 2 * nz)
    along_z = [[o for o in phase if not o & 2] for phase in gather.phases]
    along_z = [phase for phase in along_z if phase]
    for i, phase in enumerate(reversed(along_z)):
        bits = sorted({o & -o for o in phase}, reverse=True)
        sends = [[o for o in phase if o & -o == bit] for bit in bits]
        last_step = i == len(along_z) - 1
        scatter.level(near, far, sends + [along_x[-1:]] * last_step, 2 if last_step else 4 << i)
    arrays = []
    children = scatter.children(0, arrays)
    came = scatter.came_in(arrays)
    shapes = [jax.ShapeDtypeStruct((rows, width), f32), jax.ShapeDtypeStruct((C, width), f32)]
    if moving:
        shapes.append(jax.ShapeDtypeStruct((C, ROWS_DEV), f32))
    grad_chol, grad_mean, *moved = pl.pallas_call(
        functools.partial(finish_kernel, nz, children, came),
        out_shape=shapes,
        in_specs=[VMEM] * (4 + len(arrays)),
        out_specs=[VMEM] * len(shapes),
        compiler_params=SMALL,
        name="finish",
    )(scatter.state, near, variational_chol, variational_mean, *arrays)
    chances = moved[0] if moving else chances
    return (chances, grad_chol, grad_mean)


def solution(mesh):
    placed = (
        P(None, "obs"),
        P("obs"),
        P(),
        P(None, "ind"),
        P("ind"),
        P(),
        P(),
        P(),
        P(("ind", "obs"), None),
        P(("ind", "obs"), None),
        P(None, "ind"),
    )
    return jax.shard_map(
        body,
        mesh=mesh,
        in_specs=placed,
        out_specs=(P(None, "obs"), P(("ind", "obs"), None), P(None, "ind")),
        check_vma=False,
    )
```
